128 devices in a mesh: dp: 32 (over y, z, core), branch: 4 (over x).
Axes of the slice: x: 4, y: 4, z: 4, core: 2. Of those that a mesh axis runs over, the one named last changes fastest.
Arguments:
- block_input: bfloat16 [65536, 768], P(('dp', 'branch')), may hold values from -6 to 6
- cotangent: bfloat16 [65536, 768], P(('dp', 'branch')), may hold values from -6 to 6
- image_owner: int32 [140], replicated, may hold values from 0 to 31, as said below
- image_length: int32 [140], replicated, may hold values from 196 to 2048, as said below
- image_start: int32 [140], replicated, may hold values from 0 to 1764
- qkv_weight: float32 [3, 768, 768], P(None, 'dp', 'branch'), may hold values from -0.28867513 to 0.28867513
- qkv_first: float32 [3, 768, 768], P(None, 'dp', 'branch'), may hold values from -0.00061035156 to 0.00061035156
- qkv_second: float32 [3, 768, 768], P(None, 'dp', 'branch'), may hold values from 7.426626e-09 to 2.9650028e-08
- out_weight: float32 [768, 768], P('branch', 'dp'), may hold values from -0.75 to 0.75
- out_first: float32 [768, 768], P('branch', 'dp'), may hold values from -0.00061035156 to 0.00061035156
- out_second: float32 [768, 768], P('branch', 'dp'), may hold values from 7.426626e-09 to 2.9650028e-08
- up_weight: float32 [768, 3072], P('dp', 'branch'), may hold values from -0.28867513 to 0.28867513
- up_first: float32 [768, 3072], P('dp', 'branch'), may hold values from -0.00061035156 to 0.00061035156
- up_second: float32 [768, 3072], P('dp', 'branch'), may hold values from 7.426626e-09 to 2.9650028e-08
- down_weight: float32 [3072, 768], P('branch', 'dp'), may hold values from -0.109375 to 0.109375
- down_first: float32 [3072, 768], P('branch', 'dp'), may hold values from -0.00061035156 to 0.00061035156
- down_second: float32 [3072, 768], P('branch', 'dp'), may hold values from 7.426626e-09 to 2.9650028e-08
- small_weight: float32 [4736], replicated, may hold values from -1.2 to 3.6
- small_first: float32 [4736], replicated, may hold values from -0.0012207031 to 0.0012207031
- small_second: float32 [4736], replicated, may hold values from 2.9650028e-08 to 1.1860011e-07
Outputs:
- block_output: bfloat16 [65536, 768], P(('dp', 'branch'))
- input_grad: bfloat16 [65536, 768], P(('dp', 'branch'))
- grad_norm: float32 [], replicated
- qkv_clipped: float32 [3, 768, 768], P(None, 'dp', 'branch')
- qkv_second_new: float32 [3, 768, 768], P(None, 'dp', 'branch')
- qkv_updated: float32 [3, 768, 768], P(None, 'dp', 'branch')
- out_clipped: float32 [768, 768], P('branch', 'dp')
- out_second_new: float32 [768, 768], P('branch', 'dp')
- out_updated: float32 [768, 768], P('branch', 'dp')
- up_clipped: float32 [768, 3072], P('dp', 'branch')
- up_second_new: float32 [768, 3072], P('dp', 'branch')
- up_updated: float32 [768, 3072], P('dp', 'branch')
- down_clipped: float32 [3072, 768], P('branch', 'dp')
- down_second_new: float32 [3072, 768], P('branch', 'dp')
- down_updated: float32 [3072, 768], P('branch', 'dp')
- small_clipped: float32 [4736], replicated
- small_second_new: float32 [4736], replicated
- small_updated: float32 [4736], replicated
The draws below stay inside these ranges and needn't reach their ends.
Inputs may be any that keep to these rules, and one draw needn't show every extreme that they name: `image_owner`: images are listed by owner, owners ascending; every dp index owns one image or more; the images of one index lie back to back from its row 0 in list order; some index holds exactly 2048 tokens. `image_length`: an image has 196 or 2048 tokens, and no dp index holds more than 2048.
All inputs are finite; a program needn't handle non-finite values.
Results may differ from the reference program's by a relative error of at most 0.005.
The reference program's roundings to bfloat16 on the way count: a program that leaves them out, or rounds other values in their place, can miss the bound.
Values may be sent and summed in bfloat16 or wider, within the bound.
No kernel may reach another device: no remote copies, remote signals or barrier semaphores. Data moves between devices by JAX's collectives and lax.ppermute only.
A program may use at most 192 MiB of HBM per device.

```python
import math
import jax
import jax.numpy as jnp
from jax import lax

D = 768
HEADS = 12
HEAD = 64
FF = 3072
CAP = 2048
SMALL_LEN = 196
STEP = 10
HD = 768
QBLK = 512
SLOTS = 10
N_BIG = 8
NIMG = 140
TOKENS = 65536
SMALLN = 4736
P_ALL = 7082624
N_DP = 32


def image_plan(key):
    role_key, pair_key = jax.random.split(key)
    ranking = jax.random.permutation(role_key, N_DP).astype(jnp.int32)
    pair_count = (N_DP - N_BIG) // 2
    pair_loads = jax.random.randint(pair_key, (pair_count,), 1, SLOTS + 1).astype(jnp.int32)
    pair_loads = pair_loads.at[0].set(SLOTS)
    paired = jnp.maximum(ranking - N_BIG, 0)
    chosen = pair_loads[paired // 2]
    holds_big = ranking < N_BIG
    image_counts = jnp.where(holds_big, 1, jnp.where(paired % 2 == 0, chosen, SLOTS + 1 - chosen)).astype(jnp.int32)
    count_ends = jnp.cumsum(image_counts).astype(jnp.int32)
    image_index = jnp.arange(NIMG, dtype=jnp.int32)
    owners = jnp.sum((count_ends[None, :] <= image_index[:, None]).astype(jnp.int32), axis=1).astype(jnp.int32)
    first_image = (count_ends - image_counts)[owners]
    local_index = image_index - first_image
    lengths = jnp.where(holds_big[owners], CAP, SMALL_LEN).astype(jnp.int32)
    starts = (local_index * SMALL_LEN).astype(jnp.int32)
    return (owners, lengths, starts)


def draw_image_owner(key, part):
    return image_plan(key)[0]


def draw_image_length(key, part):
    return image_plan(key)[1]


def draw_image_start(key, part):
    return image_plan(key)[2]


def rising(count, ratio):
    return ratio ** (jnp.arange(count, dtype=jnp.float32) / max(count - 1, 1))


def entries_of(key, shape, width, ratio):
    entries = jnp.clip(jax.random.normal(key, shape, jnp.float32), -4.0, 4.0)
    return entries * 0.6 * rising(width, ratio)


def draw_qkv_weight(key, part):
    key = jax.random.fold_in(key, 11)
    entries = entries_of(key, (3, D, HD), HD, 3.0)
    return entries * D ** (-0.5)


def draw_up_weight(key, part):
    key = jax.random.fold_in(key, 12)
    entries = entries_of(key, (D, FF), FF, 3.0)
    return entries * D ** (-0.5)


def draw_small_weight(key, part):
    key = jax.random.fold_in(key, 13)
    gain_key, query_key, key_key, bias_key, hidden_key = jax.random.split(key, 5)
    ratio = 3.0
    out_bias = 0.3 * jnp.clip(jax.random.normal(bias_key, (D,), jnp.float32), -4.0, 4.0)
    hidden_bias = 0.3 * jnp.clip(jax.random.normal(hidden_key, (FF,), jnp.float32), -4.0, 4.0)
    ln_gain = 0.6 * rising(D, ratio) * jax.random.uniform(gain_key, (D,), jnp.float32, 0.8, 1.2)
    query_gain = jax.random.uniform(query_key, (HEAD,), jnp.float32, 1.2, 1.8)
    key_gain = jax.random.uniform(key_key, (HEAD,), jnp.float32, 1.2, 1.8)
    return jnp.concatenate([ln_gain, query_gain, key_gain, out_bias, hidden_bias])


def level_of(own_key, extent, pieces, least, largest):
    level, own = 1.0, jax.random.fold_in(own_key, 6)
    for dim, blocks in pieces:
        heights = jnp.exp(jax.random.uniform(jax.random.fold_in(own, dim), (blocks,), jnp.float32, least / len(pieces), largest / len(pieces)))
        level = level * jnp.repeat(heights, extent[dim] // blocks).reshape([-1 if axis == dim else 1 for axis in range(len(extent))])
    return level


def scatter_about(stream_key, dims, scale, limit, cuts=(), kind=jnp.bfloat16):
    values = scale * jax.random.normal(stream_key, dims, jnp.float32)
    if cuts:
        values = values * level_of(stream_key, dims, cuts, -0.22, 0.18)
    return jnp.clip(values, -limit, limit).astype(kind)


def setup_inputs(seed: int = 0) -> dict:
    key_list = jax.random.split(jax.random.key(seed), 21)
    block_input = scatter_about(key_list[0], (TOKENS, D), 1.0, 6.0, ((0, 128),))
    cotangent = scatter_about(key_list[1], (TOKENS, D), 1.0, 6.0, ((0, 128),))
    image_owner = draw_image_owner(jax.random.fold_in(key_list[20], 71), 0)
    image_length = draw_image_length(jax.random.fold_in(key_list[20], 71), 0)
    image_start = draw_image_start(jax.random.fold_in(key_list[20], 71), 0)
    qkv_weight = draw_qkv_weight(jax.random.fold_in(key_list[20], 71), 0)
    qkv_first = scatter_about(key_list[6], (3, D, HD), (0.111 * P_ALL ** -0.5), 0.00061035156, ((1, 32), (2, 4)), jnp.float32)
    qkv_second = jnp.clip(jnp.exp(math.log(2.965002821042617e-08) - 1.3843914 * jax.random.uniform(key_list[7], (3, D, HD), jnp.float32) ** level_of(key_list[7], (3, D, HD), ((1, 32), (2, 4)), -0.2, 0.2)), 7.426625980855306e-09, 2.965002821042617e-08)
    out_weight = scatter_about(key_list[8], (HD, D), (HD // 12) ** -0.5, 0.75, ((0, 4), (1, 32)), jnp.float32)
    out_first = scatter_about(key_list[9], (HD, D), (0.111 * P_ALL ** -0.5), 0.00061035156, ((0, 4), (1, 32)), jnp.float32)
    out_second = jnp.clip(jnp.exp(math.log(2.965002821042617e-08) - 1.3843914 * jax.random.uniform(key_list[10], (HD, D), jnp.float32) ** level_of(key_list[10], (HD, D), ((0, 4), (1, 32)), -0.2, 0.2)), 7.426625980855306e-09, 2.965002821042617e-08)
    up_weight = draw_up_weight(jax.random.fold_in(key_list[20], 71), 0)
    up_first = scatter_about(key_list[12], (D, FF), (0.111 * P_ALL ** -0.5), 0.00061035156, ((0, 32), (1, 4)), jnp.float32)
    up_second = jnp.clip(jnp.exp(math.log(2.965002821042617e-08) - 1.3843914 * jax.random.uniform(key_list[13], (D, FF), jnp.float32) ** level_of(key_list[13], (D, FF), ((0, 32), (1, 4)), -0.2, 0.2)), 7.426625980855306e-09, 2.965002821042617e-08)
    down_weight = scatter_about(key_list[14], (FF, D), FF ** -0.5, 0.109375, ((0, 4), (1, 32)), jnp.float32)
    down_first = scatter_about(key_list[15], (FF, D), (0.111 * P_ALL ** -0.5), 0.00061035156, ((0, 4), (1, 32)), jnp.float32)
    down_second = jnp.clip(jnp.exp(math.log(2.965002821042617e-08) - 1.3843914 * jax.random.uniform(key_list[16], (FF, D), jnp.float32) ** level_of(key_list[16], (FF, D), ((0, 4), (1, 32)), -0.2, 0.2)), 7.426625980855306e-09, 2.965002821042617e-08)
    small_weight = draw_small_weight(jax.random.fold_in(key_list[20], 71), 0)
    small_first = scatter_about(key_list[18], (SMALLN,), (0.222 * P_ALL ** -0.5), 0.0012207031, (), jnp.float32)
    small_second = jnp.clip(jnp.exp(jax.random.uniform(key_list[19], (SMALLN,), jnp.float32, math.log(2.965002821042617e-08), math.log(1.1860011284170469e-07))), 2.965002821042617e-08, 1.1860011284170469e-07)
    return dict(block_input=block_input, cotangent=cotangent, image_owner=image_owner, image_length=image_length, image_start=image_start, qkv_weight=qkv_weight, qkv_first=qkv_first, qkv_second=qkv_second, out_weight=out_weight, out_first=out_first, out_second=out_second, up_weight=up_weight, up_first=up_first, up_second=up_second, down_weight=down_weight, down_first=down_first, down_second=down_second, small_weight=small_weight, small_first=small_first, small_second=small_second)


@jax.custom_vjp
def low(v):
    return lax.optimization_barrier(v.astype(jnp.bfloat16)).astype(jnp.float32)

@jax.custom_vjp
def low_back(v):
    return v

def low_keep(v):
    return (low(v), None)

def low_pass(kept, grad):
    return (grad,)

def back_keep(v):
    return (v, None)

def back_low(kept, grad):
    return (low(grad),)
low.defvjp(low_keep, low_pass)
low_back.defvjp(back_keep, back_low)
EPS_NORM = 1e-06
BETA_ONE = 0.9
BETA_TWO = 0.95
EPS_ADAM = 1e-08
RATE_MATRIX = 0.1
RATE_SMALL = 1.0
DECAY_MATRIX = 0.1
HIGH = lax.Precision.HIGHEST

def layer_norm(values):
    average = lax.optimization_barrier(jnp.mean(values, axis=-1, keepdims=True))
    centered = values - average
    return centered * lax.rsqrt(lax.optimization_barrier(jnp.mean(centered * centered, axis=-1, keepdims=True)) + EPS_NORM)

def segment_ids(image_owner, image_length, image_start, group_index):
    position = jnp.arange(CAP, dtype=jnp.int32)
    finish = image_start + image_length
    inside = (image_owner[:, None] == group_index) & (position[None, :] >= image_start[:, None]) & (position[None, :] < finish[:, None])
    labels = jnp.arange(1, image_owner.shape[0] + 1, dtype=jnp.int32)
    return lax.optimization_barrier(jnp.sum(jnp.where(inside, labels[:, None], 0), axis=0)).astype(jnp.int32)

def group_forward(group_rows, segments, qkv_low, out_low, up_low, down_low, small_weight):
    ln_gain = small_weight[:D]
    query_gain = small_weight[D:D + HEAD]
    key_gain = small_weight[D + HEAD:D + 2 * HEAD]
    out_bias = small_weight[D + 2 * HEAD:2 * D + 2 * HEAD]
    hidden_bias = small_weight[2 * D + 2 * HEAD:]
    normed = low(layer_norm(group_rows) * ln_gain)
    projected = jnp.einsum('rd,cdh->crh', normed, qkv_low, precision=HIGH)
    raw_query = low_back(projected[0])
    raw_key = low_back(projected[1])
    values_all = low(low_back(projected[2])).reshape(CAP, HEADS, HEAD)
    queries = low(layer_norm(raw_query.reshape(CAP, HEADS, HEAD)) * query_gain)
    keys_normed = low(layer_norm(raw_key.reshape(CAP, HEADS, HEAD)) * key_gain)

    def attend(block_index):
        query_block = lax.dynamic_slice_in_dim(queries, block_index * QBLK, QBLK, 0)
        block_segments = lax.dynamic_slice_in_dim(segments, block_index * QBLK, QBLK, 0)
        scores = jnp.einsum('qhe,khe->hqk', query_block, keys_normed, precision=HIGH) * HEAD ** (-0.5)
        scores = low_back(scores)
        same_image = block_segments[:, None] == segments[None, :]
        scores = jnp.where(same_image[None], scores, -1e+30)
        row_max = lax.optimization_barrier(jnp.max(scores, axis=-1, keepdims=True))
        exponent = jnp.exp(scores - row_max)
        probabilities = low(exponent / lax.optimization_barrier(jnp.sum(exponent, axis=-1, keepdims=True)))
        return jnp.einsum('hqk,khe->qhe', probabilities, values_all, precision=HIGH)
    mixed_blocks = lax.map(jax.checkpoint(attend), jnp.arange(CAP // QBLK, dtype=jnp.int32))
    mixed_rows = low(low_back(mixed_blocks.reshape(CAP, HD)))
    attention = jnp.dot(mixed_rows, out_low, precision=HIGH)
    hidden_pre = low_back(jnp.dot(normed, up_low, precision=HIGH) + hidden_bias)
    hidden_act = low(jax.nn.gelu(hidden_pre, approximate=False))
    feedforward = jnp.dot(hidden_act, down_low, precision=HIGH)
    return group_rows + attention + feedforward + out_bias

def forward(block_rows, qkv_weight, out_weight, up_weight, down_weight, small_weight, all_segments):
    qkv_low = low(qkv_weight)
    out_low = low(out_weight)
    up_low = low(up_weight)
    down_low = low(down_weight)
    checked = jax.checkpoint(group_forward)

    def advance(carried, inputs):
        group_rows, segments = inputs
        return (carried, checked(group_rows, segments, qkv_low, out_low, up_low, down_low, small_weight))
    start_value = jnp.zeros((), jnp.float32)
    ignored, outputs = lax.scan(advance, start_value, (block_rows.reshape(N_DP, CAP, D), all_segments))
    return outputs.reshape(N_DP * CAP, D)

def adam_update(weight, first_moment, second_moment, gradient, factor, rate, decay):
    clipped = gradient * factor
    first_new = BETA_ONE * first_moment + (1.0 - BETA_ONE) * clipped
    second_new = BETA_TWO * second_moment + (1.0 - BETA_TWO) * clipped * clipped
    ratio = first_new / (1.0 - BETA_ONE ** STEP) / (jnp.sqrt(second_new / (1.0 - BETA_TWO ** STEP)) + EPS_ADAM)
    return (clipped, second_new, weight - rate * (ratio + decay * weight))

def reference(block_input, cotangent, image_owner, image_length, image_start, qkv_weight, qkv_first, qkv_second, out_weight, out_first, out_second, up_weight, up_first, up_second, down_weight, down_first, down_second, small_weight, small_first, small_second):
    groups = jnp.arange(N_DP, dtype=jnp.int32)
    all_segments = jax.vmap(lambda group_index: segment_ids(image_owner, image_length, image_start, group_index))(groups)
    live = (all_segments > 0).reshape(N_DP * CAP, 1).astype(jnp.float32)

    def run(block_rows, qkv_value, out_value, up_value, down_value, small_value):
        return forward(block_rows, qkv_value, out_value, up_value, down_value, small_value, all_segments)
    output_rows, pullback = jax.vjp(run, block_input.astype(jnp.float32), qkv_weight, out_weight, up_weight, down_weight, small_weight)
    row_grad, qkv_grad, out_grad, up_grad, down_grad, small_grad = pullback(cotangent.astype(jnp.float32) * live)
    squares = jnp.sum(qkv_grad * qkv_grad) + jnp.sum(out_grad * out_grad) + jnp.sum(up_grad * up_grad)
    squares = squares + jnp.sum(down_grad * down_grad) + jnp.sum(small_grad * small_grad)
    grad_norm = jnp.sqrt(squares)
    factor = 1.0 / jnp.maximum(grad_norm, 1.0)
    qkv_clipped, qkv_second_new, qkv_updated = adam_update(qkv_weight, qkv_first, qkv_second, qkv_grad, factor, RATE_MATRIX, DECAY_MATRIX)
    out_clipped, out_second_new, out_updated = adam_update(out_weight, out_first, out_second, out_grad, factor, RATE_MATRIX, DECAY_MATRIX)
    up_clipped, up_second_new, up_updated = adam_update(up_weight, up_first, up_second, up_grad, factor, RATE_MATRIX, DECAY_MATRIX)
    down_clipped, down_second_new, down_updated = adam_update(down_weight, down_first, down_second, down_grad, factor, RATE_MATRIX, DECAY_MATRIX)
    small_clipped, small_second_new, small_updated = adam_update(small_weight, small_first, small_second, small_grad, factor, RATE_SMALL, 0.0)
    return (output_rows.astype(jnp.bfloat16), row_grad.astype(jnp.bfloat16), grad_norm, qkv_clipped, qkv_second_new, qkv_updated, out_clipped, out_second_new, out_updated, up_clipped, up_second_new, up_updated, down_clipped, down_second_new, down_updated, small_clipped, small_second_new, small_updated)
```

```python
import functools

import jax
import jax.numpy as jnp
from jax import lax
from jax.experimental import pallas as pl
from jax.experimental.pallas import tpu as pltpu
from jax.sharding import PartitionSpec as P

D = 768
HEADS = 12
HEAD = 64
FF = 3072
CAP = 2048
SMALL_LEN = 196
STEP = 10

EPS_NORM = 1e-06
BETA_ONE = 0.9
BETA_TWO = 0.95
EPS_ADAM = 1e-08
RATE_MATRIX = 0.1
RATE_SMALL = 1.0
DECAY_MATRIX = 0.1

F32 = jnp.float32
BF16 = jnp.bfloat16
NN = (((1,), (0,)), ((), ()))
NT = (((1,), (1,)), ((), ()))
TN = (((0,), (0,)), ((), ()))

BR = 4
HL = HEADS // BR
HID = FF // BR
CH = CAP // BR
TILE = 256
PER = CH // TILE
QT = 512
KS = 512
MS = 256
SAFE = 60.0
VMEM = 56 * 2**20


def dot(left, right, dims):
    return lax.dot_general(left, right, dims, preferred_element_type=F32)


def cost(us):
    return pl.CostEstimate(flops=int(us * 1.1e9), bytes_accessed=0, transcendentals=0)


def params():
    return pltpu.CompilerParams(vmem_limit_bytes=VMEM)


def norm_parts(values):
    average = jnp.mean(values, axis=-1, keepdims=True)
    centered = values - average
    inverse = lax.rsqrt(jnp.mean(centered * centered, axis=-1, keepdims=True) + EPS_NORM)
    return (centered * inverse, inverse)


def norm_back(grad, hat, inverse):
    return inverse * (
        grad
        - jnp.mean(grad, axis=-1, keepdims=True)
        - hat * jnp.mean(grad * hat, axis=-1, keepdims=True)
    )


def lane_sum(values):
    width = values.shape[1] // 128
    total = values[:, :128]
    for i in range(1, width):
        total = total + values[:, i * 128 : (i + 1) * 128]
    return total


def row_sum8(values):
    return jnp.sum(values.reshape(values.shape[0] // 8, 8, values.shape[1]), axis=0)


def project_kernel(rows, weight, gain, q_gain, k_gain, *refs):
    normed, q_out, k_out, v_out, q_hat, k_hat = refs[-6:]
    hat, _ = norm_parts(rows[...].astype(F32))
    low = (hat * gain[...]).astype(BF16)
    normed[...] = low
    raw = dot(low, weight[:, : 3 * HL * HEAD], NN)
    ones = jnp.ones((rows.shape[0], HEAD), F32)
    for h in range(HL):
        for part, (gains, out, hats) in enumerate(
            ((q_gain, q_out, q_hat), (k_gain, k_out, k_hat))
        ):
            start = (part * HL + h) * HEAD
            head_hat, inverse = norm_parts(raw[:, start : start + HEAD])
            value = (head_hat * gains[...]).astype(BF16)
            if part == 0:
                value = value * jnp.asarray(HEAD**-0.5, BF16)
            out[h] = value
            hats[h] = jnp.concatenate([head_hat, inverse * ones], axis=1)
        start = (2 * HL + h) * HEAD
        v_out[h] = raw[:, start : start + HEAD].astype(BF16)


def project(chunk, rows, weights, gain, q_gain, k_gain, buffers):
    whole = lambda shape: pl.BlockSpec(shape, lambda t: (0,) * len(shape))
    heads = lambda width: pl.BlockSpec((HL, TILE, width), lambda t: (0, chunk * PER + t, 0))
    shapes = [jax.ShapeDtypeStruct((CAP, D), BF16)]
    shapes += [jax.ShapeDtypeStruct((HL, CAP, HEAD), BF16)] * 3
    shapes += [jax.ShapeDtypeStruct((HL, CAP, 2 * HEAD), F32)] * 2
    held = [] if buffers is None else list(buffers)
    return pl.pallas_call(
        project_kernel,
        grid=(PER,),
        in_specs=[
            pl.BlockSpec((TILE, D), lambda t: (t, 0)),
            whole((D, D)),
            whole((1, D)),
            whole((1, HEAD)),
            whole((1, HEAD)),
        ]
        + [pl.BlockSpec(memory_space=pl.ANY)] * len(held),
        out_specs=[
            pl.BlockSpec((TILE, D), lambda t: (chunk * PER + t, 0)),
            heads(HEAD),
            heads(HEAD),
            heads(HEAD),
            heads(2 * HEAD),
            heads(2 * HEAD),
        ],
        out_shape=shapes,
        input_output_aliases={5 + i: i for i in range(len(held))},
        compiler_params=params(),
        cost_estimate=cost(3),
        name="project",
    )(rows, weights, gain, q_gain, k_gain, *held)


def mlp_kernel(
    live, cot, normed, up, down_t, out_t, bias, *refs
):
    ffn, back, act_out, pre_out, ups_out, mix_out, sums = refs[-7:]
    t = pl.program_id(0)
    pre = dot(normed[...], up[...], NN) + bias[...]
    half = 0.5 * (1.0 + lax.erf(pre * (2.0**-0.5)))
    act = (pre * half).astype(BF16)
    slope = half + pre * (jnp.exp(-0.5 * pre * pre) * 0.3989422804014327)
    act_out[...] = act
    ffn[...] = dot(act, down_t[...], NT)
    place = lax.broadcasted_iota(jnp.int32, (TILE, 1), 0) + t * TILE
    ups32 = jnp.where(place < live[0], cot[...].astype(F32), 0.0)
    ups = ups32.astype(BF16)
    ups_out[...] = ups
    grad = (dot(ups, down_t[...], NN) * slope).astype(BF16)
    pre_out[...] = grad
    back[...] = dot(grad, up[...], NT)
    mixed = dot(ups, out_t[:, 3 * HL * HEAD :], NN).astype(BF16)
    for h in range(HL):
        mix_out[h] = mixed[:, h * HEAD : (h + 1) * HEAD]

    @pl.when(t == 0)
    def _():
        sums[...] = jnp.zeros_like(sums)

    sums[:, :D] += row_sum8(ups32)
    sums[:, D:] += row_sum8(grad.astype(F32))


def mlp(chunk, live, cot, normed, up, down_t, out_t, bias, buffers):
    whole = lambda shape: pl.BlockSpec(shape, lambda t: (0,) * len(shape))
    tile = pl.BlockSpec((TILE, D), lambda t: (t, 0))
    placed = pl.BlockSpec((TILE, D), lambda t: (chunk * PER + t, 0))
    held = [] if buffers is None else list(buffers)
    shapes = [jax.ShapeDtypeStruct((CH, D), F32)] * 2
    shapes += [jax.ShapeDtypeStruct((CAP, D), BF16)] * 3
    shapes += [jax.ShapeDtypeStruct((HL, CAP, HEAD), BF16)]
    shapes += [jax.ShapeDtypeStruct((8, 2 * D), F32)]
    return pl.pallas_call(
        mlp_kernel,
        grid=(PER,),
        in_specs=[
            pl.BlockSpec(memory_space=pltpu.SMEM),
            tile,
            placed,
            whole((D, HID)),
            whole((D, HID)),
            whole((D, D)),
            whole((1, HID)),
        ]
        + [pl.BlockSpec(memory_space=pl.ANY)] * len(held),
        out_specs=[tile, tile, placed, placed, placed]
        + [
            pl.BlockSpec((HL, TILE, HEAD), lambda t: (0, chunk * PER + t, 0)),
            whole((8, 2 * D)),
        ],
        out_shape=shapes,
        input_output_aliases={7 + i: 2 + i for i in range(len(held))},
        compiler_params=params(),
        cost_estimate=cost(8),
        name="mlp",
    )(live, cot, normed, up, down_t, out_t, bias, *held)


def attend_kernel(
    plan, q_ref, k_ref, v_ref, g_ref, q_hat, k_hat, seg_row, seg_col, q_gain, k_gain,
    mixed, dq_out, dk_out, dv_out, q_gain_grad, k_gain_grad,
    probs, pgrad, dq_sum, dk_sum, dv_sum,
):
    t = pl.program_id(0)

    @pl.when(t == 0)
    def _():
        dk_sum[...] = jnp.zeros_like(dk_sum)
        dv_sum[...] = jnp.zeros_like(dv_sum)
        q_gain_grad[...] = jnp.zeros_like(q_gain_grad)

    query = q_ref[0]
    grad = g_ref[0]

    @pl.when(plan[0] == 1)
    def _():
        total = jnp.zeros((QT, 128), F32)
        weighted = jnp.zeros((QT, 128), F32)
        for j in range(CAP // KS):
            part = slice(j * KS, (j + 1) * KS)
            e = jnp.exp(dot(query, k_ref[0, part], NT))
            probs[:, part] = e
            pg = dot(grad, v_ref[0, part], NT)
            pgrad[:, part] = pg
            total = total + lane_sum(e)
            weighted = weighted + lane_sum(e * pg)
        scale = 1.0 / jnp.sum(total, axis=1, keepdims=True)
        delta = jnp.sum(weighted, axis=1, keepdims=True) * scale
        out = jnp.zeros((QT, HEAD), F32)
        dq = jnp.zeros((QT, HEAD), F32)
        for j in range(CAP // KS):
            part = slice(j * KS, (j + 1) * KS)
            p = probs[:, part] * scale
            low = p.astype(BF16)
            ds = (p * (pgrad[:, part] - delta)).astype(BF16)
            out = out + dot(low, v_ref[0, part], NN)
            dq = dq + dot(ds, k_ref[0, part], NN)
            dv_sum[:, part] += dot(grad, low, TN)
            dk_sum[:, part] += dot(query, ds, TN)
        mixed[...] = out.astype(BF16)
        dq_sum[...] = dq

    @pl.when(plan[0] == 0)
    def _():
        first, count, live = plan[1 + t], plan[5 + t], plan[9 + t]
        seg = seg_col[...]

        def strip(i):
            return pl.ds(pl.multiple_of(lax.rem(first + i, CAP // MS) * MS, MS), MS)

        def scores(i, top):
            at = strip(i)
            s = dot(query, k_ref[0, at], NT)
            s = jnp.where(seg == seg_row[:, at], s, -1e30)
            probs[:, at] = s
            return jnp.maximum(top, jnp.max(s, axis=1, keepdims=True))

        top = lax.fori_loop(0, count, scores, jnp.full((QT, 1), -1e30, F32))

        def exps(i, total):
            at = strip(i)
            e = jnp.exp(probs[:, at] - top)
            probs[:, at] = e
            return total + jnp.sum(e, axis=1, keepdims=True)

        total = lax.fori_loop(0, count, exps, jnp.zeros((QT, 1), F32))
        scale = 1.0 / total

        def sums(i, out):
            at = strip(i)
            p = probs[:, at] * scale
            probs[:, at] = p
            return out + dot(p.astype(BF16), v_ref[0, at], NN)

        out = lax.fori_loop(0, count, sums, jnp.zeros((QT, HEAD), F32))
        mixed[...] = out.astype(BF16)
        dq_sum[...] = jnp.zeros_like(dq_sum)

        @pl.when(live == 1)
        def _():
            def deltas(i, delta):
                at = strip(i)
                pg = dot(grad, v_ref[0, at], NT)
                pgrad[:, at] = pg
                return delta + jnp.sum(probs[:, at] * pg, axis=1, keepdims=True)

            delta = lax.fori_loop(0, count, deltas, jnp.zeros((QT, 1), F32))

            def backs(i, carry):
                at = strip(i)
                p = probs[:, at]
                low = p.astype(BF16)
                ds = (p * (pgrad[:, at] - delta)).astype(BF16)
                dq_sum[...] += dot(ds, k_ref[0, at], NN)
                dv_sum[:, at] += dot(grad, low, TN)
                dk_sum[:, at] += dot(query, ds, TN)
                return carry

            lax.fori_loop(0, count, backs, 0)

    dq = dq_sum[...] * HEAD**-0.5
    hat = q_hat[0, :, :HEAD]
    q_gain_grad[...] += row_sum8(dq * hat)
    dq_out[...] = norm_back(dq * q_gain[...], hat, q_hat[0, :, HEAD : HEAD + 1]).astype(BF16)

    @pl.when(t == CAP // QT - 1)
    def _():
        dv_out[...] = dv_sum[...].T.astype(BF16)
        dk = dk_sum[...].T
        key_hat = k_hat[0, :, :HEAD]
        k_gain_grad[...] = row_sum8(dk * key_hat)
        back = norm_back(dk * k_gain[...], key_hat, k_hat[0, :, HEAD : HEAD + 1])
        dk_out[...] = back.astype(BF16)


def attend(head, plan, q, k, v, g, q_hat, k_hat, seg_row, seg_col, q_gain, k_gain):
    tile = lambda width: pl.BlockSpec((1, QT, width), lambda t: (head, t, 0))
    full = lambda width: pl.BlockSpec((1, CAP, width), lambda t: (head, 0, 0))
    whole = lambda shape: pl.BlockSpec(shape, lambda t: (0,) * len(shape))
    flat = jax.ShapeDtypeStruct((CAP, HEAD), BF16)
    return pl.pallas_call(
        attend_kernel,
        grid=(CAP // QT,),
        in_specs=[
            pl.BlockSpec(memory_space=pltpu.SMEM),
            tile(HEAD),
            full(HEAD),
            full(HEAD),
            tile(HEAD),
            tile(2 * HEAD),
            full(2 * HEAD),
            whole((1, CAP)),
            pl.BlockSpec((QT, 1), lambda t: (t, 0)),
            whole((1, HEAD)),
            whole((1, HEAD)),
        ],
        out_specs=[
            pl.BlockSpec((QT, HEAD), lambda t: (t, 0)),
            pl.BlockSpec((QT, HEAD), lambda t: (t, 0)),
            whole((CAP, HEAD)),
            whole((CAP, HEAD)),
            whole((8, HEAD)),
            whole((8, HEAD)),
        ],
        out_shape=[flat, flat, flat, flat]
        + [jax.ShapeDtypeStruct((8, HEAD), F32)] * 2,
        scratch_shapes=[
            pltpu.VMEM((QT, CAP), F32),
            pltpu.VMEM((QT, CAP), F32),
            pltpu.VMEM((QT, HEAD), F32),
            pltpu.VMEM((HEAD, CAP), F32),
            pltpu.VMEM((HEAD, CAP), F32),
        ],
        compiler_params=params(),
        cost_estimate=cost(15),
        name="attend",
    )(plan, q, k, v, g, q_hat, k_hat, seg_row, seg_col, q_gain, k_gain)


def late_weight_kernel(*refs):
    normed, ups = refs[:2]
    pieces = refs[2:14]
    out = refs[14]

    @pl.when(pl.program_id(0) == 0)
    def _():
        out[...] = jnp.zeros_like(out)

    cat = jnp.concatenate([r[...] for r in pieces[:9]], axis=1)
    mixed = jnp.concatenate([r[...] for r in pieces[9:]], axis=1)
    out[:, : 9 * HEAD] += dot(normed[...], cat, TN)
    out[:, 9 * HEAD :] += dot(ups[...], mixed, TN)


def late_weights(normed, ups, pieces):
    tile = lambda width: pl.BlockSpec((QT, width), lambda t: (t, 0))
    return pl.pallas_call(
        late_weight_kernel,
        grid=(CAP // QT,),
        in_specs=[tile(D), tile(D)] + [tile(HEAD)] * 12,
        out_specs=pl.BlockSpec((D, D), lambda t: (0, 0)),
        out_shape=jax.ShapeDtypeStruct((D, D), F32),
        compiler_params=params(),
        cost_estimate=cost(5),
        name="late_weights",
    )(normed, ups, *pieces)


def close_kernel(*refs):
    weight, rows, ffn, back = refs[:4]
    pieces = refs[4:16]
    out, grad, gains = refs[16:]
    cat = jnp.concatenate([r[...] for r in pieces[:9]], axis=1)
    mixed = jnp.concatenate([r[...] for r in pieces[9:]], axis=1)
    split = 9 * HEAD
    out[...] = (ffn[...] + dot(mixed, weight[:, split:], NT)).astype(out.dtype)
    total = back[...] + dot(cat, weight[:, :split], NT)
    grad[...] = total.astype(grad.dtype)
    hat, _ = norm_parts(rows[...].astype(F32))

    @pl.when(pl.program_id(0) == 0)
    def _():
        gains[...] = jnp.zeros_like(gains)

    gains[...] += row_sum8(total * hat)


def close(chunk, kind, weight, rows, ffn, back, pieces):
    tile = pl.BlockSpec((TILE, D), lambda t: (t, 0))
    piece = pl.BlockSpec((TILE, HEAD), lambda t: (chunk * PER + t, 0))
    return pl.pallas_call(
        close_kernel,
        grid=(PER,),
        in_specs=[pl.BlockSpec((D, D), lambda t: (0, 0)), tile, tile, tile] + [piece] * 12,
        out_specs=[tile, tile, pl.BlockSpec((8, D), lambda t: (0, 0))],
        out_shape=[jax.ShapeDtypeStruct((CH, D), kind)] * 2
        + [jax.ShapeDtypeStruct((8, D), F32)],
        compiler_params=params(),
        cost_estimate=cost(3),
        name="close",
    )(weight, rows, ffn, back, *pieces)


def dp_pairs(step):
    pairs = []
    for y in range(4):
        for z in range(4):
            for c in range(2):
                y2, z2, c2 = step(y, z, c)
                pairs.append(((y * 4 + z) * 2 + c, ((y2 % 4) * 4 + z2 % 4) * 2 + c2))
    return pairs


def move_x(value, k):
    return lax.ppermute(value, "branch", [(i, (i + k) % BR) for i in range(BR)])


def move_y(value, k):
    return lax.ppermute(value, "dp", dp_pairs(lambda y, z, c: (y + k, z, c)))


def move_z(value, k):
    return lax.ppermute(value, "dp", dp_pairs(lambda y, z, c: (y, z + k, c)))


def move_core(value):
    return lax.ppermute(value, "dp", dp_pairs(lambda y, z, c: (y, z, 1 - c)))


def put(buffer, value, index, axis):
    return lax.dynamic_update_index_in_dim(buffer, value, index, axis)


def take(buffer, index, axis):
    return lax.dynamic_index_in_dim(buffer, index, axis, keepdims=False)


def gather_weights(own, y, z, c):
    line = jnp.zeros((4, *own.shape), own.dtype)
    line = put(line, own, z, 0)
    for k in (1, 3, 2):
        line = put(line, move_z(own, -k), (z + k) % 4, 0)
    plane = jnp.zeros((4, *line.shape), own.dtype)
    plane = put(plane, line, y, 0)
    for k in (1, 3, 2):
        plane = put(plane, move_y(line, -k), (y + k) % 4, 0)
    other = move_core(plane)
    both = jnp.stack(
        [jnp.where(c == 0, plane, other), jnp.where(c == 0, other, plane)], axis=2
    )
    return both.reshape(32 * own.shape[0], own.shape[1])


def scatter_sum(grad, y, z, c):
    blocks = grad.reshape(4, 4, 2, grad.shape[0] // 32, grad.shape[1])
    other = move_core(take(blocks, 1 - c, 2).astype(BF16))
    plane = take(blocks, c, 2) + other.astype(F32)
    line = take(plane, y, 0)
    for k in (2, 1, 3):
        line = line + move_y(take(plane, (y + k) % 4, 0).astype(BF16), k).astype(F32)
    own = take(line, z, 0)
    for k in (2, 1, 3):
        own = own + move_z(take(line, (z + k) % 4, 0).astype(BF16), k).astype(F32)
    return own


def adam_update(weight, first_moment, second_moment, gradient, factor, rate, decay):
    clipped = gradient * factor
    first_new = BETA_ONE * first_moment + (1.0 - BETA_ONE) * clipped
    second_new = BETA_TWO * second_moment + (1.0 - BETA_TWO) * clipped * clipped
    ratio = (
        first_new
        / (1.0 - BETA_ONE**STEP)
        / (jnp.sqrt(second_new / (1.0 - BETA_TWO**STEP)) + EPS_ADAM)
    )
    return (clipped, second_new, weight - rate * (ratio + decay * weight))


def body(
    block_input,
    cotangent,
    image_owner,
    image_length,
    image_start,
    qkv_weight,
    qkv_first,
    qkv_second,
    out_weight,
    out_first,
    out_second,
    up_weight,
    up_first,
    up_second,
    down_weight,
    down_first,
    down_second,
    small_weight,
    small_first,
    small_second,
):
    b = lax.axis_index("branch")
    g = lax.axis_index("dp")
    y, z, c = g // 8, (g // 2) % 4, g % 2
    depth = up_weight.shape[0]

    rows = [block_input] + [move_x(block_input, -k) for k in (1, 2, 3)]
    cots = [cotangent] + [move_x(cotangent, -k) for k in (1, 2, 3)]

    proj_own = jnp.concatenate(
        [qkv_weight.transpose(1, 0, 2).reshape(depth, 3 * HL * HEAD), out_weight.T], axis=1
    ).astype(BF16)
    own = jnp.concatenate(
        [proj_own, up_weight.astype(BF16), down_weight.T.astype(BF16)], axis=1
    )
    gathered = gather_weights(own, y, z, c)
    proj, up, down_t = gathered[:, :D], gathered[:, D : D + HID], gathered[:, D + HID :]

    ln_gain = small_weight[:D][None]
    q_gain = small_weight[D : D + HEAD][None]
    k_gain = small_weight[D + HEAD : D + 2 * HEAD][None]
    out_bias = small_weight[D + 2 * HEAD : 2 * D + 2 * HEAD]
    hidden_bias = lax.dynamic_slice_in_dim(small_weight[2 * D + 2 * HEAD :], b * HID, HID)[None]

    mine = image_owner == g
    tokens = jnp.sum(jnp.where(mine, image_length, 0)).astype(jnp.int32)
    big = jnp.any(mine & (image_length == CAP))
    place = (jnp.arange(CAP, dtype=jnp.int32) + CH * b) % CAP
    labels = jnp.where(place < tokens, jnp.where(big, 0, place // SMALL_LEN), CAP)
    seg_row, seg_col = labels[None, :], labels[:, None]
    tile_place = (jnp.arange(CAP // QT, dtype=jnp.int32) * QT + CH * b) % CAP
    tile_last = tile_place + QT - 1
    begin = jnp.where(tile_place < tokens, tile_place // SMALL_LEN * SMALL_LEN, tokens)
    end = jnp.minimum((tile_last // SMALL_LEN + 1) * SMALL_LEN, tokens)
    end = jnp.where(tile_last >= tokens, CAP, end)
    begin = jnp.where(big, 0, begin)
    end = jnp.where(big, CAP, end)
    first_strip = (begin // MS - (CH // MS) * b) % (CAP // MS)
    strips = (end + MS - 1) // MS - begin // MS
    tile_live = (tile_place < tokens).astype(jnp.int32)
    bound = 8.0 * 1.02 * jnp.max(jnp.abs(q_gain)) * jnp.max(jnp.abs(k_gain))
    plain = (big & (bound <= SAFE)).astype(jnp.int32)[None]
    plan = jnp.concatenate([plain, first_strip, strips, tile_live]).astype(jnp.int32)
    chunk_place = (jnp.arange(BR, dtype=jnp.int32) + b) % BR * CH
    live = jnp.clip(tokens - chunk_place, 0, CH).astype(jnp.int32)

    held = None
    for k in (0, 1, 3, 2):
        held = project(k, rows[k], proj, ln_gain, q_gain, k_gain, held)
    normed, q, key, v, q_hat, k_hat = held

    ffn, back, sums = [None] * BR, [None] * BR, [None] * BR
    held = None
    for k in (0, 1, 3, 2):
        ffn[k], back[k], *held, sums[k] = mlp(
            k, live[k][None], cots[k], normed, up, down_t, proj, hidden_bias, held
        )
    act, pre_grad, ups, mixed_grad = held

    up_grad = dot(normed, pre_grad, TN)
    down_grad = dot(ups, act, TN)
    out_bias_part = jnp.sum(sums[0][:, :D], axis=0)
    hidden_bias_part = sum(jnp.sum(s[:, D:], axis=0) for s in sums)
    extra = jnp.pad(jnp.stack([out_bias_part, hidden_bias_part], axis=1), ((0, 0), (0, 126)))
    early = scatter_sum(jnp.concatenate([up_grad, down_grad, extra], axis=1), y, z, c)

    pieces = []
    for h in range(HL):
        pieces.append(
            attend(
                h, plan, q, key, v, mixed_grad, q_hat, k_hat, seg_row, seg_col, q_gain, k_gain
            )
        )
    flat = [pieces[h][i] for i in (1, 2, 3, 0) for h in range(HL)]
    q_gain_part = sum(jnp.sum(pieces[h][4], axis=0) for h in range(HL))
    k_gain_part = sum(jnp.sum(pieces[h][5], axis=0) for h in range(HL))

    late = scatter_sum(late_weights(normed, ups, flat), y, z, c)

    outs, grads, gain_parts = [None] * BR, [None] * BR, []
    for k in (2, 1, 3, 0):
        kind = F32 if k == 0 else BF16
        outs[k], grads[k], part = close(k, kind, proj, rows[k], ffn[k], back[k], flat)
        gain_parts.append(jnp.sum(part, axis=0))
    out_total, grad_total = outs[0], grads[0]
    for k in (2, 1, 3):
        out_total = out_total + move_x(outs[k], k).astype(F32)
        grad_total = grad_total + move_x(grads[k], k).astype(F32)
    block_output = (block_input.astype(F32) + out_total + out_bias).astype(BF16)
    hat, inverse = norm_parts(block_input.astype(F32))
    row_grad = norm_back(grad_total * ln_gain, hat, inverse)
    own_live = (jnp.arange(CH, dtype=jnp.int32) < live[0])[:, None]
    own_ups = jnp.where(own_live, cotangent.astype(F32), 0.0)
    input_grad = (own_ups + row_grad).astype(BF16)

    qkv_share = late[:, : 3 * HL * HEAD]
    out_share = late[:, 3 * HL * HEAD :]
    up_share = early[:, :HID]
    down_share = early[:, HID : 2 * HID]
    squares = (
        jnp.sum(qkv_share * qkv_share)
        + jnp.sum(out_share * out_share)
        + jnp.sum(up_share * up_share)
        + jnp.sum(down_share * down_share)
    )
    told = jnp.concatenate(
        [
            sum(gain_parts),
            q_gain_part,
            k_gain_part,
            early[:, 2 * HID],
            early[:, 2 * HID + 1],
            squares[None],
            jnp.zeros((1024 - D - 2 * HEAD - 2 * depth - 1,), F32),
        ]
    )
    told = jnp.broadcast_to(told[None, None], (128, 1, 1024))
    heard = lax.all_to_all(told, ("dp", "branch"), 0, 0, tiled=True).reshape(32, BR, 1024)
    base = D + 2 * HEAD
    gains_grad = jnp.sum(heard[:, :, :base], axis=(0, 1))
    out_bias_grad = jnp.sum(heard[:, :, base : base + depth], axis=1).reshape(D)
    hidden_bias_grad = heard[:, :, base + depth : base + 2 * depth]
    hidden_bias_grad = hidden_bias_grad.transpose(1, 0, 2).reshape(FF)
    small_grad = jnp.concatenate([gains_grad, out_bias_grad, hidden_bias_grad])
    squares_total = jnp.sum(heard[:, :, base + 2 * depth])
    grad_norm = jnp.sqrt(squares_total + jnp.sum(small_grad * small_grad))
    factor = 1.0 / jnp.maximum(grad_norm, 1.0)

    matrix = functools.partial(adam_update, factor=factor, rate=RATE_MATRIX, decay=DECAY_MATRIX)
    qkv_new = matrix(
        qkv_weight,
        qkv_first,
        qkv_second,
        qkv_share.reshape(depth, 3, HL * HEAD).transpose(1, 0, 2),
    )
    out_new = matrix(out_weight, out_first, out_second, out_share.T)
    up_new = matrix(up_weight, up_first, up_second, up_share)
    down_new = matrix(down_weight, down_first, down_second, down_share.T)
    small_new = adam_update(
        small_weight, small_first, small_second, small_grad, factor, RATE_SMALL, 0.0
    )
    return (
        block_output,
        input_grad,
        grad_norm,
        *qkv_new,
        *out_new,
        *up_new,
        *down_new,
        *small_new,
    )


def solution(mesh):
    rows = P(("dp", "branch"), None)
    qkv = [P(None, "dp", "branch")] * 3
    out = [P("branch", "dp")] * 3
    up = [P("dp", "branch")] * 3
    small = [P()] * 3
    return jax.shard_map(
        body,
        mesh=mesh,
        in_specs=(rows, rows, P(), P(), P(), *qkv, *out, *up, *out, *small),
        out_specs=(rows, rows, P(), *qkv, *out, *up, *out, *small),
        check_vma=False,
    )
```

```python
import functools

import jax
import jax.numpy as jnp
from jax import lax
from jax.experimental import pallas as pl
from jax.experimental.pallas import tpu as pltpu
from jax.sharding import PartitionSpec as P

D = 768
HEADS = 12
HEAD = 64
FF = 3072
CAP = 2048
SMALL_LEN = 196
STEP = 10

EPS_NORM = 1e-06
BETA_ONE = 0.9
BETA_TWO = 0.95
EPS_ADAM = 1e-08
RATE_MATRIX = 0.1
RATE_SMALL = 1.0
DECAY_MATRIX = 0.1

F32 = jnp.float32
BF16 = jnp.bfloat16
NN = (((1,), (0,)), ((), ()))
NT = (((1,), (1,)), ((), ()))
TN = (((0,), (0,)), ((), ()))

BR = 4
HL = HEADS // BR
HID = FF // BR
QK = 2 * HL * HEAD
QKV = 3 * HL * HEAD
OUT_AT = QKV + HEAD
PROJ = OUT_AT + HL * HEAD
EARLY = 2 * HID + 128
CH = CAP // BR
TILE = 256
PER = CH // TILE
QT = 512
KS = 512
MS = 256
SAFE = 60.0


def dot(left, right, dims):
    return lax.dot_general(left, right, dims, preferred_element_type=F32)


def cost(us):
    return pl.CostEstimate(flops=int(us * 1.1e9), bytes_accessed=0, transcendentals=0)


def params(mib):
    return pltpu.CompilerParams(vmem_limit_bytes=mib * 2**20)


def norm_parts(values):
    average = jnp.mean(values, axis=-1, keepdims=True)
    centered = values - average
    inverse = lax.rsqrt(jnp.mean(centered * centered, axis=-1, keepdims=True) + EPS_NORM)
    return (centered * inverse, inverse)


def norm_back(grad, hat, inverse):
    return inverse * (
        grad
        - jnp.mean(grad, axis=-1, keepdims=True)
        - hat * jnp.mean(grad * hat, axis=-1, keepdims=True)
    )


def lane_sum(values):
    width = values.shape[1] // 128
    total = values[:, :128]
    for i in range(1, width):
        total = total + values[:, i * 128 : (i + 1) * 128]
    return total


def row_sum8(values):
    return jnp.sum(values.reshape(values.shape[0] // 8, 8, values.shape[1]), axis=0)


def head_means(values, heads_matrix):
    high = values.astype(BF16)
    rest = (values - high.astype(F32)).astype(BF16)
    return dot(high, heads_matrix, NN) + dot(rest, heads_matrix, NN)


def heads_of(width):
    row = lax.broadcasted_iota(jnp.int32, (width, width), 0) // HEAD
    column = lax.broadcasted_iota(jnp.int32, (width, width), 1) // HEAD
    return jnp.where(row == column, 1.0 / HEAD, 0.0).astype(BF16)


def head_norm(pair, heads_matrix):
    centered = pair - head_means(pair, heads_matrix)
    inverse = lax.rsqrt(head_means(centered * centered, heads_matrix) + EPS_NORM)
    return (centered * inverse, inverse)


def plan_kernel(spot, owner, length, plan, live, seg_row, seg_col):
    group, branch, calm = spot[0], spot[1], spot[2]

    def count(i, found):
        tokens, big = found
        mine = owner[i] == group
        size = jnp.where(mine, length[i], 0)
        return tokens + size, jnp.maximum(big, jnp.where(size == CAP, 1, 0))

    tokens, big = lax.fori_loop(0, owner.shape[0], count, (0, 0))

    def label(shape, axis):
        place = lax.broadcasted_iota(jnp.int32, shape, axis) + CH * branch
        place = jnp.where(place >= CAP, place - CAP, place)
        image = jnp.where(big == 1, 0, (place * 2675) >> 19)
        return jnp.where(place < tokens, image, CAP)

    seg_row[...] = label((1, CAP), 1)
    seg_col[...] = label((CAP, 1), 0)
    plan[0] = jnp.where(calm == 1, 1 + big, 0)
    for t in range(CAP // QT):
        start = lax.rem(t * QT + CH * branch, CAP)
        last = start + QT - 1
        begin = jnp.where(start < tokens, ((start * 2675) >> 19) * SMALL_LEN, tokens)
        end = jnp.minimum((((last * 2675) >> 19) + 1) * SMALL_LEN, tokens)
        end = jnp.where(last >= tokens, CAP, end)
        begin = jnp.where(big == 1, 0, begin)
        end = jnp.where(big == 1, CAP, end)
        strip = begin // MS
        plan[1 + t] = lax.rem(strip + CAP // MS - (CH // MS) * branch, CAP // MS)
        plan[5 + t] = (end + MS - 1) // MS - strip
        plan[9 + t] = jnp.where(start < tokens, 1, 0)
        plan[21 + t] = jnp.where(last >= tokens, 1, 0)
    for t in range(CAP // MS):
        start = lax.rem(t * MS + CH * branch, CAP)
        plan[13 + t] = jnp.where(start < tokens, 1, 0)
    for k in range(BR):
        start = lax.rem((branch + k) * CH, CAP)
        live[k] = jnp.clip(tokens - start, 0, CH)


def make_plan(spot, owner, length):
    smem = pl.BlockSpec(memory_space=pltpu.SMEM)
    vmem = pl.BlockSpec(memory_space=pltpu.VMEM)
    return pl.pallas_call(
        plan_kernel,
        in_specs=[smem] * 3,
        out_specs=[smem, smem, vmem, vmem],
        out_shape=[
            jax.ShapeDtypeStruct((25,), jnp.int32),
            jax.ShapeDtypeStruct((BR,), jnp.int32),
            jax.ShapeDtypeStruct((1, CAP), jnp.int32),
            jax.ShapeDtypeStruct((CAP, 1), jnp.int32),
        ],
        cost_estimate=cost(2),
        name="make_plan",
    )(spot, owner, length)


def project_kernel(
    rows, weight, gain, qk_gain, heads_matrix, normed, q_out, k_out, v_out
):
    hat, _ = norm_parts(rows[...].astype(F32))
    low = (hat * gain[...]).astype(BF16)
    normed[...] = low
    raw = dot(low, weight[:, :QKV], NN)
    hat, _ = head_norm(raw[:, :QK], heads_matrix[...])
    value = (hat * qk_gain[...]).astype(BF16)
    vals = raw[:, QK:].astype(BF16)
    for h in range(HL):
        lane = slice(h * HEAD, (h + 1) * HEAD)
        q_out[h] = value[:, lane] * jnp.asarray(HEAD**-0.5, BF16)
        k_out[h] = value[:, QK // 2 + h * HEAD : QK // 2 + (h + 1) * HEAD]
        v_out[h] = vals[:, lane]


def project(rows, weights, gain, qk_gain, heads_matrix):
    whole = lambda shape: pl.BlockSpec(shape, lambda t: (0,) * len(shape))
    heads = pl.BlockSpec((HL, TILE, HEAD), lambda t: (0, t, 0))
    tile = pl.BlockSpec((TILE, D), lambda t: (t, 0))
    return pl.pallas_call(
        project_kernel,
        grid=(PER,),
        in_specs=[tile, whole((D, PROJ)), whole((1, D)), whole((1, QK)), whole((QK, QK))],
        out_specs=[tile, heads, heads, heads],
        out_shape=[jax.ShapeDtypeStruct((CH, D), BF16)]
        + [pltpu.HBM((HL, CH, HEAD), BF16)] * 3,
        compiler_params=params(16),
        cost_estimate=cost(3),
        name="project",
    )(rows, weights, gain, qk_gain, heads_matrix)


def mlp_kernel(
    live, cot, normed, up, down_t, proj, bias,
    ffn, back, act_out, pre_out, ups_out, mix_out,
):
    t = pl.program_id(0)
    pre = dot(normed[...], up[...], NN) + bias[...]
    half = 0.5 * (1.0 + lax.erf(pre * (2.0**-0.5)))
    act = (pre * half).astype(BF16)
    slope = half + pre * (jnp.exp(-0.5 * pre * pre) * 0.3989422804014327)
    act_out[...] = act
    ffn[...] = dot(act, down_t[...], NT).astype(ffn.dtype)
    place = lax.broadcasted_iota(jnp.int32, (TILE, 1), 0) + t * TILE
    ups = jnp.where(place < live[0], cot[...].astype(F32), 0.0).astype(BF16)
    ups_out[...] = ups
    grad = (dot(ups, down_t[...], NN) * slope).astype(BF16)
    pre_out[...] = grad
    back[...] = dot(grad, up[...], NT)
    mixed = dot(ups, proj[:, OUT_AT:], NN).astype(BF16)
    for h in range(HL):
        mix_out[h] = mixed[:, h * HEAD : (h + 1) * HEAD]


def mlp(live, cot, normed, perceptron, proj, bias, kind):
    whole = lambda shape: pl.BlockSpec(shape, lambda t: (0,) * len(shape))
    tile = pl.BlockSpec((TILE, D), lambda t: (t, 0))
    return pl.pallas_call(
        mlp_kernel,
        grid=(PER,),
        in_specs=[
            pl.BlockSpec(memory_space=pltpu.SMEM),
            tile,
            tile,
            pl.BlockSpec((D, HID), lambda t: (0, 0)),
            pl.BlockSpec((D, HID), lambda t: (0, 1)),
            whole((D, PROJ)),
            whole((1, HID)),
        ],
        out_specs=[tile] * 5 + [pl.BlockSpec((HL, TILE, HEAD), lambda t: (0, t, 0))],
        out_shape=[pltpu.HBM((CH, D), kind), pltpu.HBM((CH, D), F32)]
        + [jax.ShapeDtypeStruct((CH, D), BF16)] * 3
        + [pltpu.HBM((HL, CH, HEAD), BF16)],
        compiler_params=params(20),
        cost_estimate=cost(6),
        name="mlp",
    )(live, cot, normed, perceptron, perceptron, proj, bias)


def attend_kernel(plan, *refs):
    q_refs, k_refs, v_refs, g_refs = (refs[i * BR : (i + 1) * BR] for i in range(4))
    seg_row, seg_col, mixed, dq_out, dk_out, dv_out = refs[4 * BR : 4 * BR + 6]
    probs, pgrad, dk_sum, dv_sum, q_ref, k_ref, v_ref, g_ref = refs[4 * BR + 6 :]
    t = pl.program_id(0)
    for k in range(BR):

        @pl.when(t == k)
        def _():
            q_ref[...] = q_refs[k][...]
            g_ref[...] = g_refs[k][...]

    @pl.when(t == 0)
    def _():
        dk_sum[...] = jnp.zeros_like(dk_sum)
        dv_sum[...] = jnp.zeros_like(dv_sum)
        for k in range(BR):
            k_ref[:, k * CH : (k + 1) * CH] = k_refs[k][...]
            v_ref[:, k * CH : (k + 1) * CH] = v_refs[k][...]

    query = q_ref[0]
    grad = g_ref[0]

    @pl.when(plan[0] == 2)
    def _():
        total = jnp.zeros((QT, 128), F32)
        weighted = jnp.zeros((QT, 128), F32)
        for j in range(CAP // KS):
            part = slice(j * KS, (j + 1) * KS)
            e = jnp.exp(dot(query, k_ref[0, part], NT))
            probs[:, part] = e
            pg = dot(grad, v_ref[0, part], NT)
            pgrad[:, part] = pg
            total = total + lane_sum(e)
            weighted = weighted + lane_sum(e * pg)
        scale = 1.0 / jnp.sum(total, axis=1, keepdims=True)
        delta = jnp.sum(weighted, axis=1, keepdims=True) * scale
        out = jnp.zeros((QT, HEAD), F32)
        dq = jnp.zeros((QT, HEAD), F32)
        for j in range(CAP // KS):
            part = slice(j * KS, (j + 1) * KS)
            p = probs[:, part] * scale
            low = p.astype(BF16)
            ds = (p * (pgrad[:, part] - delta)).astype(BF16)
            out = out + dot(low, v_ref[0, part], NN)
            dq = dq + dot(ds, k_ref[0, part], NN)
            dv_sum[:, part] += dot(grad, low, TN)
            dk_sum[:, part] += dot(query, ds, TN)
        mixed[...] = out.astype(BF16)
        dq_out[...] = dq * HEAD**-0.5

    @pl.when(plan[0] == 1)
    def _():
        mixed[...] = jnp.zeros_like(mixed)
        dq_out[...] = jnp.zeros_like(dq_out)
        for s in range(QT // MS):
            index = t * (QT // MS) + s
            at = slice(s * MS, (s + 1) * MS)

            @pl.when(plan[13 + index] == 1)
            def _():
                qs, gs, seg = query[at], grad[at], seg_col[at, :]
                strips, es, pgs = [], [], []
                for j in range(3):
                    near = lax.rem(index + (CAP // MS - 1) + j, CAP // MS)
                    strip = pl.ds(pl.multiple_of(near * MS, MS), MS)
                    score = dot(qs, k_ref[0, strip], NT)
                    strips.append(strip)
                    es.append(jnp.where(seg == seg_row[:, strip], jnp.exp(score), 0.0))
                    pgs.append(dot(gs, v_ref[0, strip], NT))
                total = sum(lane_sum(e) for e in es)
                weighted = sum(lane_sum(e * pg) for e, pg in zip(es, pgs))
                scale = 1.0 / jnp.sum(total, axis=1, keepdims=True)
                delta = jnp.sum(weighted, axis=1, keepdims=True) * scale
                out = jnp.zeros((MS, HEAD), F32)
                dq = jnp.zeros((MS, HEAD), F32)
                for strip, e, pg in zip(strips, es, pgs):
                    p = e * scale
                    low = p.astype(BF16)
                    ds = (p * (pg - delta)).astype(BF16)
                    out = out + dot(low, v_ref[0, strip], NN)
                    dq = dq + dot(ds, k_ref[0, strip], NN)
                    dv_sum[:, strip] += dot(gs, low, TN)
                    dk_sum[:, strip] += dot(qs, ds, TN)
                mixed[at, :] = out.astype(BF16)
                dq_out[at, :] = dq * HEAD**-0.5

        @pl.when(plan[21 + t] == 1)
        def _():
            total = jnp.zeros((QT, 128), F32)
            for j in range(CAP // KS):
                part = slice(j * KS, (j + 1) * KS)
                e = jnp.exp(dot(query, k_ref[0, part], NT))
                e = jnp.where(seg_row[:, part] == CAP, e, 0.0)
                probs[:, part] = e
                total = total + lane_sum(e)
            scale = 1.0 / jnp.sum(total, axis=1, keepdims=True)
            out = jnp.zeros((QT, HEAD), F32)
            for j in range(CAP // KS):
                part = slice(j * KS, (j + 1) * KS)
                out = out + dot((probs[:, part] * scale).astype(BF16), v_ref[0, part], NN)
            mixed[...] = jnp.where(seg_col[...] == CAP, out, mixed[...].astype(F32)).astype(BF16)

    @pl.when(plan[0] == 0)
    def _():
        first, count, live = plan[1 + t], plan[5 + t], plan[9 + t]
        seg = seg_col[...]

        def strip(i):
            return pl.ds(pl.multiple_of(lax.rem(first + i, CAP // MS) * MS, MS), MS)

        def scores(i, top):
            at = strip(i)
            s = dot(query, k_ref[0, at], NT)
            s = jnp.where(seg == seg_row[:, at], s, -1e30)
            probs[:, at] = s
            return jnp.maximum(top, jnp.max(s, axis=1, keepdims=True))

        top = lax.fori_loop(0, count, scores, jnp.full((QT, 1), -1e30, F32))

        def exps(i, total):
            at = strip(i)
            e = jnp.exp(probs[:, at] - top)
            probs[:, at] = e
            return total + jnp.sum(e, axis=1, keepdims=True)

        total = lax.fori_loop(0, count, exps, jnp.zeros((QT, 1), F32))
        scale = 1.0 / total

        def sums(i, out):
            at = strip(i)
            p = probs[:, at] * scale
            probs[:, at] = p
            return out + dot(p.astype(BF16), v_ref[0, at], NN)

        out = lax.fori_loop(0, count, sums, jnp.zeros((QT, HEAD), F32))
        mixed[...] = out.astype(BF16)
        dq_out[...] = jnp.zeros_like(dq_out)

        @pl.when(live == 1)
        def _():
            def deltas(i, delta):
                at = strip(i)
                pg = dot(grad, v_ref[0, at], NT)
                pgrad[:, at] = pg
                return delta + jnp.sum(probs[:, at] * pg, axis=1, keepdims=True)

            delta = lax.fori_loop(0, count, deltas, jnp.zeros((QT, 1), F32))

            def backs(i, carry):
                at = strip(i)
                p = probs[:, at]
                low = p.astype(BF16)
                ds = (p * (pgrad[:, at] - delta)).astype(BF16)
                dq_out[...] += dot(ds, k_ref[0, at], NN) * HEAD**-0.5
                dv_sum[:, at] += dot(grad, low, TN)
                dk_sum[:, at] += dot(query, ds, TN)
                return carry

            lax.fori_loop(0, count, backs, 0)

    @pl.when(t == CAP // QT - 1)
    def _():
        dv_out[...] = dv_sum[...].T.astype(BF16)
        dk_out[...] = dk_sum[...].T


def attend(head, plan, q, k, v, g, seg_row, seg_col):
    chunk = pl.BlockSpec((1, CH, HEAD), lambda t: (head, 0, 0))
    whole = lambda shape: pl.BlockSpec(shape, lambda t: (0,) * len(shape))
    out = pl.BlockSpec((QT, HEAD), lambda t: (t, 0))
    flat = lambda kind: jax.ShapeDtypeStruct((CAP, HEAD), kind)
    return pl.pallas_call(
        attend_kernel,
        grid=(CAP // QT,),
        in_specs=[pl.BlockSpec(memory_space=pltpu.SMEM)]
        + [chunk] * (4 * BR)
        + [whole((1, CAP)), pl.BlockSpec((QT, 1), lambda t: (t, 0))],
        out_specs=[out, out, whole((CAP, HEAD)), whole((CAP, HEAD))],
        out_shape=[flat(BF16), flat(F32), flat(F32), flat(BF16)],
        scratch_shapes=[
            pltpu.VMEM((QT, CAP), F32),
            pltpu.VMEM((QT, CAP), F32),
            pltpu.VMEM((HEAD, CAP), F32),
            pltpu.VMEM((HEAD, CAP), F32),
            pltpu.VMEM((1, QT, HEAD), BF16),
            pltpu.VMEM((1, CAP, HEAD), BF16),
            pltpu.VMEM((1, CAP, HEAD), BF16),
            pltpu.VMEM((1, QT, HEAD), BF16),
        ],
        compiler_params=params(24),
        cost_estimate=cost(16),
        name="attend",
    )(plan, *q, *k, *v, *g, seg_row, seg_col)


def part_halves(core, total, kept, sent):
    depth = D // 32
    for i in range(16):
        here = pl.multiple_of((2 * i + core) * depth, 8)
        there = pl.multiple_of((2 * i + 1 - core) * depth, 8)
        kept[i] = total[pl.ds(here, depth), :]
        sent[i] = total[pl.ds(there, depth), :].astype(BF16)


def halves(width):
    shapes = [jax.ShapeDtypeStruct((16, D // 32, width), kind) for kind in (F32, BF16)]
    return shapes, [pl.BlockSpec((16, D // 32, width), lambda t: (0, 0, 0))] * 2


def early_kernel(core, *refs):
    normed, pre, ups, act = (refs[i * BR : (i + 1) * BR] for i in range(4))
    kept, sent, normed_out, ups_out, total = refs[4 * BR :]
    t = pl.program_id(0)

    @pl.when(t == 0)
    def _():
        total[...] = jnp.zeros_like(total)

    def joined(parts):
        return jnp.concatenate([part[...] for part in parts], axis=0)

    for k in range(BR):
        normed_out[k] = normed[k][...]
        ups_out[k] = ups[k][...]
    lane = lax.broadcasted_iota(jnp.int32, (CH, 128), 1)
    first = jnp.where(lane == 0, 1.0, 0.0).astype(BF16)
    second = jnp.where(lane == 1, 1.0, 0.0).astype(BF16)
    normed, pre, ups, act = joined(normed), joined(pre), joined(ups), joined(act)
    total[:, :HID] += dot(normed, pre, TN)
    total[:, HID : 2 * HID] += dot(ups, act, TN)
    total[:, 2 * HID :] += dot(ups, first, TN) + dot(pre, second, TN)

    @pl.when(t == BR - 1)
    def _():
        part_halves(core[0], total, kept, sent)


def early_weights(core, normed, pre, ups, act):
    tile = pl.BlockSpec((CH // BR, D), lambda t: (t, 0))
    joined = pl.BlockSpec((BR, CH // BR, D), lambda t: (0, t, 0))
    shapes, specs = halves(EARLY)
    return pl.pallas_call(
        early_kernel,
        grid=(BR,),
        in_specs=[pl.BlockSpec(memory_space=pltpu.SMEM)] + [tile] * (4 * BR),
        out_specs=specs + [joined] * 2,
        out_shape=shapes + [pltpu.HBM((BR, CH, D), BF16)] * 2,
        scratch_shapes=[pltpu.VMEM((D, EARLY), F32)],
        compiler_params=params(28),
        cost_estimate=cost(6),
        name="early_weights",
    )(core, *normed, *pre, *ups, *act)


def late_kernel(*refs):
    core, normed, ups, proj, qk_gain, heads_matrix = refs[:6]
    pieces = refs[6:18]
    kept, sent, grads_out, mixed_out, gains, out = refs[18:]
    t = pl.program_id(0)

    @pl.when(t == 0)
    def _():
        out[...] = jnp.zeros_like(out)
        gains[...] = jnp.zeros_like(gains)

    matrix = heads_matrix[...]
    hat, inverse = head_norm(dot(normed[0], proj[:, :QK], NN), matrix)
    pair = jnp.concatenate([r[...] for r in pieces[:6]], axis=1)
    gains[...] += row_sum8(pair * hat)
    scaled = pair * qk_gain[...]
    mean = head_means(scaled, matrix)
    slope = head_means(scaled * hat, matrix)
    raw = inverse * (scaled - mean - hat * slope)
    cat = jnp.concatenate([raw.astype(BF16)] + [r[...] for r in pieces[6:9]], axis=1)
    mixed = jnp.concatenate([r[...] for r in pieces[9:]], axis=1)
    grads_out[...] = cat
    mixed_out[...] = mixed
    out[:, :QKV] += dot(normed[0], cat, TN)
    out[:, QKV:] += dot(ups[0], mixed, TN)

    @pl.when(t == CAP // QT - 1)
    def _():
        part_halves(core[0], out, kept, sent)


def late_weights(core, normed, ups, proj, qk_gain, heads_matrix, pieces):
    tile = lambda width: pl.BlockSpec((QT, width), lambda t: (t, 0))
    whole = lambda shape: pl.BlockSpec(shape, lambda t: (0,) * len(shape))
    shapes, specs = halves(D)
    return pl.pallas_call(
        late_kernel,
        grid=(CAP // QT,),
        in_specs=[pl.BlockSpec(memory_space=pltpu.SMEM)]
        + [pl.BlockSpec((1, CH, D), lambda t: (t, 0, 0))] * 2
        + [whole((D, PROJ)), whole((1, QK)), whole((QK, QK))]
        + [tile(HEAD)] * 12,
        out_specs=specs + [tile(QKV), tile(HL * HEAD), whole((8, QK))],
        out_shape=shapes
        + [
            jax.ShapeDtypeStruct((CAP, QKV), BF16),
            jax.ShapeDtypeStruct((CAP, HL * HEAD), BF16),
            jax.ShapeDtypeStruct((8, QK), F32),
        ],
        scratch_shapes=[pltpu.VMEM((D, D), F32)],
        compiler_params=params(24),
        cost_estimate=cost(8),
        name="late_weights",
    )(core, normed, ups, proj, qk_gain, heads_matrix, *pieces)


def close_kernel(weight, rows, back, grads, out, gains):
    total = back[...] + dot(grads[...], weight[:, :QKV], NT)
    out[...] = total.astype(out.dtype)
    hat, _ = norm_parts(rows[...].astype(F32))

    @pl.when(pl.program_id(0) == 0)
    def _():
        gains[...] = jnp.zeros_like(gains)

    gains[...] += row_sum8(total * hat)


def close(chunk, weight, rows, back, grads):
    tile = pl.BlockSpec((TILE, D), lambda t: (t, 0))
    whole = lambda shape: pl.BlockSpec(shape, lambda t: (0,) * len(shape))
    return pl.pallas_call(
        close_kernel,
        grid=(PER,),
        in_specs=[
            whole((D, PROJ)),
            tile,
            tile,
            pl.BlockSpec((TILE, QKV), lambda t: (chunk * PER + t, 0)),
        ],
        out_specs=[tile, whole((8, D))],
        out_shape=[
            jax.ShapeDtypeStruct((CH, D), F32 if chunk == 0 else BF16),
            jax.ShapeDtypeStruct((8, D), F32),
        ],
        compiler_params=params(12),
        cost_estimate=cost(3),
        name="close",
    )(weight, rows, back, grads)


def output_kernel(rows, own, part1, part2, part3, bias, *refs):
    out = refs[-1]
    total = rows[...].astype(F32) + own[...] + bias[...]
    for part in (part1, part2, part3):
        total = total + part[...].astype(F32)
    for mixed, weight in zip(refs[:BR], refs[BR : 2 * BR]):
        total = total + dot(mixed[...], weight[...], NT)
    out[...] = total.astype(BF16)


def output_rows(rows, own, parts, bias, mixed, weights):
    tile = lambda width: pl.BlockSpec((TILE, width), lambda t: (t, 0))
    whole = lambda shape: pl.BlockSpec(shape, lambda t: (0,) * len(shape))
    return pl.pallas_call(
        output_kernel,
        grid=(PER,),
        in_specs=[tile(D)] * 5
        + [whole((1, D))]
        + [tile(HL * HEAD)] * BR
        + [whole((D, HL * HEAD))] * BR,
        out_specs=tile(D),
        out_shape=jax.ShapeDtypeStruct((CH, D), BF16),
        compiler_params=params(16),
        cost_estimate=cost(4),
        name="output_rows",
    )(rows, own, *parts, bias, *mixed, *weights)


def input_kernel(live, rows, cot, own, part1, part2, part3, gain, out):
    total = own[...]
    for part in (part1, part2, part3):
        total = total + part[...].astype(F32)
    hat, inverse = norm_parts(rows[...].astype(F32))
    place = lax.broadcasted_iota(jnp.int32, (TILE, 1), 0) + pl.program_id(0) * TILE
    ups = jnp.where(place < live[0], cot[...].astype(F32), 0.0)
    out[...] = (ups + norm_back(total * gain[...], hat, inverse)).astype(BF16)


def input_rows(live, rows, cot, own, parts, gain):
    tile = pl.BlockSpec((TILE, D), lambda t: (t, 0))
    return pl.pallas_call(
        input_kernel,
        grid=(PER,),
        in_specs=[pl.BlockSpec(memory_space=pltpu.SMEM)]
        + [tile] * 6
        + [pl.BlockSpec((1, D), lambda t: (0, 0))],
        out_specs=tile,
        out_shape=jax.ShapeDtypeStruct((CH, D), BF16),
        compiler_params=params(12),
        cost_estimate=cost(4),
        name="input_rows",
    )(live, rows, cot, own, *parts, gain)


def dp_pairs(step):
    pairs = []
    for y in range(4):
        for z in range(4):
            for c in range(2):
                y2, z2, c2 = step(y, z, c)
                pairs.append(((y * 4 + z) * 2 + c, ((y2 % 4) * 4 + z2 % 4) * 2 + c2))
    return pairs


def move_x(value, k):
    return lax.ppermute(value, "branch", [(i, (i + k) % BR) for i in range(BR)])


def move_y(value, k):
    return lax.ppermute(value, "dp", dp_pairs(lambda y, z, c: (y + k, z, c)))


def move_z(value, k):
    return lax.ppermute(value, "dp", dp_pairs(lambda y, z, c: (y, z + k, c)))


def move_core(value):
    return lax.ppermute(value, "dp", dp_pairs(lambda y, z, c: (y, z, 1 - c)))


def put(buffer, value, index, axis):
    return lax.dynamic_update_index_in_dim(buffer, value, index, axis)


def take(buffer, index, axis):
    return lax.dynamic_index_in_dim(buffer, index, axis, keepdims=False)


def gather_weights(own, y, z, c):
    line = jnp.zeros((4, *own.shape), own.dtype)
    line = put(line, own, z, 0)
    for k in (1, 3, 2):
        line = put(line, move_z(own, -k), (z + k) % 4, 0)
    plane = jnp.zeros((4, *line.shape), own.dtype)
    plane = put(plane, line, y, 0)
    for k in (1, 3, 2):
        plane = put(plane, move_y(line, -k), (y + k) % 4, 0)
    whole = jnp.zeros((4, 4, 2, *own.shape), own.dtype)
    whole = put(whole, plane, c, 2)
    whole = put(whole, move_core(plane), 1 - c, 2)
    return whole.reshape(32 * own.shape[0], own.shape[1]), line


def after(values, *earlier):
    return lax.optimization_barrier((values, earlier))[0]


def gather_rows(own):
    right, left = move_x(own, -1), move_x(own, 1)
    half = own.shape[0] // 2
    far = [move_x(right[:half], -1), move_x(left[half:], 1)]
    return [own, right, jnp.concatenate(far, axis=0), left]


def sum_cores(kept, sent):
    total = kept + move_core(sent).astype(F32)
    return total.reshape(4, 4, *total.shape[1:])


def sum_ring(blocks, index, move):
    total = take(blocks, index, 0)
    for k in (2, 1, 3):
        total = total + move(take(blocks, (index + k) % 4, 0).astype(BF16), k).astype(F32)
    return total


def adam_update(weight, first_moment, second_moment, gradient, factor, rate, decay):
    clipped = gradient * factor
    first_new = BETA_ONE * first_moment + (1.0 - BETA_ONE) * clipped
    second_new = BETA_TWO * second_moment + (1.0 - BETA_TWO) * clipped * clipped
    ratio = (
        first_new
        / (1.0 - BETA_ONE**STEP)
        / (jnp.sqrt(second_new / (1.0 - BETA_TWO**STEP)) + EPS_ADAM)
    )
    return (clipped, second_new, weight - rate * (ratio + decay * weight))


def body(
    block_input,
    cotangent,
    image_owner,
    image_length,
    image_start,
    qkv_weight,
    qkv_first,
    qkv_second,
    out_weight,
    out_first,
    out_second,
    up_weight,
    up_first,
    up_second,
    down_weight,
    down_first,
    down_second,
    small_weight,
    small_first,
    small_second,
):
    b = lax.axis_index("branch")
    g = lax.axis_index("dp")
    y, z, c = g // 8, (g // 2) % 4, g % 2
    depth = up_weight.shape[0]

    low = lambda value: value.astype(BF16)
    proj_own = jnp.concatenate(
        [
            low(qkv_weight).transpose(1, 0, 2).reshape(depth, QKV),
            jnp.zeros((depth, OUT_AT - QKV), BF16),
            low(out_weight).T,
        ],
        axis=1,
    )
    mlp_own = jnp.concatenate([low(up_weight), low(down_weight).T], axis=1)
    proj, line = gather_weights(proj_own, y, z, c)
    perceptron, _ = gather_weights(after(mlp_own, line), y, z, c)
    out_t = proj[:, OUT_AT:]

    rows = gather_rows(block_input)
    cots = gather_rows(after(cotangent, rows[1], rows[3]))

    small_early, image_owner = after((small_weight, image_owner), line)
    ln_gain = small_early[:D][None]
    q_gain = small_early[D : D + HEAD]
    k_gain = small_early[D + HEAD : D + 2 * HEAD]
    qk_gain = jnp.concatenate([q_gain] * HL + [k_gain] * HL)[None]
    out_bias = small_early[D + 2 * HEAD : 2 * D + 2 * HEAD][None]
    hidden_bias = lax.dynamic_slice_in_dim(small_early[2 * D + 2 * HEAD :], b * HID, HID)[None]
    heads_matrix = heads_of(QK)
    core = c[None].astype(jnp.int32)

    bound = 8.0 * 1.02 * jnp.max(jnp.abs(q_gain)) * jnp.max(jnp.abs(k_gain))
    spot = jnp.stack([g, b, (bound <= SAFE)]).astype(jnp.int32)
    plan, live, seg_row, seg_col = make_plan(spot, image_owner, image_length)

    normed, q, key, v = [None] * BR, [None] * BR, [None] * BR, [None] * BR
    for k in (0, 1, 3, 2):
        normed[k], q[k], key[k], v[k] = project(rows[k], proj, ln_gain, qk_gain, heads_matrix)

    ffn, back, act, pre, ups, mixed_grad = ([None] * BR for _ in range(6))
    for k in (0, 1, 3, 2):
        ffn[k], back[k], act[k], pre[k], ups[k], mixed_grad[k] = mlp(
            live[k][None], cots[k], normed[k], perceptron, proj, hidden_bias, BF16 if k else F32
        )

    ffn_parts = [move_x(ffn[k], k) for k in (1, 2, 3)]
    out_ts = [out_t] + [move_x(out_t, k) for k in (1, 2, 3)]
    kept, sent, normed, ups = early_weights(core, normed, pre, ups, act)
    pieces = [attend(0, plan, q, key, v, after(mixed_grad, sent), seg_row, seg_col)]
    plane = sum_cores(kept, sent)
    gate = after(mixed_grad, plane, ffn_parts[0])
    pieces.append(attend(1, plan, q, key, v, gate, seg_row, seg_col))
    line = sum_ring(plane, y, move_y)
    gate = after(mixed_grad, line, ffn_parts[1], ffn_parts[2])
    pieces.append(attend(2, plan, q, key, v, gate, seg_row, seg_col))
    early = sum_ring(line, z, move_z)

    flat = [pieces[h][i] for i in (1, 2, 3, 0) for h in range(HL)]
    flat[0] = after(flat[0], early, out_ts)
    kept, sent, qkv_grads, mixed, gains_part = late_weights(
        core, normed, ups, proj, qk_gain, heads_matrix, flat
    )
    gains_part = jnp.sum(gains_part, axis=0).reshape(2, HL, HEAD)
    qk_gain_part = jnp.sum(gains_part, axis=1).reshape(2 * HEAD)
    late = sum_ring(sum_ring(sum_cores(kept, sent), y, move_y), z, move_z)

    mixed = [mixed[:CH]] + [move_x(mixed[k * CH : (k + 1) * CH], k) for k in (1, 2, 3)]
    block_output = output_rows(block_input, ffn[0], ffn_parts, out_bias, mixed, out_ts)

    grads, gain_parts = [None] * BR, []
    for k in (2, 1, 3, 0):
        grads[k], part = close(k, proj, rows[k], back[k], qkv_grads)
        gain_parts.append(jnp.sum(part, axis=0))
    input_grad = input_rows(
        live[:1],
        block_input,
        cotangent,
        grads[0],
        [move_x(grads[k], k) for k in (1, 2, 3)],
        ln_gain,
    )

    qkv_share = late[:, :QKV]
    out_share = late[:, QKV:]
    up_share = early[:, :HID]
    down_share = early[:, HID : 2 * HID]
    squares = (
        jnp.sum(qkv_share * qkv_share)
        + jnp.sum(out_share * out_share)
        + jnp.sum(up_share * up_share)
        + jnp.sum(down_share * down_share)
    )
    told = jnp.concatenate(
        [
            sum(gain_parts),
            qk_gain_part,
            early[:, 2 * HID],
            early[:, 2 * HID + 1],
            squares[None],
            jnp.zeros((1024 - D - 2 * HEAD - 2 * depth - 1,), F32),
        ]
    )
    told = jnp.broadcast_to(told[None, None], (128, 1, 1024))
    heard = lax.all_to_all(told, ("dp", "branch"), 0, 0, tiled=True).reshape(32, BR, 1024)
    base = D + 2 * HEAD
    gains_grad = jnp.sum(heard[:, :, :base], axis=(0, 1))
    out_bias_grad = heard[:, 0, base : base + depth].reshape(D)
    hidden_bias_grad = heard[:, :, base + depth : base + 2 * depth]
    hidden_bias_grad = hidden_bias_grad.transpose(1, 0, 2).reshape(FF)
    small_grad = jnp.concatenate([gains_grad, out_bias_grad, hidden_bias_grad])
    squares_total = jnp.sum(heard[:, :, base + 2 * depth])
    grad_norm = jnp.sqrt(squares_total + jnp.sum(small_grad * small_grad))
    factor = 1.0 / jnp.maximum(grad_norm, 1.0)

    matrix = functools.partial(adam_update, factor=factor, rate=RATE_MATRIX, decay=DECAY_MATRIX)
    qkv_new = matrix(
        qkv_weight,
        qkv_first,
        qkv_second,
        qkv_share.reshape(depth, 3, HL * HEAD).transpose(1, 0, 2),
    )
    out_new = matrix(out_weight, out_first, out_second, out_share.T)
    up_new = matrix(up_weight, up_first, up_second, up_share)
    down_new = matrix(down_weight, down_first, down_second, down_share.T)
    small_new = adam_update(
        small_weight, small_first, small_second, small_grad, factor, RATE_SMALL, 0.0
    )
    return (
        block_output,
        input_grad,
        grad_norm,
        *qkv_new,
        *out_new,
        *up_new,
        *down_new,
        *small_new,
    )


def solution(mesh):
    rows = P(("dp", "branch"), None)
    qkv = [P(None, "dp", "branch")] * 3
    out = [P("branch", "dp")] * 3
    up = [P("dp", "branch")] * 3
    small = [P()] * 3
    return jax.shard_map(
        body,
        mesh=mesh,
        in_specs=(rows, rows, P(), P(), P(), *qkv, *out, *up, *out, *small),
        out_specs=(rows, rows, P(), *qkv, *out, *up, *out, *small),
        check_vma=False,
    )
```

```python
import functools

import jax
import jax.numpy as jnp
from jax import lax
from jax.experimental import pallas as pl
from jax.experimental.pallas import tpu as pltpu
from jax.sharding import PartitionSpec as P

D = 768
HEADS = 12
HEAD = 64
FF = 3072
CAP = 2048
SMALL_LEN = 196
STEP = 10

EPS_NORM = 1e-06
BETA_ONE = 0.9
BETA_TWO = 0.95
EPS_ADAM = 1e-08
RATE_MATRIX = 0.1
RATE_SMALL = 1.0
DECAY_MATRIX = 0.1

F32 = jnp.float32
BF16 = jnp.bfloat16
NN = (((1,), (0,)), ((), ()))
NT = (((1,), (1,)), ((), ()))
TN = (((0,), (0,)), ((), ()))

BR = 4
HL = HEADS // BR
HID = FF // BR
QK = 2 * HL * HEAD
QKV = 3 * HL * HEAD
EARLY = 2 * HID + 128
CH = CAP // BR
MSG = CH + HL * HEAD
TILE = 256
PER = CH // TILE
QT = 512
KS = 512
MS = 256
SAFE = 60.0


def dot(left, right, dims):
    return lax.dot_general(left, right, dims, preferred_element_type=F32)


def cost(us):
    return pl.CostEstimate(flops=int(us * 1.1e9), bytes_accessed=0, transcendentals=0)


def params(mib):
    return pltpu.CompilerParams(vmem_limit_bytes=mib * 2**20)


def far_from(arrays):
    return [pltpu.with_memory_space_constraint(value, pltpu.HBM) for value in arrays]


def norm_parts(values):
    average = jnp.mean(values, axis=-1, keepdims=True)
    centered = values - average
    inverse = lax.rsqrt(jnp.mean(centered * centered, axis=-1, keepdims=True) + EPS_NORM)
    return (centered * inverse, inverse)


def norm_back(grad, hat, inverse):
    return inverse * (
        grad
        - jnp.mean(grad, axis=-1, keepdims=True)
        - hat * jnp.mean(grad * hat, axis=-1, keepdims=True)
    )


def lane_sum(values):
    width = values.shape[1] // 128
    total = values[:, :128]
    for i in range(1, width):
        total = total + values[:, i * 128 : (i + 1) * 128]
    return total


def row_sum8(values):
    return jnp.sum(values.reshape(values.shape[0] // 8, 8, values.shape[1]), axis=0)


def head_means(values, heads_matrix):
    high = values.astype(BF16)
    rest = (values - high.astype(F32)).astype(BF16)
    return dot(high, heads_matrix, NN) + dot(rest, heads_matrix, NN)


def heads_of(width):
    row = lax.broadcasted_iota(jnp.int32, (width, width), 0) >> 6
    column = lax.broadcasted_iota(jnp.int32, (width, width), 1) >> 6
    return jnp.where(row == column, 1.0 / HEAD, 0.0).astype(BF16)


def head_norm(pair, heads_matrix):
    centered = pair - head_means(pair, heads_matrix)
    inverse = lax.rsqrt(head_means(centered * centered, heads_matrix) + EPS_NORM)
    return (centered * inverse, inverse)


def pack_kernel(up, down_t, qkv, out_t, packed):
    packed[:, :HID] = up[...].astype(BF16)
    packed[:, HID : 2 * HID] = down_t[...].astype(BF16)
    parts = [qkv[j] for j in range(3)] + [out_t[...]]
    packed[:, 2 * HID :] = jnp.concatenate(parts, axis=1).astype(BF16)


def pack(up, down_t, qkv, out_t):
    return pl.pallas_call(
        pack_kernel,
        out_shape=jax.ShapeDtypeStruct((D // 32, 2 * HID + D), BF16),
        cost_estimate=cost(1),
        name="pack",
    )(up, down_t, qkv, out_t)


def plan_kernel(
    small, owner, length,
    plan, live, seg_row, seg_col, ln_gain, qk_gain, out_bias, hidden_bias,
):
    group, branch = lax.axis_index("dp"), lax.axis_index("branch")
    gains = D // 128
    for i in range(gains):
        lane = slice(i * 128, (i + 1) * 128)
        ln_gain[:, lane] = small[i : i + 1, :]
        out_bias[:, lane] = small[gains + 1 + i : gains + 2 + i, :]
        hidden_bias[:, lane] = small[pl.ds(2 * gains + 1 + branch * (HID // 128) + i, 1), :]
    both = small[gains : gains + 1, :]
    q_gain, k_gain = both[:, :HEAD], both[:, HEAD:]
    qk_gain[...] = jnp.concatenate([q_gain] * HL + [k_gain] * HL, axis=1)
    bound = 8.0 * 1.02 * jnp.max(jnp.abs(q_gain)) * jnp.max(jnp.abs(k_gain))

    size = jnp.where(owner[...] == group, length[...], 0)
    tokens = jnp.sum(size)
    big = jnp.where(jnp.max(size) == CAP, 1, 0)

    def label(shape, axis):
        place = lax.broadcasted_iota(jnp.int32, shape, axis) + CH * branch
        place = jnp.where(place >= CAP, place - CAP, place)
        image = jnp.where(big == 1, 0, (place * 2675) >> 19)
        return jnp.where(place < tokens, image, CAP)

    seg_row[...] = label((1, CAP), 1)
    seg_col[...] = label((CAP, 1), 0)
    plan[0] = jnp.where(bound <= SAFE, 1 + big, 0)
    for t in range(CAP // QT):
        start = lax.rem(t * QT + CH * branch, CAP)
        last = start + QT - 1
        begin = jnp.where(start < tokens, ((start * 2675) >> 19) * SMALL_LEN, tokens)
        end = jnp.minimum((((last * 2675) >> 19) + 1) * SMALL_LEN, tokens)
        end = jnp.where(last >= tokens, CAP, end)
        begin = jnp.where(big == 1, 0, begin)
        end = jnp.where(big == 1, CAP, end)
        strip = begin // MS
        plan[1 + t] = lax.rem(strip + CAP // MS - (CH // MS) * branch, CAP // MS)
        plan[5 + t] = (end + MS - 1) // MS - strip
        plan[9 + t] = jnp.where(start < tokens, 1, 0)
        plan[21 + t] = jnp.where(last >= tokens, 1, 0)
    for t in range(CAP // MS):
        start = lax.rem(t * MS + CH * branch, CAP)
        plan[13 + t] = jnp.where(start < tokens, 1, 0)
    for k in range(BR):
        start = lax.rem((branch + k) * CH, CAP)
        live[k] = jnp.clip(tokens - start, 0, CH)


def make_plan(small, owner, length):
    smem = pl.BlockSpec(memory_space=pltpu.SMEM)
    vmem = pl.BlockSpec(memory_space=pltpu.VMEM)
    row = lambda width, kind=F32: jax.ShapeDtypeStruct((1, width), kind)
    return pl.pallas_call(
        plan_kernel,
        in_specs=[vmem] * 3,
        out_specs=[smem, smem] + [vmem] * 6,
        out_shape=[
            jax.ShapeDtypeStruct((25,), jnp.int32),
            jax.ShapeDtypeStruct((BR,), jnp.int32),
            row(CAP, jnp.int32),
            jax.ShapeDtypeStruct((CAP, 1), jnp.int32),
            row(D),
            row(QK),
            row(D),
            row(HID),
        ],
        cost_estimate=cost(3),
        name="make_plan",
    )(small, owner, length)


def project_kernel(
    rows, weight, gain, qk_gain, normed, q_out, k_out, v_out, qk_hat, qk_inverse
):
    hat, _ = norm_parts(rows[...].astype(F32))
    low = (hat * gain[...]).astype(BF16)
    normed[...] = low
    raw = dot(low, weight[:, :QKV], NN)
    hat, inverse = head_norm(raw[:, :QK], heads_of(QK))
    qk_hat[...] = hat
    qk_inverse[...] = inverse
    value = (hat * qk_gain[...]).astype(BF16)
    vals = raw[:, QK:].astype(BF16)
    for h in range(HL):
        lane = slice(h * HEAD, (h + 1) * HEAD)
        q_out[h] = value[:, lane] * jnp.asarray(HEAD**-0.5, BF16)
        k_out[h] = value[:, QK // 2 + h * HEAD : QK // 2 + (h + 1) * HEAD]
        v_out[h] = vals[:, lane]


def project(rows, weights, gain, qk_gain):
    whole = lambda shape: pl.BlockSpec(shape, lambda t: (0,) * len(shape))
    heads = pl.BlockSpec((HL, TILE, HEAD), lambda t: (0, t, 0))
    tile = pl.BlockSpec((TILE, D), lambda t: (t, 0))
    return pl.pallas_call(
        project_kernel,
        grid=(PER,),
        in_specs=[
            tile,
            pl.BlockSpec((D, D), lambda t: (0, 2)),
            whole((1, D)),
            whole((1, QK)),
        ],
        out_specs=[tile, heads, heads, heads] + [pl.BlockSpec((TILE, QK), lambda t: (t, 0))] * 2,
        out_shape=[jax.ShapeDtypeStruct((CH, D), BF16)]
        + [pltpu.HBM((HL, CH, HEAD), BF16)] * 3
        + [pltpu.HBM((CH, QK), F32)] * 2,
        compiler_params=params(16),
        cost_estimate=cost(3),
        name="project",
    )(rows, weights, gain, qk_gain)


def mlp_kernel(
    live, cot, normed, up, down_t, proj, bias,
    ffn, back, act_out, pre_out, ups_out, mix_out,
):
    t = pl.program_id(0)
    pre = dot(normed[...], up[...], NN) + bias[...]
    half = 0.5 * (1.0 + lax.erf(pre * (2.0**-0.5)))
    act = (pre * half).astype(BF16)
    slope = half + pre * (jnp.exp(-0.5 * pre * pre) * 0.3989422804014327)
    act_out[...] = act
    ffn[pl.ds(t * TILE, TILE), :] = dot(act, down_t[...], NT).astype(ffn.dtype)
    place = lax.broadcasted_iota(jnp.int32, (TILE, 1), 0) + t * TILE
    ups = jnp.where(place < live[0], cot[...].astype(F32), 0.0).astype(BF16)
    ups_out[...] = ups
    grad = (dot(ups, down_t[...], NN) * slope).astype(BF16)
    pre_out[...] = grad
    back[...] = dot(grad, up[...], NT)
    mixed = dot(ups, proj[:, QKV:], NN).astype(BF16)
    if ffn.shape[0] > CH:

        @pl.when(t == 0)
        def _():
            ffn[CH:, :] = proj[:, QKV:].astype(F32).T.astype(BF16)

    for h in range(HL):
        mix_out[h] = mixed[:, h * HEAD : (h + 1) * HEAD]


def mlp(live, cot, normed, weights, bias, height, kind):
    whole = lambda shape: pl.BlockSpec(shape, lambda t: (0,) * len(shape))
    tile = pl.BlockSpec((TILE, D), lambda t: (t, 0))
    return pl.pallas_call(
        mlp_kernel,
        grid=(PER,),
        in_specs=[
            pl.BlockSpec(memory_space=pltpu.SMEM),
            tile,
            tile,
            pl.BlockSpec((D, HID), lambda t: (0, 0)),
            pl.BlockSpec((D, HID), lambda t: (0, 1)),
            pl.BlockSpec((D, D), lambda t: (0, 2)),
            whole((1, HID)),
        ],
        out_specs=[whole((height, D))]
        + [tile] * 4
        + [pl.BlockSpec((HL, TILE, HEAD), lambda t: (0, t, 0))],
        out_shape=[pltpu.HBM((height, D), kind), pltpu.HBM((CH, D), F32)]
        + [jax.ShapeDtypeStruct((CH, D), BF16)] * 3
        + [pltpu.HBM((HL, CH, HEAD), BF16)],
        compiler_params=params(20),
        cost_estimate=cost(6),
        name="mlp",
    )(live, cot, normed, weights, weights, weights, bias)


def attend_kernel(plan, *refs):
    q_refs, k_refs, v_refs, g_refs = (refs[i * BR : (i + 1) * BR] for i in range(4))
    seg_row, seg_col, mixed, dq_out, dk_out, dv_out = refs[4 * BR : 4 * BR + 6]
    probs, pgrad, dk_sum, dv_sum, q_ref, k_ref, v_ref, g_ref = refs[4 * BR + 6 :]
    t = pl.program_id(1)
    for k in range(BR):

        @pl.when(t == k)
        def _():
            q_ref[...] = q_refs[k][...]
            g_ref[...] = g_refs[k][...]

    @pl.when(t == 0)
    def _():
        dk_sum[...] = jnp.zeros_like(dk_sum)
        dv_sum[...] = jnp.zeros_like(dv_sum)
        for k in range(BR):
            k_ref[:, k * CH : (k + 1) * CH] = k_refs[k][...]
            v_ref[:, k * CH : (k + 1) * CH] = v_refs[k][...]

    query = q_ref[0]
    grad = g_ref[0]

    @pl.when(plan[0] == 2)
    def _():
        total = jnp.zeros((QT, 128), F32)
        weighted = jnp.zeros((QT, 128), F32)
        for j in range(CAP // KS):
            part = slice(j * KS, (j + 1) * KS)
            e = jnp.exp(dot(query, k_ref[0, part], NT))
            probs[:, part] = e
            pg = dot(grad, v_ref[0, part], NT)
            pgrad[:, part] = pg
            total = total + lane_sum(e)
            weighted = weighted + lane_sum(e * pg)
        scale = 1.0 / jnp.sum(total, axis=1, keepdims=True)
        delta = jnp.sum(weighted, axis=1, keepdims=True) * scale
        out = jnp.zeros((QT, HEAD), F32)
        dq = jnp.zeros((QT, HEAD), F32)
        for j in range(CAP // KS):
            part = slice(j * KS, (j + 1) * KS)
            p = probs[:, part] * scale
            low = p.astype(BF16)
            ds = (p * (pgrad[:, part] - delta)).astype(BF16)
            out = out + dot(low, v_ref[0, part], NN)
            dq = dq + dot(ds, k_ref[0, part], NN)
            dv_sum[:, part] += dot(grad, low, TN)
            dk_sum[:, part] += dot(query, ds, TN)
        mixed[0] = out.astype(BF16)
        dq_out[0] = dq * HEAD**-0.5

    @pl.when(plan[0] == 1)
    def _():
        mixed[...] = jnp.zeros_like(mixed)
        dq_out[...] = jnp.zeros_like(dq_out)
        for s in range(QT // MS):
            index = t * (QT // MS) + s
            at = slice(s * MS, (s + 1) * MS)

            @pl.when(plan[13 + index] == 1)
            def _():
                qs, gs, seg = query[at], grad[at], seg_col[at, :]
                strips, es, pgs = [], [], []
                for j in range(3):
                    near = lax.rem(index + (CAP // MS - 1) + j, CAP // MS)
                    strip = pl.ds(pl.multiple_of(near * MS, MS), MS)
                    score = dot(qs, k_ref[0, strip], NT)
                    strips.append(strip)
                    es.append(jnp.where(seg == seg_row[:, strip], jnp.exp(score), 0.0))
                    pgs.append(dot(gs, v_ref[0, strip], NT))
                total = sum(lane_sum(e) for e in es)
                weighted = sum(lane_sum(e * pg) for e, pg in zip(es, pgs))
                scale = 1.0 / jnp.sum(total, axis=1, keepdims=True)
                delta = jnp.sum(weighted, axis=1, keepdims=True) * scale
                out = jnp.zeros((MS, HEAD), F32)
                dq = jnp.zeros((MS, HEAD), F32)
                for strip, e, pg in zip(strips, es, pgs):
                    p = e * scale
                    low = p.astype(BF16)
                    ds = (p * (pg - delta)).astype(BF16)
                    out = out + dot(low, v_ref[0, strip], NN)
                    dq = dq + dot(ds, k_ref[0, strip], NN)
                    dv_sum[:, strip] += dot(gs, low, TN)
                    dk_sum[:, strip] += dot(qs, ds, TN)
                mixed[0, at, :] = out.astype(BF16)
                dq_out[0, at, :] = dq * HEAD**-0.5

        @pl.when(plan[21 + t] == 1)
        def _():
            total = jnp.zeros((QT, 128), F32)
            for j in range(CAP // KS):
                part = slice(j * KS, (j + 1) * KS)
                e = jnp.exp(dot(query, k_ref[0, part], NT))
                e = jnp.where(seg_row[:, part] == CAP, e, 0.0)
                probs[:, part] = e
                total = total + lane_sum(e)
            scale = 1.0 / jnp.sum(total, axis=1, keepdims=True)
            out = jnp.zeros((QT, HEAD), F32)
            for j in range(CAP // KS):
                part = slice(j * KS, (j + 1) * KS)
                out = out + dot((probs[:, part] * scale).astype(BF16), v_ref[0, part], NN)
            mixed[0] = jnp.where(seg_col[...] == CAP, out, mixed[0].astype(F32)).astype(BF16)

    @pl.when(plan[0] == 0)
    def _():
        first, count, live = plan[1 + t], plan[5 + t], plan[9 + t]
        seg = seg_col[...]

        def strip(i):
            return pl.ds(pl.multiple_of(lax.rem(first + i, CAP // MS) * MS, MS), MS)

        def scores(i, top):
            at = strip(i)
            s = dot(query, k_ref[0, at], NT)
            s = jnp.where(seg == seg_row[:, at], s, -1e30)
            probs[:, at] = s
            return jnp.maximum(top, jnp.max(s, axis=1, keepdims=True))

        top = lax.fori_loop(0, count, scores, jnp.full((QT, 1), -1e30, F32))

        def exps(i, total):
            at = strip(i)
            e = jnp.exp(probs[:, at] - top)
            probs[:, at] = e
            return total + jnp.sum(e, axis=1, keepdims=True)

        total = lax.fori_loop(0, count, exps, jnp.zeros((QT, 1), F32))
        scale = 1.0 / total

        def sums(i, out):
            at = strip(i)
            p = probs[:, at] * scale
            probs[:, at] = p
            return out + dot(p.astype(BF16), v_ref[0, at], NN)

        out = lax.fori_loop(0, count, sums, jnp.zeros((QT, HEAD), F32))
        mixed[0] = out.astype(BF16)
        dq_out[...] = jnp.zeros_like(dq_out)

        @pl.when(live == 1)
        def _():
            def deltas(i, delta):
                at = strip(i)
                pg = dot(grad, v_ref[0, at], NT)
                pgrad[:, at] = pg
                return delta + jnp.sum(probs[:, at] * pg, axis=1, keepdims=True)

            delta = lax.fori_loop(0, count, deltas, jnp.zeros((QT, 1), F32))

            def backs(i, carry):
                at = strip(i)
                p = probs[:, at]
                low = p.astype(BF16)
                ds = (p * (pgrad[:, at] - delta)).astype(BF16)
                dq_out[0] += dot(ds, k_ref[0, at], NN) * HEAD**-0.5
                dv_sum[:, at] += dot(grad, low, TN)
                dk_sum[:, at] += dot(query, ds, TN)
                return carry

            lax.fori_loop(0, count, backs, 0)

    @pl.when(t == CAP // QT - 1)
    def _():
        dv_out[0] = dv_sum[...].T.astype(BF16)
        dk_out[0] = dk_sum[...].T


def attend(plan, q, k, v, g, seg_row, seg_col):
    chunk = pl.BlockSpec((1, CH, HEAD), lambda h, t: (h, 0, 0))
    out = pl.BlockSpec((1, QT, HEAD), lambda h, t: (h, t, 0))
    full = pl.BlockSpec((1, CAP, HEAD), lambda h, t: (h, 0, 0))
    flat = lambda kind: pltpu.HBM((HL, CAP, HEAD), kind)
    return pl.pallas_call(
        attend_kernel,
        grid=(HL, CAP // QT),
        in_specs=[pl.BlockSpec(memory_space=pltpu.SMEM)]
        + [chunk] * (4 * BR)
        + [
            pl.BlockSpec((1, CAP), lambda h, t: (0, 0)),
            pl.BlockSpec((QT, 1), lambda h, t: (t, 0)),
        ],
        out_specs=[out, out, full, full],
        out_shape=[flat(BF16), flat(F32), flat(F32), flat(BF16)],
        scratch_shapes=[
            pltpu.VMEM((QT, CAP), F32),
            pltpu.VMEM((QT, CAP), F32),
            pltpu.VMEM((HEAD, CAP), F32),
            pltpu.VMEM((HEAD, CAP), F32),
            pltpu.VMEM((1, QT, HEAD), BF16),
            pltpu.VMEM((1, CAP, HEAD), BF16),
            pltpu.VMEM((1, CAP, HEAD), BF16),
            pltpu.VMEM((1, QT, HEAD), BF16),
        ],
        compiler_params=params(24),
        cost_estimate=cost(48),
        name="attend",
    )(plan, *far_from([*q, *k, *v, *g]), seg_row, seg_col)


def early_kernel(*refs):
    normed, pre, ups, act = (refs[i * BR : (i + 1) * BR] for i in range(4))
    out, normed_out, ups_out, total, bias = refs[4 * BR :]
    t = pl.program_id(0)

    @pl.when(t == 0)
    def _():
        total[...] = jnp.zeros_like(total)
        bias[...] = jnp.zeros_like(bias)

    def joined(parts):
        return jnp.concatenate([part[...] for part in parts], axis=0)

    for k in range(BR):
        normed_out[k] = normed[k][...]
        ups_out[k] = ups[k][...]
        bias[...] += row_sum8(pre[k][...].astype(F32))
    lane = lax.broadcasted_iota(jnp.int32, (CH, 128), 1)
    first = jnp.where(lane == 0, 1.0, 0.0).astype(BF16)
    total[:, :HID] += dot(joined(normed), joined(pre), TN)
    right = jnp.concatenate([joined(act), first], axis=1)
    total[:, HID:] += dot(joined(ups), right, TN)

    @pl.when(t == BR - 1)
    def _():
        out[:, : 2 * HID] = total[:, : 2 * HID].astype(BF16)
        column = jnp.sum(bias[...].T, axis=1, keepdims=True)
        lane = lax.broadcasted_iota(jnp.int32, (D, 128), 1)
        out[:, 2 * HID :] = jnp.where(lane == 1, column, total[:, 2 * HID :]).astype(BF16)


def early_weights(normed, pre, ups, act):
    tile = pl.BlockSpec((CH // BR, D), lambda t: (t, 0))
    joined = pl.BlockSpec((BR, CH // BR, D), lambda t: (0, t, 0))
    return pl.pallas_call(
        early_kernel,
        grid=(BR,),
        in_specs=[tile] * (4 * BR),
        out_specs=[pl.BlockSpec((D, EARLY), lambda t: (0, 0)), joined, joined],
        out_shape=[pltpu.HBM((D, EARLY), BF16)]
        + [pltpu.HBM((BR, CH, D), BF16)] * 2,
        scratch_shapes=[pltpu.VMEM((D, EARLY), F32), pltpu.VMEM((8, HID), F32)],
        compiler_params=params(26),
        cost_estimate=cost(6),
        name="early_weights",
    )(*normed, *pre, *ups, *act)


def late_kernel(*refs):
    normed, ups, qk_gain = refs[:3]
    hats, inverses, pieces = refs[3 : 3 + BR], refs[3 + BR : 3 + 2 * BR], refs[3 + 2 * BR : -5]
    out, grads_out, mixed_out, gains, total = refs[-5:]
    t = pl.program_id(0)

    @pl.when(t == 0)
    def _():
        total[...] = jnp.zeros_like(total)
        gains[...] = jnp.zeros_like(gains)

    matrix = heads_of(QK)
    dq, dk, dv, mixed = pieces
    pair = jnp.concatenate([r[h] for r in (dq, dk) for h in range(HL)], axis=1)

    def back(hat, inverse):
        gains[...] += row_sum8(pair * hat)
        scaled = pair * qk_gain[...]
        mean = dot(scaled.astype(BF16), matrix, NN)
        slope = dot((scaled * hat).astype(BF16), matrix, NN)
        raw = inverse * (scaled - mean - hat * slope)
        grads_out[:, :QK] = raw.astype(BF16)

    for k in range(BR):

        @pl.when(t == k)
        def _():
            back(hats[k][...], inverses[k][...])

    grads_out[:, QK:] = jnp.concatenate([dv[h] for h in range(HL)], axis=1)
    mixed = jnp.concatenate([mixed[h] for h in range(HL)], axis=1)
    mixed_out[...] = mixed
    total[:, :QKV] += dot(normed[0], grads_out[...], TN)
    total[:, QKV:] += dot(ups[0], mixed, TN)

    @pl.when(t == BR - 1)
    def _():
        out[...] = total[...].astype(BF16)


def late_weights(normed, ups, qk_gain, hats, inverses, pieces):
    tile = lambda width: pl.BlockSpec((CH, width), lambda t: (t, 0))
    whole = lambda shape: pl.BlockSpec(shape, lambda t: (0,) * len(shape))
    return pl.pallas_call(
        late_kernel,
        grid=(BR,),
        in_specs=[pl.BlockSpec((1, CH, D), lambda t: (t, 0, 0))] * 2
        + [whole((1, QK))]
        + [whole((CH, QK))] * (2 * BR)
        + [pl.BlockSpec((HL, CH, HEAD), lambda t: (0, t, 0))] * 4,
        out_specs=[whole((D, D)), tile(QKV), tile(HL * HEAD), whole((8, QK))],
        out_shape=[
            pltpu.HBM((D, D), BF16),
            jax.ShapeDtypeStruct((CAP, QKV), BF16),
            pltpu.HBM((CAP, HL * HEAD), BF16),
            jax.ShapeDtypeStruct((8, QK), F32),
        ],
        scratch_shapes=[pltpu.VMEM((D, D), F32)],
        compiler_params=params(32),
        cost_estimate=cost(8),
        name="late_weights",
    )(*far_from((normed, ups)), qk_gain, *far_from(hats), *far_from(inverses), *far_from(pieces))


def close_kernel(weight, rows, back, grads, out, gains):
    total = back[...] + dot(grads[...], weight[:, :QKV], NT)
    out[...] = total.astype(out.dtype)
    hat, _ = norm_parts(rows[...].astype(F32))

    @pl.when(pl.program_id(0) == 0)
    def _():
        gains[...] = jnp.zeros_like(gains)

    gains[...] += row_sum8(total * hat)


def close(chunk, weight, rows, back, grads):
    tile = pl.BlockSpec((TILE, D), lambda t: (t, 0))
    whole = lambda shape: pl.BlockSpec(shape, lambda t: (0,) * len(shape))
    return pl.pallas_call(
        close_kernel,
        grid=(PER,),
        in_specs=[
            pl.BlockSpec((D, D), lambda t: (0, 2)),
            tile,
            tile,
            pl.BlockSpec((TILE, QKV), lambda t: (chunk * PER + t, 0)),
        ],
        out_specs=[tile, whole((8, D))],
        out_shape=[
            pltpu.HBM((CH, D), F32 if chunk == 0 else BF16),
            jax.ShapeDtypeStruct((8, D), F32),
        ],
        compiler_params=params(12),
        cost_estimate=cost(3),
        name="close",
    )(weight, rows, back, grads)


def output_kernel(rows, own, part1, part2, part3, bias, *refs):
    out = refs[-1]
    total = rows[...].astype(F32) + own[...] + bias[...]
    for part in (part1, part2, part3):
        total = total + part[...].astype(F32)
    own_mixed, own_weight = refs[0], refs[BR]
    total = total + dot(own_mixed[...], own_weight[:, QKV:], NT)
    for mixed, weight in zip(refs[1:BR], refs[BR + 1 : 2 * BR]):
        total = total + dot(mixed[...], weight[CH : CH + HL * HEAD, :], NN)
    out[...] = total.astype(BF16)


def output_rows(rows, own, parts, bias, mixed, weights):
    tile = lambda width: pl.BlockSpec((TILE, width), lambda t: (t, 0))
    whole = lambda shape: pl.BlockSpec(shape, lambda t: (0,) * len(shape))
    return pl.pallas_call(
        output_kernel,
        grid=(PER,),
        in_specs=[tile(D)] * 5
        + [whole((1, D))]
        + [tile(HL * HEAD)] * BR
        + [pl.BlockSpec((D, D), lambda t: (0, 2))]
        + [whole((MSG, D))] * (BR - 1),
        out_specs=tile(D),
        out_shape=jax.ShapeDtypeStruct((CH, D), BF16),
        compiler_params=params(16),
        cost_estimate=cost(4),
        name="output_rows",
    )(rows, *far_from([own, *parts]), bias, *far_from(mixed), weights, *far_from(parts))


def input_kernel(live, rows, cot, own, part1, part2, part3, gain, out):
    total = own[...]
    for part in (part1, part2, part3):
        total = total + part[...].astype(F32)
    hat, inverse = norm_parts(rows[...].astype(F32))
    place = lax.broadcasted_iota(jnp.int32, (TILE, 1), 0) + pl.program_id(0) * TILE
    ups = jnp.where(place < live[0], cot[...].astype(F32), 0.0)
    out[...] = (ups + norm_back(total * gain[...], hat, inverse)).astype(BF16)


def input_rows(live, rows, cot, own, parts, gain):
    tile = pl.BlockSpec((TILE, D), lambda t: (t, 0))
    return pl.pallas_call(
        input_kernel,
        grid=(PER,),
        in_specs=[pl.BlockSpec(memory_space=pltpu.SMEM)]
        + [tile] * 6
        + [pl.BlockSpec((1, D), lambda t: (0, 0))],
        out_specs=tile,
        out_shape=jax.ShapeDtypeStruct((CH, D), BF16),
        compiler_params=params(12),
        cost_estimate=cost(4),
        name="input_rows",
    )(live, *far_from([rows, cot, own, *parts]), gain)


def dp_pairs(step):
    pairs = []
    for y in range(4):
        for z in range(4):
            for c in range(2):
                y2, z2, c2 = step(y, z, c)
                pairs.append(((y * 4 + z) * 2 + c, ((y2 % 4) * 4 + z2 % 4) * 2 + c2))
    return pairs


def move_x(value, k):
    return lax.ppermute(value, "branch", [(i, (i + k) % BR) for i in range(BR)])


def move_y(value, k):
    return lax.ppermute(value, "dp", dp_pairs(lambda y, z, c: (y + k, z, c)))


def move_z(value, k):
    return lax.ppermute(value, "dp", dp_pairs(lambda y, z, c: (y, z + k, c)))


def move_core(value):
    return lax.ppermute(value, "dp", dp_pairs(lambda y, z, c: (y, z, 1 - c)))


def put(buffer, value, index, axis):
    return lax.dynamic_update_index_in_dim(buffer, value, index, axis)


def take(buffer, index, axis):
    return lax.dynamic_index_in_dim(buffer, index, axis, keepdims=False)


def gather_plane(own, y, z):
    line = jnp.zeros((4, *own.shape), own.dtype)
    line = put(line, own, z, 0)
    for k in (1, 3, 2):
        line = put(line, move_z(own, -k), (z + k) % 4, 0)
    plane = jnp.zeros((4, *line.shape), own.dtype)
    plane = put(plane, line, y, 0)
    came = [move_y(line, -k) for k in (1, 3, 2)]
    for k, part in zip((1, 3, 2), came):
        plane = put(plane, part, (y + k) % 4, 0)
    return plane, came[0]


def gather_cores(plane, other, c):
    whole = jnp.zeros((4, 4, 2, *plane.shape[2:]), plane.dtype)
    whole = put(whole, plane, c, 2)
    whole = put(whole, other, 1 - c, 2)
    return whole.reshape(32 * plane.shape[2], plane.shape[3])


def after(values, *earlier):
    return lax.optimization_barrier((values, earlier))[0]


def gather_rows(own):
    near = [move_x(own, -k) for k in (1, 3)]
    return [own, near[0], move_x(own, -2), near[1]]


def scatter_sum(grad):
    parts = lax.all_to_all(grad.reshape(32, D // 32, -1), "dp", 0, 0, tiled=True)
    return jnp.sum(parts.astype(F32), axis=0)


def adam_update(weight, first_moment, second_moment, gradient, factor, rate, decay):
    clipped = gradient * factor
    first_new = BETA_ONE * first_moment + (1.0 - BETA_ONE) * clipped
    second_new = BETA_TWO * second_moment + (1.0 - BETA_TWO) * clipped * clipped
    ratio = (
        first_new
        / (1.0 - BETA_ONE**STEP)
        / (jnp.sqrt(second_new / (1.0 - BETA_TWO**STEP)) + EPS_ADAM)
    )
    return (clipped, second_new, weight - rate * (ratio + decay * weight))


def body(
    block_input,
    cotangent,
    image_owner,
    image_length,
    image_start,
    qkv_weight,
    qkv_first,
    qkv_second,
    out_weight,
    out_first,
    out_second,
    up_weight,
    up_first,
    up_second,
    down_weight,
    down_first,
    down_second,
    small_weight,
    small_first,
    small_second,
):
    b = lax.axis_index("branch")
    g = lax.axis_index("dp")
    y, z, c = g // 8, (g // 2) % 4, g % 2
    depth = up_weight.shape[0]

    own = pack(up_weight, down_weight.T, qkv_weight, out_weight.T)
    plane, came = gather_plane(own, y, z)

    rows = gather_rows(block_input)
    other = move_core(after(plane, rows[1:]))
    weights = gather_cores(plane, other, c)
    cots = gather_rows(after(cotangent, rows[2]))

    plan, live, seg_row, seg_col, ln_gain, qk_gain, out_bias, hidden_bias = make_plan(
        after(small_weight, came).reshape(-1, 128), image_owner[None], image_length[None]
    )

    normed, q, key, v, hats, inverses = ([None] * BR for _ in range(6))
    for k in (0, 1, 3, 2):
        normed[k], q[k], key[k], v[k], hats[k], inverses[k] = project(
            rows[k], weights, ln_gain, qk_gain
        )

    ffn, back, act, pre, ups, mixed_grad = ([None] * BR for _ in range(6))
    for k in (0, 1, 3, 2):
        ffn[k], back[k], act[k], pre[k], ups[k], mixed_grad[k] = mlp(
            live[k][None], cots[k], normed[k], weights, hidden_bias, *((MSG, BF16) if k else (CH, F32))
        )

    ffn_parts = [move_x(ffn[k], k) for k in (1, 2, 3)]
    early_grad, normed, ups = early_weights(normed, pre, ups, act)
    mixed, dq, dk, dv = attend(plan, q, key, v, after(mixed_grad, early_grad), seg_row, seg_col)
    early = scatter_sum(early_grad)

    late_grad, qkv_grads, mixed, gains_part = late_weights(
        normed, ups, qk_gain, hats, inverses, (after(dq, early, ffn_parts), dk, dv, mixed)
    )
    late = scatter_sum(late_grad)
    gains_part = jnp.sum(gains_part, axis=0).reshape(2, HL, HEAD)
    qk_gain_part = jnp.sum(gains_part, axis=1).reshape(2 * HEAD)

    mixed = [mixed[:CH]] + [move_x(mixed[k * CH : (k + 1) * CH], k) for k in (1, 2, 3)]
    grads, gain_parts = [None] * BR, [None] * BR
    for k in (2, 1, 3, 0):
        grads[k], gain_parts[k] = close(k, weights, rows[k], back[k], qkv_grads)
    parts = [move_x(grads[2], 2)]
    parts += [move_x(after(grads[k], mixed[1:]), k) for k in (1, 3)]
    block_output = output_rows(block_input, ffn[0], ffn_parts, out_bias, mixed, weights)
    input_grad = input_rows(live[:1], block_input, cotangent, grads[0], parts, ln_gain)

    qkv_share = late[:, :QKV]
    out_share = late[:, QKV:]
    up_share = early[:, :HID]
    down_share = early[:, HID : 2 * HID]
    squares = (
        jnp.sum(qkv_share * qkv_share)
        + jnp.sum(out_share * out_share)
        + jnp.sum(up_share * up_share)
        + jnp.sum(down_share * down_share)
    )
    told = jnp.concatenate(
        [
            jnp.sum(sum(gain_parts), axis=0),
            qk_gain_part,
            early[:, 2 * HID],
            early[:, 2 * HID + 1],
            squares[None],
            jnp.zeros((1024 - D - 2 * HEAD - 2 * depth - 1,), F32),
        ]
    )
    told = jnp.broadcast_to(told[None, None], (128, 1, 1024))
    heard = lax.all_to_all(told, ("dp", "branch"), 0, 0, tiled=True).reshape(32, BR, 1024)
    base = D + 2 * HEAD
    gains_grad = jnp.sum(heard[:, :, :base], axis=(0, 1))
    out_bias_grad = heard[:, 0, base : base + depth].reshape(D)
    hidden_bias_grad = heard[:, :, base + depth : base + 2 * depth]
    hidden_bias_grad = hidden_bias_grad.transpose(1, 0, 2).reshape(FF)
    small_grad = jnp.concatenate([gains_grad, out_bias_grad, hidden_bias_grad])
    squares_total = jnp.sum(heard[:, :, base + 2 * depth])
    grad_norm = jnp.sqrt(squares_total + jnp.sum(small_grad * small_grad))
    factor = 1.0 / jnp.maximum(grad_norm, 1.0)

    matrix = functools.partial(adam_update, factor=factor, rate=RATE_MATRIX, decay=DECAY_MATRIX)
    qkv_new = matrix(
        qkv_weight,
        qkv_first,
        qkv_second,
        qkv_share.reshape(depth, 3, HL * HEAD).transpose(1, 0, 2),
    )
    out_new = matrix(out_weight, out_first, out_second, out_share.T)
    up_new = matrix(up_weight, up_first, up_second, up_share)
    down_new = matrix(down_weight, down_first, down_second, down_share.T)
    small_new = adam_update(
        small_weight, small_first, small_second, small_grad, factor, RATE_SMALL, 0.0
    )
    return (
        block_output,
        input_grad,
        grad_norm,
        *qkv_new,
        *out_new,
        *up_new,
        *down_new,
        *small_new,
    )


def solution(mesh):
    rows = P(("dp", "branch"), None)
    qkv = [P(None, "dp", "branch")] * 3
    out = [P("branch", "dp")] * 3
    up = [P("dp", "branch")] * 3
    small = [P()] * 3
    return jax.shard_map(
        body,
        mesh=mesh,
        in_specs=(rows, rows, P(), P(), P(), *qkv, *out, *up, *out, *small),
        out_specs=(rows, rows, P(), *qkv, *out, *up, *out, *small),
        check_vma=False,
    )
```

```python
import functools

import jax
import jax.numpy as jnp
from jax import lax
from jax.experimental import pallas as pl
from jax.experimental.pallas import tpu as pltpu
from jax.sharding import PartitionSpec as P

D = 768
HEADS = 12
HEAD = 64
FF = 3072
CAP = 2048
SMALL_LEN = 196
STEP = 10

EPS_NORM = 1e-06
BETA_ONE = 0.9
BETA_TWO = 0.95
EPS_ADAM = 1e-08
RATE_MATRIX = 0.1
RATE_SMALL = 1.0
DECAY_MATRIX = 0.1

F32 = jnp.float32
BF16 = jnp.bfloat16
NN = (((1,), (0,)), ((), ()))
NT = (((1,), (1,)), ((), ()))
TN = (((0,), (0,)), ((), ()))

BR = 4
HL = HEADS // BR
HID = FF // BR
QK = 2 * HL * HEAD
QKV = 3 * HL * HEAD
EARLY = 2 * HID + 128
BASE = D + 2 * HEAD
TOLD = 1024
CH = CAP // BR
MSG = CH + HL * HEAD
TILE = 256
PER = CH // TILE
QT = 512
KS = 512
MS = 256
SAFE = 60.0


def dot(left, right, dims):
    return lax.dot_general(left, right, dims, preferred_element_type=F32)


def cost(us):
    return pl.CostEstimate(flops=int(us * 1.1e9), bytes_accessed=0, transcendentals=0)


def params(mib):
    return pltpu.CompilerParams(vmem_limit_bytes=mib * 2**20)


def far_from(arrays):
    return [pltpu.with_memory_space_constraint(value, pltpu.HBM) for value in arrays]


def norm_parts(values):
    average = jnp.mean(values, axis=-1, keepdims=True)
    centered = values - average
    inverse = lax.rsqrt(jnp.mean(centered * centered, axis=-1, keepdims=True) + EPS_NORM)
    return (centered * inverse, inverse)


def norm_back(grad, hat, inverse):
    return inverse * (
        grad
        - jnp.mean(grad, axis=-1, keepdims=True)
        - hat * jnp.mean(grad * hat, axis=-1, keepdims=True)
    )


def lane_sum(values):
    width = values.shape[1] // 128
    total = values[:, :128]
    for i in range(1, width):
        total = total + values[:, i * 128 : (i + 1) * 128]
    return total


def row_sum8(values):
    return jnp.sum(values.reshape(values.shape[0] // 8, 8, values.shape[1]), axis=0)


def head_means(values, heads_matrix):
    high = values.astype(BF16)
    rest = (values - high.astype(F32)).astype(BF16)
    return dot(high, heads_matrix, NN) + dot(rest, heads_matrix, NN)


def heads_of(width):
    row = lax.broadcasted_iota(jnp.int32, (width, width), 0) >> 6
    column = lax.broadcasted_iota(jnp.int32, (width, width), 1) >> 6
    return jnp.where(row == column, 1.0 / HEAD, 0.0).astype(BF16)


def head_norm(pair, heads_matrix):
    centered = pair - head_means(pair, heads_matrix)
    inverse = lax.rsqrt(head_means(centered * centered, heads_matrix) + EPS_NORM)
    return (centered * inverse, inverse)


def pack_kernel(up, down_t, qkv, out_t, packed):
    packed[:, :HID] = up[...].astype(BF16)
    packed[:, HID : 2 * HID] = down_t[...].astype(BF16)
    parts = [qkv[j] for j in range(3)] + [out_t[...]]
    packed[:, 2 * HID :] = jnp.concatenate(parts, axis=1).astype(BF16)


def pack(up, down_t, qkv, out_t):
    return pl.pallas_call(
        pack_kernel,
        out_shape=jax.ShapeDtypeStruct((D // 32, 2 * HID + D), BF16),
        cost_estimate=cost(1),
        name="pack",
    )(up, down_t, qkv, out_t)


def plan_kernel(
    small, owner, length,
    plan, live, seg_row, seg_col, ln_gain, qk_gain, out_bias, hidden_bias,
):
    group, branch = lax.axis_index("dp"), lax.axis_index("branch")
    gains = D // 128
    for i in range(gains):
        lane = slice(i * 128, (i + 1) * 128)
        ln_gain[:, lane] = small[i : i + 1, :]
        out_bias[:, lane] = small[gains + 1 + i : gains + 2 + i, :]
        hidden_bias[:, lane] = small[pl.ds(2 * gains + 1 + branch * (HID // 128) + i, 1), :]
    both = small[gains : gains + 1, :]
    q_gain, k_gain = both[:, :HEAD], both[:, HEAD:]
    qk_gain[...] = jnp.concatenate([q_gain] * HL + [k_gain] * HL, axis=1)
    bound = 8.0 * 1.02 * jnp.max(jnp.abs(q_gain)) * jnp.max(jnp.abs(k_gain))

    size = jnp.where(owner[...] == group, length[...], 0)
    tokens = jnp.sum(size)
    big = jnp.where(jnp.max(size) == CAP, 1, 0)

    def label(shape, axis):
        place = lax.broadcasted_iota(jnp.int32, shape, axis) + CH * branch
        place = jnp.where(place >= CAP, place - CAP, place)
        image = jnp.where(big == 1, 0, (place * 2675) >> 19)
        return jnp.where(place < tokens, image, CAP)

    seg_row[...] = label((1, CAP), 1)
    seg_col[...] = label((CAP, 1), 0)
    plan[0] = jnp.where(bound <= SAFE, 1 + big, 0)
    for t in range(CAP // QT):
        start = lax.rem(t * QT + CH * branch, CAP)
        last = start + QT - 1
        begin = jnp.where(start < tokens, ((start * 2675) >> 19) * SMALL_LEN, tokens)
        end = jnp.minimum((((last * 2675) >> 19) + 1) * SMALL_LEN, tokens)
        end = jnp.where(last >= tokens, CAP, end)
        begin = jnp.where(big == 1, 0, begin)
        end = jnp.where(big == 1, CAP, end)
        strip = begin // MS
        plan[1 + t] = lax.rem(strip + CAP // MS - (CH // MS) * branch, CAP // MS)
        plan[5 + t] = (end + MS - 1) // MS - strip
        plan[9 + t] = jnp.where(start < tokens, 1, 0)
        plan[21 + t] = jnp.where(last >= tokens, 1, 0)
    for t in range(CAP // MS):
        start = lax.rem(t * MS + CH * branch, CAP)
        plan[13 + t] = jnp.where(start < tokens, 1, 0)
    for k in range(BR):
        start = lax.rem((branch + k) * CH, CAP)
        live[k] = jnp.clip(tokens - start, 0, CH)


def make_plan(small, owner, length):
    smem = pl.BlockSpec(memory_space=pltpu.SMEM)
    vmem = pl.BlockSpec(memory_space=pltpu.VMEM)
    row = lambda width, kind=F32: jax.ShapeDtypeStruct((1, width), kind)
    return pl.pallas_call(
        plan_kernel,
        in_specs=[vmem] * 3,
        out_specs=[smem, smem] + [vmem] * 6,
        out_shape=[
            jax.ShapeDtypeStruct((25,), jnp.int32),
            jax.ShapeDtypeStruct((BR,), jnp.int32),
            row(CAP, jnp.int32),
            jax.ShapeDtypeStruct((CAP, 1), jnp.int32),
            row(D),
            row(QK),
            row(D),
            row(HID),
        ],
        cost_estimate=cost(3),
        name="make_plan",
    )(small, owner, length)


def tiles_of(chunk):
    if isinstance(chunk, tuple):
        return list(chunk), [pl.BlockSpec((TILE, D), lambda t: (0, 0))] * 2
    specs = [pl.BlockSpec((TILE, D), lambda t, i=i: (i, 0)) for i in range(PER)]
    return [chunk] * PER, specs


def tile_now(first, second):
    return jnp.where(pl.program_id(0) == 0, first[...], second[...]).astype(F32)


def project_kernel(
    rows_0, rows_1, weight, gain, qk_gain, normed, q_out, k_out, v_out, qk_hat, qk_inverse
):
    hat, _ = norm_parts(tile_now(rows_0, rows_1))
    low = (hat * gain[...]).astype(BF16)
    normed[...] = low
    raw = dot(low, weight[:, :QKV], NN)
    hat, inverse = head_norm(raw[:, :QK], heads_of(QK))
    qk_hat[...] = hat
    qk_inverse[...] = inverse
    value = (hat * qk_gain[...]).astype(BF16)
    vals = raw[:, QK:].astype(BF16)
    for h in range(HL):
        lane = slice(h * HEAD, (h + 1) * HEAD)
        q_out[h] = value[:, lane] * jnp.asarray(HEAD**-0.5, BF16)
        k_out[h] = value[:, QK // 2 + h * HEAD : QK // 2 + (h + 1) * HEAD]
        v_out[h] = vals[:, lane]


def project(rows, weights, gain, qk_gain):
    whole = lambda shape: pl.BlockSpec(shape, lambda t: (0,) * len(shape))
    heads = pl.BlockSpec((HL, TILE, HEAD), lambda t: (0, t, 0))
    tile = pl.BlockSpec((TILE, D), lambda t: (t, 0))
    rows, rows_specs = tiles_of(rows)
    return pl.pallas_call(
        project_kernel,
        grid=(PER,),
        in_specs=rows_specs
        + [
            pl.BlockSpec((D, D), lambda t: (0, 2)),
            whole((1, D)),
            whole((1, QK)),
        ],
        out_specs=[tile, heads, heads, heads] + [pl.BlockSpec((TILE, QK), lambda t: (t, 0))] * 2,
        out_shape=[jax.ShapeDtypeStruct((CH, D), BF16)]
        + [pltpu.HBM((HL, CH, HEAD), BF16)] * 3
        + [pltpu.HBM((CH, QK), F32)] * 2,
        compiler_params=params(16),
        cost_estimate=cost(3),
        name="project",
    )(*rows, weights, gain, qk_gain)


def mlp_kernel(
    live, cot_0, cot_1, normed, up, down_t, proj, bias,
    ffn, back, act_out, pre_out, ups_out, mix_out,
):
    t = pl.program_id(0)
    pre = dot(normed[...], up[...], NN) + bias[...]
    half = 0.5 * (1.0 + lax.erf(pre * (2.0**-0.5)))
    act = (pre * half).astype(BF16)
    slope = half + pre * (jnp.exp(-0.5 * pre * pre) * 0.3989422804014327)
    act_out[...] = act
    ffn[pl.ds(t * TILE, TILE), :] = dot(act, down_t[...], NT).astype(ffn.dtype)
    place = lax.broadcasted_iota(jnp.int32, (TILE, 1), 0) + t * TILE
    ups = jnp.where(place < live[0], tile_now(cot_0, cot_1), 0.0).astype(BF16)
    ups_out[...] = ups
    grad = (dot(ups, down_t[...], NN) * slope).astype(BF16)
    pre_out[...] = grad
    back[...] = dot(grad, up[...], NT)
    mixed = dot(ups, proj[:, QKV:], NN).astype(BF16)
    if ffn.shape[0] > CH:

        @pl.when(t == 0)
        def _():
            ffn[CH:, :] = proj[:, QKV:].astype(F32).T.astype(BF16)

    for h in range(HL):
        mix_out[h] = mixed[:, h * HEAD : (h + 1) * HEAD]


def mlp(live, cot, normed, weights, bias, height, kind):
    whole = lambda shape: pl.BlockSpec(shape, lambda t: (0,) * len(shape))
    tile = pl.BlockSpec((TILE, D), lambda t: (t, 0))
    cot, cot_specs = tiles_of(cot)
    return pl.pallas_call(
        mlp_kernel,
        grid=(PER,),
        in_specs=[pl.BlockSpec(memory_space=pltpu.SMEM)]
        + cot_specs
        + [
            tile,
            pl.BlockSpec((D, HID), lambda t: (0, 0)),
            pl.BlockSpec((D, HID), lambda t: (0, 1)),
            pl.BlockSpec((D, D), lambda t: (0, 2)),
            whole((1, HID)),
        ],
        out_specs=[whole((height, D))]
        + [tile] * 4
        + [pl.BlockSpec((HL, TILE, HEAD), lambda t: (0, t, 0))],
        out_shape=[pltpu.HBM((height, D), kind), pltpu.HBM((CH, D), F32)]
        + [jax.ShapeDtypeStruct((CH, D), BF16)] * 3
        + [pltpu.HBM((HL, CH, HEAD), BF16)],
        compiler_params=params(20),
        cost_estimate=cost(6),
        name="mlp",
    )(live, *cot, normed, weights, weights, weights, bias)


def attend_kernel(plan, *refs):
    q_refs, k_refs, v_refs, g_refs = (refs[i * BR : (i + 1) * BR] for i in range(4))
    seg_row, seg_col, mixed, dq_out, dk_out, dv_out = refs[4 * BR : 4 * BR + 6]
    probs, pgrad, dk_sum, dv_sum, q_ref, k_ref, v_ref, g_ref = refs[4 * BR + 6 :]
    t = pl.program_id(1)
    for k in range(BR):

        @pl.when(t == k)
        def _():
            q_ref[...] = q_refs[k][...]
            g_ref[...] = g_refs[k][...]

    @pl.when(t == 0)
    def _():
        dk_sum[...] = jnp.zeros_like(dk_sum)
        dv_sum[...] = jnp.zeros_like(dv_sum)
        for k in range(BR):
            k_ref[:, k * CH : (k + 1) * CH] = k_refs[k][...]
            v_ref[:, k * CH : (k + 1) * CH] = v_refs[k][...]

    query = q_ref[0]
    grad = g_ref[0]

    @pl.when(plan[0] == 2)
    def _():
        total = jnp.zeros((QT, 128), F32)
        weighted = jnp.zeros((QT, 128), F32)
        for j in range(CAP // KS):
            part = slice(j * KS, (j + 1) * KS)
            e = jnp.exp(dot(query, k_ref[0, part], NT))
            probs[:, part] = e
            pg = dot(grad, v_ref[0, part], NT)
            pgrad[:, part] = pg
            total = total + lane_sum(e)
            weighted = weighted + lane_sum(e * pg)
        scale = 1.0 / jnp.sum(total, axis=1, keepdims=True)
        delta = jnp.sum(weighted, axis=1, keepdims=True) * scale
        out = jnp.zeros((QT, HEAD), F32)
        dq = jnp.zeros((QT, HEAD), F32)
        for j in range(CAP // KS):
            part = slice(j * KS, (j + 1) * KS)
            p = probs[:, part] * scale
            low = p.astype(BF16)
            ds = (p * (pgrad[:, part] - delta)).astype(BF16)
            out = out + dot(low, v_ref[0, part], NN)
            dq = dq + dot(ds, k_ref[0, part], NN)
            dv_sum[:, part] += dot(grad, low, TN)
            dk_sum[:, part] += dot(query, ds, TN)
        mixed[0] = out.astype(BF16)
        dq_out[0] = dq * HEAD**-0.5

    @pl.when(plan[0] == 1)
    def _():
        mixed[...] = jnp.zeros_like(mixed)
        dq_out[...] = jnp.zeros_like(dq_out)
        for s in range(QT // MS):
            index = t * (QT // MS) + s
            at = slice(s * MS, (s + 1) * MS)

            @pl.when(plan[13 + index] == 1)
            def _():
                qs, gs, seg = query[at], grad[at], seg_col[at, :]
                strips, es, pgs = [], [], []
                for j in range(3):
                    near = lax.rem(index + (CAP // MS - 1) + j, CAP // MS)
                    strip = pl.ds(pl.multiple_of(near * MS, MS), MS)
                    score = dot(qs, k_ref[0, strip], NT)
                    strips.append(strip)
                    es.append(jnp.where(seg == seg_row[:, strip], jnp.exp(score), 0.0))
                    pgs.append(dot(gs, v_ref[0, strip], NT))
                total = sum(lane_sum(e) for e in es)
                weighted = sum(lane_sum(e * pg) for e, pg in zip(es, pgs))
                scale = 1.0 / jnp.sum(total, axis=1, keepdims=True)
                delta = jnp.sum(weighted, axis=1, keepdims=True) * scale
                out = jnp.zeros((MS, HEAD), F32)
                dq = jnp.zeros((MS, HEAD), F32)
                for strip, e, pg in zip(strips, es, pgs):
                    p = e * scale
                    low = p.astype(BF16)
                    ds = (p * (pg - delta)).astype(BF16)
                    out = out + dot(low, v_ref[0, strip], NN)
                    dq = dq + dot(ds, k_ref[0, strip], NN)
                    dv_sum[:, strip] += dot(gs, low, TN)
                    dk_sum[:, strip] += dot(qs, ds, TN)
                mixed[0, at, :] = out.astype(BF16)
                dq_out[0, at, :] = dq * HEAD**-0.5

        @pl.when(plan[21 + t] == 1)
        def _():
            total = jnp.zeros((QT, 128), F32)
            for j in range(CAP // KS):
                part = slice(j * KS, (j + 1) * KS)
                e = jnp.exp(dot(query, k_ref[0, part], NT))
                e = jnp.where(seg_row[:, part] == CAP, e, 0.0)
                probs[:, part] = e
                total = total + lane_sum(e)
            scale = 1.0 / jnp.sum(total, axis=1, keepdims=True)
            out = jnp.zeros((QT, HEAD), F32)
            for j in range(CAP // KS):
                part = slice(j * KS, (j + 1) * KS)
                out = out + dot((probs[:, part] * scale).astype(BF16), v_ref[0, part], NN)
            mixed[0] = jnp.where(seg_col[...] == CAP, out, mixed[0].astype(F32)).astype(BF16)

    @pl.when(plan[0] == 0)
    def _():
        first, count, live = plan[1 + t], plan[5 + t], plan[9 + t]
        seg = seg_col[...]

        def strip(i):
            return pl.ds(pl.multiple_of(lax.rem(first + i, CAP // MS) * MS, MS), MS)

        def scores(i, top):
            at = strip(i)
            s = dot(query, k_ref[0, at], NT)
            s = jnp.where(seg == seg_row[:, at], s, -1e30)
            probs[:, at] = s
            return jnp.maximum(top, jnp.max(s, axis=1, keepdims=True))

        top = lax.fori_loop(0, count, scores, jnp.full((QT, 1), -1e30, F32))

        def exps(i, total):
            at = strip(i)
            e = jnp.exp(probs[:, at] - top)
            probs[:, at] = e
            return total + jnp.sum(e, axis=1, keepdims=True)

        total = lax.fori_loop(0, count, exps, jnp.zeros((QT, 1), F32))
        scale = 1.0 / total

        def sums(i, out):
            at = strip(i)
            p = probs[:, at] * scale
            probs[:, at] = p
            return out + dot(p.astype(BF16), v_ref[0, at], NN)

        out = lax.fori_loop(0, count, sums, jnp.zeros((QT, HEAD), F32))
        mixed[0] = out.astype(BF16)
        dq_out[...] = jnp.zeros_like(dq_out)

        @pl.when(live == 1)
        def _():
            def deltas(i, delta):
                at = strip(i)
                pg = dot(grad, v_ref[0, at], NT)
                pgrad[:, at] = pg
                return delta + jnp.sum(probs[:, at] * pg, axis=1, keepdims=True)

            delta = lax.fori_loop(0, count, deltas, jnp.zeros((QT, 1), F32))

            def backs(i, carry):
                at = strip(i)
                p = probs[:, at]
                low = p.astype(BF16)
                ds = (p * (pgrad[:, at] - delta)).astype(BF16)
                dq_out[0] += dot(ds, k_ref[0, at], NN) * HEAD**-0.5
                dv_sum[:, at] += dot(grad, low, TN)
                dk_sum[:, at] += dot(query, ds, TN)
                return carry

            lax.fori_loop(0, count, backs, 0)

    @pl.when(t == CAP // QT - 1)
    def _():
        dv_out[0] = dv_sum[...].T.astype(BF16)
        dk_out[0] = dk_sum[...].T


def attend(plan, q, k, v, g, seg_row, seg_col):
    chunk = pl.BlockSpec((1, CH, HEAD), lambda h, t: (h, 0, 0))
    out = pl.BlockSpec((1, QT, HEAD), lambda h, t: (h, t, 0))
    full = pl.BlockSpec((1, CAP, HEAD), lambda h, t: (h, 0, 0))
    flat = lambda kind: pltpu.HBM((HL, CAP, HEAD), kind)
    return pl.pallas_call(
        attend_kernel,
        grid=(HL, CAP // QT),
        in_specs=[pl.BlockSpec(memory_space=pltpu.SMEM)]
        + [chunk] * (4 * BR)
        + [
            pl.BlockSpec((1, CAP), lambda h, t: (0, 0)),
            pl.BlockSpec((QT, 1), lambda h, t: (t, 0)),
        ],
        out_specs=[out, out, full, full],
        out_shape=[flat(BF16), flat(F32), flat(F32), flat(BF16)],
        scratch_shapes=[
            pltpu.VMEM((QT, CAP), F32),
            pltpu.VMEM((QT, CAP), F32),
            pltpu.VMEM((HEAD, CAP), F32),
            pltpu.VMEM((HEAD, CAP), F32),
            pltpu.VMEM((1, QT, HEAD), BF16),
            pltpu.VMEM((1, CAP, HEAD), BF16),
            pltpu.VMEM((1, CAP, HEAD), BF16),
            pltpu.VMEM((1, QT, HEAD), BF16),
        ],
        compiler_params=params(24),
        cost_estimate=cost(48),
        name="attend",
    )(plan, *far_from([*q, *k, *v, *g]), seg_row, seg_col)


def early_kernel(*refs):
    normed, pre, ups, act = (refs[i * BR : (i + 1) * BR] for i in range(4))
    out, normed_out, ups_out, total, bias = refs[4 * BR :]
    t = pl.program_id(0)

    @pl.when(t == 0)
    def _():
        total[...] = jnp.zeros_like(total)
        bias[...] = jnp.zeros_like(bias)

    def joined(parts):
        return jnp.concatenate([part[...] for part in parts], axis=0)

    for k in range(BR):
        normed_out[k] = normed[k][...]
        ups_out[k] = ups[k][...]
        bias[...] += row_sum8(pre[k][...].astype(F32))
    lane = lax.broadcasted_iota(jnp.int32, (CH, 128), 1)
    first = jnp.where(lane == 0, 1.0, 0.0).astype(BF16)
    total[:, :HID] += dot(joined(normed), joined(pre), TN)
    right = jnp.concatenate([joined(act), first], axis=1)
    total[:, HID:] += dot(joined(ups), right, TN)

    @pl.when(t == BR - 1)
    def _():
        out[:, : 2 * HID] = total[:, : 2 * HID].astype(BF16)
        column = jnp.sum(bias[...].T, axis=1, keepdims=True)
        lane = lax.broadcasted_iota(jnp.int32, (D, 128), 1)
        out[:, 2 * HID :] = jnp.where(lane == 1, column, total[:, 2 * HID :]).astype(BF16)


def early_weights(normed, pre, ups, act):
    tile = pl.BlockSpec((CH // BR, D), lambda t: (t, 0))
    joined = pl.BlockSpec((BR, CH // BR, D), lambda t: (0, t, 0))
    return pl.pallas_call(
        early_kernel,
        grid=(BR,),
        in_specs=[tile] * (4 * BR),
        out_specs=[pl.BlockSpec((D, EARLY), lambda t: (0, 0)), joined, joined],
        out_shape=[pltpu.HBM((D, EARLY), BF16)]
        + [pltpu.HBM((BR, CH, D), BF16)] * 2,
        scratch_shapes=[pltpu.VMEM((D, EARLY), F32), pltpu.VMEM((8, HID), F32)],
        compiler_params=params(26),
        cost_estimate=cost(6),
        name="early_weights",
    )(*normed, *pre, *ups, *act)


def late_kernel(*refs):
    normed, ups, qk_gain = refs[:3]
    hats, inverses, pieces = refs[3 : 3 + BR], refs[3 + BR : 3 + 2 * BR], refs[3 + 2 * BR : -5]
    out, grads_out, mixed_out, gains, total = refs[-5:]
    t = pl.program_id(0)

    @pl.when(t == 0)
    def _():
        total[...] = jnp.zeros_like(total)
        gains[...] = jnp.zeros_like(gains)

    matrix = heads_of(QK)
    dq, dk, dv, mixed = pieces
    pair = jnp.concatenate([r[h] for r in (dq, dk) for h in range(HL)], axis=1)

    def back(hat, inverse):
        gains[...] += row_sum8(pair * hat)
        scaled = pair * qk_gain[...]
        mean = dot(scaled.astype(BF16), matrix, NN)
        slope = dot((scaled * hat).astype(BF16), matrix, NN)
        raw = inverse * (scaled - mean - hat * slope)
        grads_out[:, :QK] = raw.astype(BF16)

    for k in range(BR):

        @pl.when(t == k)
        def _():
            back(hats[k][...], inverses[k][...])

    grads_out[:, QK:] = jnp.concatenate([dv[h] for h in range(HL)], axis=1)
    mixed = jnp.concatenate([mixed[h] for h in range(HL)], axis=1)
    mixed_out[...] = mixed
    total[:, :QKV] += dot(normed[0], grads_out[...], TN)
    total[:, QKV:] += dot(ups[0], mixed, TN)

    @pl.when(t == BR - 1)
    def _():
        out[...] = total[...].astype(BF16)


def late_weights(normed, ups, qk_gain, hats, inverses, pieces):
    tile = lambda width: pl.BlockSpec((CH, width), lambda t: (t, 0))
    whole = lambda shape: pl.BlockSpec(shape, lambda t: (0,) * len(shape))
    return pl.pallas_call(
        late_kernel,
        grid=(BR,),
        in_specs=[pl.BlockSpec((1, CH, D), lambda t: (t, 0, 0))] * 2
        + [whole((1, QK))]
        + [whole((CH, QK))] * (2 * BR)
        + [pl.BlockSpec((HL, CH, HEAD), lambda t: (0, t, 0))] * 4,
        out_specs=[whole((D, D)), tile(QKV), tile(HL * HEAD), whole((8, QK))],
        out_shape=[
            pltpu.HBM((D, D), BF16),
            pltpu.HBM((CAP, QKV), BF16),
            pltpu.HBM((CAP, HL * HEAD), BF16),
            jax.ShapeDtypeStruct((8, QK), F32),
        ],
        scratch_shapes=[pltpu.VMEM((D, D), F32)],
        compiler_params=params(32),
        cost_estimate=cost(8),
        name="late_weights",
    )(*far_from((normed, ups)), qk_gain, *far_from(hats), *far_from(inverses), *far_from(pieces))


def close_kernel(weight, rows_0, rows_1, back, grads, *refs):
    out, gains = refs[-2:]
    t = pl.program_id(0)
    total = back[...] + dot(grads[...], weight[:, :QKV], NT)
    out[pl.ds(t * TILE, TILE), :] = total.astype(out.dtype)
    hat, _ = norm_parts(tile_now(rows_0, rows_1))

    @pl.when(t == 0)
    def _():
        gains[...] = jnp.zeros_like(gains)
        if len(refs) > 2:
            width = HL * HEAD
            for i in range(4):
                part = refs[0][i * 128 : (i + 1) * 128, :]
                out[CH:, i * width : (i + 1) * width] = part

    gains[...] += row_sum8(total * hat)


def close(chunk, weight, rows, back, grads, mixed):
    tile = pl.BlockSpec((TILE, D), lambda t: (t, 0))
    whole = lambda shape: pl.BlockSpec(shape, lambda t: (0,) * len(shape))
    rows, rows_specs = tiles_of(rows)
    height, kind = (CH, F32) if chunk == 0 else (CH + 128, BF16)
    more, more_specs = [], []
    if chunk != 0:
        more, more_specs = [mixed], [pl.BlockSpec((CH, HL * HEAD), lambda t: (chunk, 0))]
    return pl.pallas_call(
        close_kernel,
        grid=(PER,),
        in_specs=[pl.BlockSpec((D, D), lambda t: (0, 2))]
        + rows_specs
        + [tile, pl.BlockSpec((TILE, QKV), lambda t: (chunk * PER + t, 0))]
        + more_specs,
        out_specs=[whole((height, D)), whole((8, D))],
        out_shape=[pltpu.HBM((height, D), kind), pltpu.HBM((8, D), F32)],
        compiler_params=params(14),
        cost_estimate=cost(3),
        name="close",
    )(weight, *far_from(rows), *far_from([back, grads, *more]))


def output_kernel(rows, own, part1, part2, part3, bias, mixed, weight, *refs):
    out = refs[-1]
    total = rows[...].astype(F32) + own[...] + bias[...]
    for part in (part1, part2, part3):
        total = total + part[...].astype(F32)
    total = total + dot(mixed[...], weight[:, QKV:], NT)
    width = HL * HEAD
    for message, their in zip(refs[:3], refs[3:6]):
        blocks = [message[:, i * width : (i + 1) * width] for i in range(4)]
        first = jnp.concatenate(blocks[:2], axis=0)
        second = jnp.concatenate(blocks[2:], axis=0)
        theirs = jnp.where(pl.program_id(0) == 0, first, second)
        total = total + dot(theirs, their[...], NN)
    out[...] = total.astype(BF16)


def output_rows(rows, own, parts, bias, mixed, weights, messages):
    tile = lambda width: pl.BlockSpec((TILE, width), lambda t: (t, 0))
    whole = lambda shape: pl.BlockSpec(shape, lambda t: (0,) * len(shape))
    below = [
        pl.BlockSpec((128, D), lambda t: (CH // 128, 0)),
        pl.BlockSpec((pl.Element(HL * HEAD), pl.Element(D)), lambda t: (CH, 0)),
    ]
    return pl.pallas_call(
        output_kernel,
        grid=(PER,),
        in_specs=[tile(D)] * 5
        + [whole((1, D)), tile(HL * HEAD), pl.BlockSpec((D, D), lambda t: (0, 2))]
        + [below[0]] * 3
        + [below[1]] * 3,
        out_specs=tile(D),
        out_shape=jax.ShapeDtypeStruct((CH, D), BF16),
        compiler_params=params(16),
        cost_estimate=cost(4),
        name="output_rows",
    )(
        rows,
        *far_from([own, *parts]),
        bias,
        *far_from([mixed]),
        weights,
        *far_from([*messages, *parts]),
    )


def input_kernel(live, rows, cot, own, part1, part2, part3, gain, out):
    total = own[...]
    for part in (part1, part2, part3):
        total = total + part[...].astype(F32)
    hat, inverse = norm_parts(rows[...].astype(F32))
    place = lax.broadcasted_iota(jnp.int32, (TILE, 1), 0) + pl.program_id(0) * TILE
    ups = jnp.where(place < live[0], cot[...].astype(F32), 0.0)
    out[...] = (ups + norm_back(total * gain[...], hat, inverse)).astype(BF16)


def input_rows(live, rows, cot, own, parts, gain):
    tile = pl.BlockSpec((TILE, D), lambda t: (t, 0))
    return pl.pallas_call(
        input_kernel,
        grid=(PER,),
        in_specs=[pl.BlockSpec(memory_space=pltpu.SMEM)]
        + [tile] * 6
        + [pl.BlockSpec((1, D), lambda t: (0, 0))],
        out_specs=tile,
        out_shape=jax.ShapeDtypeStruct((CH, D), BF16),
        compiler_params=params(12),
        cost_estimate=cost(4),
        name="input_rows",
    )(live, *far_from([rows, cot, own, *parts]), gain)


def tell_kernel(late_parts, early, gains_0, gains_1, gains_2, gains_3, head_gains, told, late):
    late[...] = jnp.sum(late_parts[...].astype(F32), axis=0)
    squares = jnp.sum(late[...] * late[...])
    squares = squares + jnp.sum(early[:, : 2 * HID] * early[:, : 2 * HID])
    gains = gains_0[...] + gains_1[...] + gains_2[...] + gains_3[...]
    gains = jnp.sum(gains, axis=0, keepdims=True)
    heads = jnp.sum(head_gains[...], axis=0, keepdims=True)
    q_part = sum(heads[:, h * HEAD : (h + 1) * HEAD] for h in range(HL))
    k_part = sum(heads[:, QK // 2 + h * HEAD : QK // 2 + (h + 1) * HEAD] for h in range(HL))
    biases = early[:, 2 * HID :].T
    depth = D // 32
    lane = lax.broadcasted_iota(jnp.int32, (1, TOLD - BASE - 2 * depth), 1)
    last = jnp.where(lane == 0, squares, 0.0)
    row = [gains, q_part, k_part, biases[0:1, :], biases[1:2, :], last]
    told[...] = jnp.broadcast_to(jnp.concatenate(row, axis=1)[None], told.shape)


def tell(late_parts, early, gains, head_gains):
    return pl.pallas_call(
        tell_kernel,
        out_shape=[
            pltpu.HBM((128, 1, TOLD), F32),
            pltpu.HBM((D // 32, D), F32),
        ],
        compiler_params=params(16),
        cost_estimate=cost(2),
        name="tell",
    )(*far_from([late_parts, early, *gains, head_gains]))


def finish_kernel(heard, early, late, *refs):
    ins, outs, norm, out_bias, hidden_bias, small = refs[:15], refs[15:30], *refs[30:]
    depth = D // 32
    for g in range(32):
        lane = slice(g * depth, (g + 1) * depth)
        rows = heard[4 * g : 4 * g + 4, BASE : BASE + 2 * depth]
        out_bias[:, lane] = rows[0:1, :depth]
        hidden_bias[:, lane] = rows[:, depth:]
    totals = jnp.sum(heard[...], axis=0, keepdims=True)
    for i in range(D // 128):
        lane = slice(i * 128, (i + 1) * 128)
        small[i : i + 1, :] = totals[:, lane]
        small[7 + i : 8 + i, :] = out_bias[:, lane]
        for j in range(BR):
            place = 13 + j * (HID // 128) + i
            small[place : place + 1, :] = hidden_bias[j : j + 1, lane]
    small[6:7, :] = totals[:, D:BASE]
    squares = totals[:, BASE + 2 * depth : BASE + 2 * depth + 1]
    small_squares = jnp.sum(small[...] * small[...], axis=1, keepdims=True)
    squares = squares + jnp.sum(small_squares, axis=0, keepdims=True)
    length = jnp.sqrt(squares)
    norm[...] = length
    factor = 1.0 / jnp.maximum(length, 1.0)

    def update(i, gradient, at=Ellipsis, rate=RATE_MATRIX, decay=DECAY_MATRIX):
        news = adam_update(
            ins[3 * i][at], ins[3 * i + 1][at], ins[3 * i + 2][at], gradient, factor, rate, decay
        )
        for out, new in zip(outs[3 * i : 3 * i + 3], news):
            out[at] = new

    for j in range(3):
        update(0, late[:, j * HL * HEAD : (j + 1) * HL * HEAD], at=j)
    update(1, late[:, QKV:])
    update(2, early[:, :HID])
    update(3, early[:, HID : 2 * HID])
    update(4, small[...], rate=RATE_SMALL, decay=0.0)


def finish(heard, early, late, arrays):
    return pl.pallas_call(
        finish_kernel,
        out_shape=[jax.ShapeDtypeStruct(value.shape, F32) for value in arrays]
        + [jax.ShapeDtypeStruct((1, 1), F32)],
        scratch_shapes=[
            pltpu.VMEM((1, D), F32),
            pltpu.VMEM((BR, HID), F32),
            pltpu.VMEM((37, 128), F32),
        ],
        compiler_params=params(16),
        cost_estimate=cost(4),
        name="finish",
    )(heard, *far_from([early, late, *arrays]))


def dp_pairs(step):
    pairs = []
    for y in range(4):
        for z in range(4):
            for c in range(2):
                y2, z2, c2 = step(y, z, c)
                pairs.append(((y * 4 + z) * 2 + c, ((y2 % 4) * 4 + z2 % 4) * 2 + c2))
    return pairs


def move_x(value, k):
    return lax.ppermute(value, "branch", [(i, (i + k) % BR) for i in range(BR)])


def move_y(value, k):
    return lax.ppermute(value, "dp", dp_pairs(lambda y, z, c: (y + k, z, c)))


def move_z(value, k):
    return lax.ppermute(value, "dp", dp_pairs(lambda y, z, c: (y, z + k, c)))


def move_core(value):
    return lax.ppermute(value, "dp", dp_pairs(lambda y, z, c: (y, z, 1 - c)))


def put(buffer, value, index, axis):
    return lax.dynamic_update_index_in_dim(buffer, value, index, axis)


def take(buffer, index, axis):
    return lax.dynamic_index_in_dim(buffer, index, axis, keepdims=False)


def gather_plane(own, y, z):
    line = jnp.zeros((4, *own.shape), own.dtype)
    line = put(line, own, z, 0)
    for k in (1, 3, 2):
        line = put(line, move_z(own, -k), (z + k) % 4, 0)
    plane = jnp.zeros((4, *line.shape), own.dtype)
    plane = put(plane, line, y, 0)
    came = [move_y(line, -k) for k in (1, 3, 2)]
    for k, part in zip((1, 3, 2), came):
        plane = put(plane, part, (y + k) % 4, 0)
    return plane, came[0]


def gather_cores(plane, other, c):
    whole = jnp.zeros((4, 4, 2, *plane.shape[2:]), plane.dtype)
    whole = put(whole, plane, c, 2)
    whole = put(whole, other, 1 - c, 2)
    return whole.reshape(32 * plane.shape[2], plane.shape[3])


def after(values, *earlier):
    return lax.optimization_barrier((values, earlier))[0]


def gather_rows(own):
    near = [move_x(own, -k) for k in (1, 3)]
    half = own.shape[0] // 2
    far = (move_x(near[0][:half], -1), move_x(near[1][half:], 1))
    return [own, near[0], far, near[1]]


def to_owners(grad):
    return lax.all_to_all(grad.reshape(32, D // 32, -1), "dp", 0, 0, tiled=True)


def adam_update(weight, first_moment, second_moment, gradient, factor, rate, decay):
    clipped = gradient * factor
    first_new = BETA_ONE * first_moment + (1.0 - BETA_ONE) * clipped
    second_new = BETA_TWO * second_moment + (1.0 - BETA_TWO) * clipped * clipped
    ratio = (
        first_new
        / (1.0 - BETA_ONE**STEP)
        / (jnp.sqrt(second_new / (1.0 - BETA_TWO**STEP)) + EPS_ADAM)
    )
    return (clipped, second_new, weight - rate * (ratio + decay * weight))


def body(
    block_input,
    cotangent,
    image_owner,
    image_length,
    image_start,
    qkv_weight,
    qkv_first,
    qkv_second,
    out_weight,
    out_first,
    out_second,
    up_weight,
    up_first,
    up_second,
    down_weight,
    down_first,
    down_second,
    small_weight,
    small_first,
    small_second,
):
    b = lax.axis_index("branch")
    g = lax.axis_index("dp")
    y, z, c = g // 8, (g // 2) % 4, g % 2
    depth = up_weight.shape[0]

    own = pack(up_weight, down_weight.T, qkv_weight, out_weight.T)
    plane, came = gather_plane(own, y, z)

    rows = gather_rows(block_input)
    other = move_core(after(plane, rows[1], rows[3]))
    weights = gather_cores(plane, other, c)
    cots = gather_rows(after(cotangent, rows[1], rows[3], other))

    plan, live, seg_row, seg_col, ln_gain, qk_gain, out_bias, hidden_bias = make_plan(
        after(small_weight, came).reshape(-1, 128), image_owner[None], image_length[None]
    )

    normed, q, key, v, hats, inverses = ([None] * BR for _ in range(6))
    for k in (0, 1, 3, 2):
        normed[k], q[k], key[k], v[k], hats[k], inverses[k] = project(
            rows[k], weights, ln_gain, qk_gain
        )

    ffn, back, act, pre, ups, mixed_grad = ([None] * BR for _ in range(6))
    for k in (0, 1, 3, 2):
        ffn[k], back[k], act[k], pre[k], ups[k], mixed_grad[k] = mlp(
            live[k][None], cots[k], normed[k], weights, hidden_bias, *((MSG, BF16) if k else (CH, F32))
        )

    ffn_parts = [move_x(ffn[k], k) for k in (1, 2, 3)]
    early_grad, normed, ups = early_weights(normed, pre, ups, act)
    early_parts = to_owners(early_grad)
    mixed, dq, dk, dv = attend(plan, q, key, v, after(mixed_grad, early_grad), seg_row, seg_col)
    late_grad, qkv_grads, mixed, head_gains = late_weights(
        normed, ups, qk_gain, hats, inverses, (after(dq, early_parts, ffn_parts), dk, dv, mixed)
    )
    late_parts = to_owners(late_grad)

    grads, gain_parts = [None] * BR, [None] * BR
    for k in (2, 1, 3, 0):
        grads[k], gain_parts[k] = close(k, weights, rows[k], back[k], qkv_grads, mixed)
    messages = [move_x(grads[k], k) for k in (1, 2, 3)]
    block_output = output_rows(
        block_input, ffn[0], ffn_parts, out_bias, mixed, weights, messages
    )
    input_grad = input_rows(live[:1], block_input, cotangent, grads[0], messages, ln_gain)

    early = jnp.sum(early_parts.astype(F32), axis=0)
    told, late = tell(late_parts, early, gain_parts, head_gains)
    heard = lax.all_to_all(told, ("dp", "branch"), 0, 0, tiled=True).reshape(128, TOLD)
    flat = lambda value: value.reshape(-1, 128)
    *news, norm = finish(
        heard,
        early,
        late,
        (
            *(qkv_weight, qkv_first, qkv_second),
            *(out_weight.T, out_first.T, out_second.T),
            *(up_weight, up_first, up_second),
            *(down_weight.T, down_first.T, down_second.T),
            *(flat(small_weight), flat(small_first), flat(small_second)),
        ),
    )
    qkv_new, out_new, up_new, down_new, small_new = (news[3 * i : 3 * i + 3] for i in range(5))
    return (
        block_output,
        input_grad,
        norm.reshape(()),
        *qkv_new,
        *(value.T for value in out_new),
        *up_new,
        *(value.T for value in down_new),
        *(value.reshape(-1) for value in small_new),
    )


def solution(mesh):
    rows = P(("dp", "branch"), None)
    qkv = [P(None, "dp", "branch")] * 3
    out = [P("branch", "dp")] * 3
    up = [P("dp", "branch")] * 3
    small = [P()] * 3
    return jax.shard_map(
        body,
        mesh=mesh,
        in_specs=(rows, rows, P(), P(), P(), *qkv, *out, *up, *out, *small),
        out_specs=(rows, rows, P(), *qkv, *out, *up, *out, *small),
        check_vma=False,
    )
```

```python
import functools

import jax
import jax.numpy as jnp
from jax import lax
from jax.experimental import pallas as pl
from jax.experimental.pallas import tpu as pltpu
from jax.sharding import PartitionSpec as P

D = 768
HEADS = 12
HEAD = 64
FF = 3072
CAP = 2048
SMALL_LEN = 196
STEP = 10

EPS_NORM = 1e-06
BETA_ONE = 0.9
BETA_TWO = 0.95
EPS_ADAM = 1e-08
RATE_MATRIX = 0.1
RATE_SMALL = 1.0
DECAY_MATRIX = 0.1

F32 = jnp.float32
BF16 = jnp.bfloat16
NN = (((1,), (0,)), ((), ()))
NT = (((1,), (1,)), ((), ()))
TN = (((0,), (0,)), ((), ()))

BR = 4
HL = HEADS // BR
HID = FF // BR
QK = 2 * HL * HEAD
QKV = 3 * HL * HEAD
EARLY = 2 * HID + 128
BASE = D + 2 * HEAD
TOLD = 1024
CH = CAP // BR
MSG = CH + HL * HEAD
TILE = 256
PER = CH // TILE
QT = 512
KS = 512
MS = 256
SAFE = 60.0


def dot(left, right, dims):
    return lax.dot_general(left, right, dims, preferred_element_type=F32)


def cost(us):
    return pl.CostEstimate(flops=int(us * 1.1e9), bytes_accessed=0, transcendentals=0)


def params(mib):
    return pltpu.CompilerParams(vmem_limit_bytes=mib * 2**20)


def far_from(arrays):
    return [pltpu.with_memory_space_constraint(value, pltpu.HBM) for value in arrays]


def norm_parts(values):
    average = jnp.mean(values, axis=-1, keepdims=True)
    centered = values - average
    inverse = lax.rsqrt(jnp.mean(centered * centered, axis=-1, keepdims=True) + EPS_NORM)
    return (centered * inverse, inverse)


def norm_back(grad, hat, inverse):
    return inverse * (
        grad
        - jnp.mean(grad, axis=-1, keepdims=True)
        - hat * jnp.mean(grad * hat, axis=-1, keepdims=True)
    )


def lane_sum(values):
    width = values.shape[1] // 128
    total = values[:, :128]
    for i in range(1, width):
        total = total + values[:, i * 128 : (i + 1) * 128]
    return total


def row_sum8(values):
    return jnp.sum(values.reshape(values.shape[0] // 8, 8, values.shape[1]), axis=0)


def head_means(values, heads_matrix):
    high = values.astype(BF16)
    rest = (values - high.astype(F32)).astype(BF16)
    return dot(high, heads_matrix, NN) + dot(rest, heads_matrix, NN)


def heads_of(width):
    row = lax.broadcasted_iota(jnp.int32, (width, width), 0) >> 6
    column = lax.broadcasted_iota(jnp.int32, (width, width), 1) >> 6
    return jnp.where(row == column, 1.0 / HEAD, 0.0).astype(BF16)


def head_norm(pair, heads_matrix):
    centered = pair - head_means(pair, heads_matrix)
    inverse = lax.rsqrt(head_means(centered * centered, heads_matrix) + EPS_NORM)
    return (centered * inverse, inverse)


def pack_kernel(up, down_t, qkv, out_t, packed):
    packed[:, :HID] = up[...].astype(BF16)
    packed[:, HID : 2 * HID] = down_t[...].astype(BF16)
    parts = [qkv[j] for j in range(3)] + [out_t[...]]
    packed[:, 2 * HID :] = jnp.concatenate(parts, axis=1).astype(BF16)


def pack(up, down_t, qkv, out_t):
    return pl.pallas_call(
        pack_kernel,
        out_shape=jax.ShapeDtypeStruct((D // 32, 2 * HID + D), BF16),
        cost_estimate=cost(1),
        name="pack",
    )(up, down_t, qkv, out_t)


def plan_kernel(
    small, owner, length,
    plan, live, seg_row, seg_col, ln_gain, qk_gain, out_bias, hidden_bias,
):
    group, branch = lax.axis_index("dp"), lax.axis_index("branch")
    gains = D // 128
    for i in range(gains):
        lane = slice(i * 128, (i + 1) * 128)
        ln_gain[:, lane] = small[i : i + 1, :]
        out_bias[:, lane] = small[gains + 1 + i : gains + 2 + i, :]
        hidden_bias[:, lane] = small[pl.ds(2 * gains + 1 + branch * (HID // 128) + i, 1), :]
    both = small[gains : gains + 1, :]
    q_gain, k_gain = both[:, :HEAD], both[:, HEAD:]
    qk_gain[...] = jnp.concatenate([q_gain] * HL + [k_gain] * HL, axis=1)
    bound = 8.0 * 1.02 * jnp.max(jnp.abs(q_gain)) * jnp.max(jnp.abs(k_gain))

    size = jnp.where(owner[...] == group, length[...], 0)
    tokens = jnp.sum(size)
    big = jnp.where(jnp.max(size) == CAP, 1, 0)

    def label(shape, axis):
        place = lax.broadcasted_iota(jnp.int32, shape, axis) + CH * branch
        place = jnp.where(place >= CAP, place - CAP, place)
        image = jnp.where(big == 1, 0, (place * 2675) >> 19)
        return jnp.where(place < tokens, image, CAP)

    seg_row[...] = label((1, CAP), 1)
    seg_col[...] = label((CAP, 1), 0)
    plan[0] = jnp.where(bound <= SAFE, 1 + big, 0)
    for t in range(CAP // QT):
        start = lax.rem(t * QT + CH * branch, CAP)
        last = start + QT - 1
        begin = jnp.where(start < tokens, ((start * 2675) >> 19) * SMALL_LEN, tokens)
        end = jnp.minimum((((last * 2675) >> 19) + 1) * SMALL_LEN, tokens)
        end = jnp.where(last >= tokens, CAP, end)
        begin = jnp.where(big == 1, 0, begin)
        end = jnp.where(big == 1, CAP, end)
        strip = begin // MS
        plan[1 + t] = lax.rem(strip + CAP // MS - (CH // MS) * branch, CAP // MS)
        plan[5 + t] = (end + MS - 1) // MS - strip
        plan[9 + t] = jnp.where(start < tokens, 1, 0)
        plan[21 + t] = jnp.where(last >= tokens, 1, 0)
    for t in range(CAP // MS):
        start = lax.rem(t * MS + CH * branch, CAP)
        plan[13 + t] = jnp.where(start < tokens, 1, 0)
    for k in range(BR):
        start = lax.rem((branch + k) * CH, CAP)
        live[k] = jnp.clip(tokens - start, 0, CH)


def make_plan(small, owner, length):
    smem = pl.BlockSpec(memory_space=pltpu.SMEM)
    vmem = pl.BlockSpec(memory_space=pltpu.VMEM)
    row = lambda width, kind=F32: jax.ShapeDtypeStruct((1, width), kind)
    return pl.pallas_call(
        plan_kernel,
        in_specs=[vmem] * 3,
        out_specs=[smem, smem] + [vmem] * 6,
        out_shape=[
            jax.ShapeDtypeStruct((25,), jnp.int32),
            jax.ShapeDtypeStruct((BR,), jnp.int32),
            row(CAP, jnp.int32),
            jax.ShapeDtypeStruct((CAP, 1), jnp.int32),
            row(D),
            row(QK),
            row(D),
            row(HID),
        ],
        cost_estimate=cost(3),
        name="make_plan",
    )(small, owner, length)


def tiles_of(chunk):
    if isinstance(chunk, tuple):
        return list(chunk), [pl.BlockSpec((TILE, D), lambda t: (0, 0))] * 2
    specs = [pl.BlockSpec((TILE, D), lambda t, i=i: (i, 0)) for i in range(PER)]
    return [chunk] * PER, specs


def tile_now(first, second):
    return jnp.where(pl.program_id(0) == 0, first[...], second[...]).astype(F32)


def project_kernel(
    rows_0, rows_1, weight, gain, qk_gain, normed, q_out, k_out, v_out, qk_hat, qk_inverse
):
    hat, _ = norm_parts(tile_now(rows_0, rows_1))
    low = (hat * gain[...]).astype(BF16)
    normed[...] = low
    raw = dot(low, weight[:, :QKV], NN)
    hat, inverse = head_norm(raw[:, :QK], heads_of(QK))
    qk_hat[...] = hat
    qk_inverse[...] = inverse
    value = (hat * qk_gain[...]).astype(BF16)
    vals = raw[:, QK:].astype(BF16)
    for h in range(HL):
        lane = slice(h * HEAD, (h + 1) * HEAD)
        q_out[h] = value[:, lane] * jnp.asarray(HEAD**-0.5, BF16)
        k_out[h] = value[:, QK // 2 + h * HEAD : QK // 2 + (h + 1) * HEAD]
        v_out[h] = vals[:, lane]


def project(rows, weights, gain, qk_gain):
    whole = lambda shape: pl.BlockSpec(shape, lambda t: (0,) * len(shape))
    heads = pl.BlockSpec((HL, TILE, HEAD), lambda t: (0, t, 0))
    tile = pl.BlockSpec((TILE, D), lambda t: (t, 0))
    rows, rows_specs = tiles_of(rows)
    return pl.pallas_call(
        project_kernel,
        grid=(PER,),
        in_specs=rows_specs
        + [
            pl.BlockSpec((D, D), lambda t: (0, 2)),
            whole((1, D)),
            whole((1, QK)),
        ],
        out_specs=[tile, heads, heads, heads] + [pl.BlockSpec((TILE, QK), lambda t: (t, 0))] * 2,
        out_shape=[jax.ShapeDtypeStruct((CH, D), BF16)]
        + [pltpu.HBM((HL, CH, HEAD), BF16)] * 3
        + [pltpu.HBM((CH, QK), F32)] * 2,
        compiler_params=params(16),
        cost_estimate=cost(3),
        name="project",
    )(*rows, weights, gain, qk_gain)


def mlp_kernel(
    live, cot_0, cot_1, normed, up, down_t, proj, bias,
    ffn, back, act_out, pre_out, ups_out, mix_out,
):
    t = pl.program_id(0)
    pre = dot(normed[...], up[...], NN) + bias[...]
    half = 0.5 * (1.0 + lax.erf(pre * (2.0**-0.5)))
    act = (pre * half).astype(BF16)
    slope = half + pre * (jnp.exp(-0.5 * pre * pre) * 0.3989422804014327)
    act_out[...] = act
    ffn[pl.ds(t * TILE, TILE), :] = dot(act, down_t[...], NT).astype(ffn.dtype)
    place = lax.broadcasted_iota(jnp.int32, (TILE, 1), 0) + t * TILE
    ups = jnp.where(place < live[0], tile_now(cot_0, cot_1), 0.0).astype(BF16)
    ups_out[...] = ups
    grad = (dot(ups, down_t[...], NN) * slope).astype(BF16)
    pre_out[...] = grad
    back[...] = dot(grad, up[...], NT)
    mixed = dot(ups, proj[:, QKV:], NN).astype(BF16)
    if ffn.shape[0] > CH:

        @pl.when(t == 0)
        def _():
            ffn[CH:, :] = proj[:, QKV:].astype(F32).T.astype(BF16)

    for h in range(HL):
        mix_out[h] = mixed[:, h * HEAD : (h + 1) * HEAD]


def mlp(live, cot, normed, weights, bias, height, kind):
    whole = lambda shape: pl.BlockSpec(shape, lambda t: (0,) * len(shape))
    tile = pl.BlockSpec((TILE, D), lambda t: (t, 0))
    cot, cot_specs = tiles_of(cot)
    return pl.pallas_call(
        mlp_kernel,
        grid=(PER,),
        in_specs=[pl.BlockSpec(memory_space=pltpu.SMEM)]
        + cot_specs
        + [
            tile,
            pl.BlockSpec((D, HID), lambda t: (0, 0)),
            pl.BlockSpec((D, HID), lambda t: (0, 1)),
            pl.BlockSpec((D, D), lambda t: (0, 2)),
            whole((1, HID)),
        ],
        out_specs=[whole((height, D))]
        + [tile] * 4
        + [pl.BlockSpec((HL, TILE, HEAD), lambda t: (0, t, 0))],
        out_shape=[pltpu.HBM((height, D), kind), pltpu.HBM((CH, D), F32)]
        + [jax.ShapeDtypeStruct((CH, D), BF16)] * 3
        + [pltpu.HBM((HL, CH, HEAD), BF16)],
        compiler_params=params(20),
        cost_estimate=cost(6),
        name="mlp",
    )(live, *cot, normed, weights, weights, weights, bias)


def attend_kernel(plan, *refs):
    q_refs, k_refs, v_refs, g_refs = (refs[i * BR : (i + 1) * BR] for i in range(4))
    seg_row, seg_col, mixed, dq_out, dk_out, dv_out = refs[4 * BR : 4 * BR + 6]
    probs, pgrad, dk_sum, dv_sum, q_ref, k_ref, v_ref, g_ref = refs[4 * BR + 6 :]
    t = pl.program_id(1)
    for k in range(BR):

        @pl.when(t == k)
        def _():
            q_ref[...] = q_refs[k][...]
            g_ref[...] = g_refs[k][...]

    @pl.when(t == 0)
    def _():
        dk_sum[...] = jnp.zeros_like(dk_sum)
        dv_sum[...] = jnp.zeros_like(dv_sum)
        for k in range(BR):
            k_ref[:, k * CH : (k + 1) * CH] = k_refs[k][...]
            v_ref[:, k * CH : (k + 1) * CH] = v_refs[k][...]

    query = q_ref[0]
    grad = g_ref[0]

    @pl.when(plan[0] == 2)
    def _():
        total = jnp.zeros((QT, 128), F32)
        weighted = jnp.zeros((QT, 128), F32)
        for j in range(CAP // KS):
            part = slice(j * KS, (j + 1) * KS)
            e = jnp.exp(dot(query, k_ref[0, part], NT))
            probs[:, part] = e
            pg = dot(grad, v_ref[0, part], NT)
            pgrad[:, part] = pg
            total = total + lane_sum(e)
            weighted = weighted + lane_sum(e * pg)
        scale = 1.0 / jnp.sum(total, axis=1, keepdims=True)
        delta = jnp.sum(weighted, axis=1, keepdims=True) * scale
        out = jnp.zeros((QT, HEAD), F32)
        dq = jnp.zeros((QT, HEAD), F32)
        for j in range(CAP // KS):
            part = slice(j * KS, (j + 1) * KS)
            p = probs[:, part] * scale
            low = p.astype(BF16)
            ds = (p * (pgrad[:, part] - delta)).astype(BF16)
            out = out + dot(low, v_ref[0, part], NN)
            dq = dq + dot(ds, k_ref[0, part], NN)
            dv_sum[:, part] += dot(grad, low, TN)
            dk_sum[:, part] += dot(query, ds, TN)
        mixed[0] = out.astype(BF16)
        dq_out[0] = dq * HEAD**-0.5

    @pl.when(plan[0] == 1)
    def _():
        mixed[...] = jnp.zeros_like(mixed)
        dq_out[...] = jnp.zeros_like(dq_out)
        for s in range(QT // MS):
            index = t * (QT // MS) + s
            at = slice(s * MS, (s + 1) * MS)

            @pl.when(plan[13 + index] == 1)
            def _():
                qs, gs, seg = query[at], grad[at], seg_col[at, :]
                strips, es, pgs = [], [], []
                for j in range(3):
                    near = lax.rem(index + (CAP // MS - 1) + j, CAP // MS)
                    strip = pl.ds(pl.multiple_of(near * MS, MS), MS)
                    score = dot(qs, k_ref[0, strip], NT)
                    strips.append(strip)
                    es.append(jnp.where(seg == seg_row[:, strip], jnp.exp(score), 0.0))
                    pgs.append(dot(gs, v_ref[0, strip], NT))
                total = sum(lane_sum(e) for e in es)
                weighted = sum(lane_sum(e * pg) for e, pg in zip(es, pgs))
                scale = 1.0 / jnp.sum(total, axis=1, keepdims=True)
                delta = jnp.sum(weighted, axis=1, keepdims=True) * scale
                out = jnp.zeros((MS, HEAD), F32)
                dq = jnp.zeros((MS, HEAD), F32)
                for strip, e, pg in zip(strips, es, pgs):
                    p = e * scale
                    low = p.astype(BF16)
                    ds = (p * (pg - delta)).astype(BF16)
                    out = out + dot(low, v_ref[0, strip], NN)
                    dq = dq + dot(ds, k_ref[0, strip], NN)
                    dv_sum[:, strip] += dot(gs, low, TN)
                    dk_sum[:, strip] += dot(qs, ds, TN)
                mixed[0, at, :] = out.astype(BF16)
                dq_out[0, at, :] = dq * HEAD**-0.5

        @pl.when(plan[21 + t] == 1)
        def _():
            total = jnp.zeros((QT, 128), F32)
            for j in range(CAP // KS):
                part = slice(j * KS, (j + 1) * KS)
                e = jnp.exp(dot(query, k_ref[0, part], NT))
                e = jnp.where(seg_row[:, part] == CAP, e, 0.0)
                probs[:, part] = e
                total = total + lane_sum(e)
            scale = 1.0 / jnp.sum(total, axis=1, keepdims=True)
            out = jnp.zeros((QT, HEAD), F32)
            for j in range(CAP // KS):
                part = slice(j * KS, (j + 1) * KS)
                out = out + dot((probs[:, part] * scale).astype(BF16), v_ref[0, part], NN)
            mixed[0] = jnp.where(seg_col[...] == CAP, out, mixed[0].astype(F32)).astype(BF16)

    @pl.when(plan[0] == 0)
    def _():
        first, count, live = plan[1 + t], plan[5 + t], plan[9 + t]
        seg = seg_col[...]

        def strip(i):
            return pl.ds(pl.multiple_of(lax.rem(first + i, CAP // MS) * MS, MS), MS)

        def scores(i, top):
            at = strip(i)
            s = dot(query, k_ref[0, at], NT)
            s = jnp.where(seg == seg_row[:, at], s, -1e30)
            probs[:, at] = s
            return jnp.maximum(top, jnp.max(s, axis=1, keepdims=True))

        top = lax.fori_loop(0, count, scores, jnp.full((QT, 1), -1e30, F32))

        def exps(i, total):
            at = strip(i)
            e = jnp.exp(probs[:, at] - top)
            probs[:, at] = e
            return total + jnp.sum(e, axis=1, keepdims=True)

        total = lax.fori_loop(0, count, exps, jnp.zeros((QT, 1), F32))
        scale = 1.0 / total

        def sums(i, out):
            at = strip(i)
            p = probs[:, at] * scale
            probs[:, at] = p
            return out + dot(p.astype(BF16), v_ref[0, at], NN)

        out = lax.fori_loop(0, count, sums, jnp.zeros((QT, HEAD), F32))
        mixed[0] = out.astype(BF16)
        dq_out[...] = jnp.zeros_like(dq_out)

        @pl.when(live == 1)
        def _():
            def deltas(i, delta):
                at = strip(i)
                pg = dot(grad, v_ref[0, at], NT)
                pgrad[:, at] = pg
                return delta + jnp.sum(probs[:, at] * pg, axis=1, keepdims=True)

            delta = lax.fori_loop(0, count, deltas, jnp.zeros((QT, 1), F32))

            def backs(i, carry):
                at = strip(i)
                p = probs[:, at]
                low = p.astype(BF16)
                ds = (p * (pgrad[:, at] - delta)).astype(BF16)
                dq_out[0] += dot(ds, k_ref[0, at], NN) * HEAD**-0.5
                dv_sum[:, at] += dot(grad, low, TN)
                dk_sum[:, at] += dot(query, ds, TN)
                return carry

            lax.fori_loop(0, count, backs, 0)

    @pl.when(t == CAP // QT - 1)
    def _():
        dv_out[0] = dv_sum[...].T.astype(BF16)
        dk_out[0] = dk_sum[...].T


def attend(plan, q, k, v, g, seg_row, seg_col):
    chunk = pl.BlockSpec((1, CH, HEAD), lambda h, t: (h, 0, 0))
    out = pl.BlockSpec((1, QT, HEAD), lambda h, t: (h, t, 0))
    full = pl.BlockSpec((1, CAP, HEAD), lambda h, t: (h, 0, 0))
    flat = lambda kind: pltpu.HBM((HL, CAP, HEAD), kind)
    return pl.pallas_call(
        attend_kernel,
        grid=(HL, CAP // QT),
        in_specs=[pl.BlockSpec(memory_space=pltpu.SMEM)]
        + [chunk] * (4 * BR)
        + [
            pl.BlockSpec((1, CAP), lambda h, t: (0, 0)),
            pl.BlockSpec((QT, 1), lambda h, t: (t, 0)),
        ],
        out_specs=[out, out, full, full],
        out_shape=[flat(BF16), flat(F32), flat(F32), flat(BF16)],
        scratch_shapes=[
            pltpu.VMEM((QT, CAP), F32),
            pltpu.VMEM((QT, CAP), F32),
            pltpu.VMEM((HEAD, CAP), F32),
            pltpu.VMEM((HEAD, CAP), F32),
            pltpu.VMEM((1, QT, HEAD), BF16),
            pltpu.VMEM((1, CAP, HEAD), BF16),
            pltpu.VMEM((1, CAP, HEAD), BF16),
            pltpu.VMEM((1, QT, HEAD), BF16),
        ],
        compiler_params=params(24),
        cost_estimate=cost(48),
        name="attend",
    )(plan, *far_from([*q, *k, *v, *g]), seg_row, seg_col)


def early_kernel(*refs):
    normed, pre, ups, act = (refs[i * BR : (i + 1) * BR] for i in range(4))
    out, normed_out, ups_out, total, bias = refs[4 * BR :]
    t = pl.program_id(0)

    @pl.when(t == 0)
    def _():
        total[...] = jnp.zeros_like(total)
        bias[...] = jnp.zeros_like(bias)

    def joined(parts):
        return jnp.concatenate([part[...] for part in parts], axis=0)

    for k in range(BR):
        normed_out[k] = normed[k][...]
        ups_out[k] = ups[k][...]
        bias[...] += row_sum8(pre[k][...].astype(F32))
    lane = lax.broadcasted_iota(jnp.int32, (CH, 128), 1)
    first = jnp.where(lane == 0, 1.0, 0.0).astype(BF16)
    total[:, :HID] += dot(joined(normed), joined(pre), TN)
    right = jnp.concatenate([joined(act), first], axis=1)
    total[:, HID:] += dot(joined(ups), right, TN)

    @pl.when(t == BR - 1)
    def _():
        out[:, : 2 * HID] = total[:, : 2 * HID].astype(BF16)
        column = jnp.sum(bias[...].T, axis=1, keepdims=True)
        lane = lax.broadcasted_iota(jnp.int32, (D, 128), 1)
        out[:, 2 * HID :] = jnp.where(lane == 1, column, total[:, 2 * HID :]).astype(BF16)


def early_weights(normed, pre, ups, act):
    tile = pl.BlockSpec((CH // BR, D), lambda t: (t, 0))
    joined = pl.BlockSpec((BR, CH // BR, D), lambda t: (0, t, 0))
    return pl.pallas_call(
        early_kernel,
        grid=(BR,),
        in_specs=[tile] * (4 * BR),
        out_specs=[pl.BlockSpec((D, EARLY), lambda t: (0, 0)), joined, joined],
        out_shape=[pltpu.HBM((D, EARLY), BF16)]
        + [pltpu.HBM((BR, CH, D), BF16)] * 2,
        scratch_shapes=[pltpu.VMEM((D, EARLY), F32), pltpu.VMEM((8, HID), F32)],
        compiler_params=params(26),
        cost_estimate=cost(6),
        name="early_weights",
    )(*normed, *pre, *ups, *act)


def back_kernel(qk_gain, *refs):
    hats, inverses, pieces = refs[:BR], refs[BR : 2 * BR], refs[2 * BR : -3]
    grads_out, mixed_out, gains = refs[-3:]
    t = pl.program_id(0)
    dq, dk, dv, mixed = pieces

    @pl.when(t == 0)
    def _():
        gains[...] = jnp.zeros_like(gains)

    matrix = heads_of(QK)
    pair = jnp.concatenate([r[h] for r in (dq, dk) for h in range(HL)], axis=1)

    def back(hat, inverse):
        gains[...] += row_sum8(pair * hat)
        scaled = pair * qk_gain[...]
        mean = dot(scaled.astype(BF16), matrix, NN)
        slope = dot((scaled * hat).astype(BF16), matrix, NN)
        raw = inverse * (scaled - mean - hat * slope)
        grads_out[:, :QK] = raw.astype(BF16)

    for k in range(BR):

        @pl.when(t == k)
        def _():
            back(hats[k][...], inverses[k][...])

    grads_out[:, QK:] = jnp.concatenate([dv[h] for h in range(HL)], axis=1)
    mixed_out[...] = jnp.concatenate([mixed[h] for h in range(HL)], axis=1)


def back_heads(qk_gain, hats, inverses, pieces):
    tile = lambda width: pl.BlockSpec((CH, width), lambda t: (t, 0))
    whole = lambda shape: pl.BlockSpec(shape, lambda t: (0,) * len(shape))
    once = pl.BlockSpec((CH, QK), lambda t: (0, 0), pipeline_mode=pl.Buffered(1))
    return pl.pallas_call(
        back_kernel,
        grid=(BR,),
        in_specs=[whole((1, QK))]
        + [once] * (2 * BR)
        + [pl.BlockSpec((HL, CH, HEAD), lambda t: (0, t, 0))] * 4,
        out_specs=[tile(QKV), tile(HL * HEAD), whole((8, QK))],
        out_shape=[
            pltpu.HBM((CAP, QKV), BF16),
            pltpu.HBM((CAP, HL * HEAD), BF16),
            jax.ShapeDtypeStruct((8, QK), F32),
        ],
        compiler_params=params(24),
        cost_estimate=cost(6),
        name="back_heads",
    )(qk_gain, *far_from([*hats, *inverses, *pieces]))


def late_kernel(normed, ups, grads, mixed, out, total):
    t = pl.program_id(0)

    @pl.when(t == 0)
    def _():
        total[...] = jnp.zeros_like(total)

    total[:, :QKV] += dot(normed[0], grads[...], TN)
    total[:, QKV:] += dot(ups[0], mixed[...], TN)

    @pl.when(t == BR - 1)
    def _():
        out[...] = total[...].astype(BF16)


def late_weights(normed, ups, grads, mixed):
    tile = lambda width: pl.BlockSpec((CH, width), lambda t: (t, 0))
    return pl.pallas_call(
        late_kernel,
        grid=(BR,),
        in_specs=[pl.BlockSpec((1, CH, D), lambda t: (t, 0, 0))] * 2
        + [tile(QKV), tile(HL * HEAD)],
        out_specs=pl.BlockSpec((D, D), lambda t: (0, 0)),
        out_shape=pltpu.HBM((D, D), BF16),
        scratch_shapes=[pltpu.VMEM((D, D), F32)],
        compiler_params=params(20),
        cost_estimate=cost(6),
        name="late_weights",
    )(*far_from((normed, ups, grads, mixed)))


def close_kernel(weight, rows_0, rows_1, back, grads, *refs):
    out, gains = refs[-2:]
    t = pl.program_id(0)
    total = back[...] + dot(grads[...], weight[:, :QKV], NT)
    out[pl.ds(t * TILE, TILE), :] = total.astype(out.dtype)
    hat, _ = norm_parts(tile_now(rows_0, rows_1))

    @pl.when(t == 0)
    def _():
        gains[...] = jnp.zeros_like(gains)
        if len(refs) > 2:
            width = HL * HEAD
            for i in range(4):
                part = refs[0][i * 128 : (i + 1) * 128, :]
                out[CH:, i * width : (i + 1) * width] = part

    gains[...] += row_sum8(total * hat)


def close(chunk, weight, rows, back, grads, mixed):
    tile = pl.BlockSpec((TILE, D), lambda t: (t, 0))
    whole = lambda shape: pl.BlockSpec(shape, lambda t: (0,) * len(shape))
    rows, rows_specs = tiles_of(rows)
    height, kind = (CH, F32) if chunk == 0 else (CH + 128, BF16)
    more, more_specs = [], []
    if chunk != 0:
        more, more_specs = [mixed], [pl.BlockSpec((CH, HL * HEAD), lambda t: (chunk, 0))]
    return pl.pallas_call(
        close_kernel,
        grid=(PER,),
        in_specs=[pl.BlockSpec((D, D), lambda t: (0, 2))]
        + rows_specs
        + [tile, pl.BlockSpec((TILE, QKV), lambda t: (chunk * PER + t, 0))]
        + more_specs,
        out_specs=[whole((height, D)), whole((8, D))],
        out_shape=[pltpu.HBM((height, D), kind), pltpu.HBM((8, D), F32)],
        compiler_params=params(14),
        cost_estimate=cost(3),
        name="close",
    )(weight, *far_from(rows), *far_from([back, grads, *more]))


def begin_kernel(rows, own, part1, part2, part3, bias, mixed, weight, out):
    total = rows[...].astype(F32) + own[...] + bias[...]
    for part in (part1, part2, part3):
        total = total + part[...].astype(F32)
    out[...] = total + dot(mixed[...], weight[:, QKV:], NT)


def begin_rows(rows, own, parts, bias, mixed, weights):
    tile = lambda width: pl.BlockSpec((TILE, width), lambda t: (t, 0))
    return pl.pallas_call(
        begin_kernel,
        grid=(PER,),
        in_specs=[tile(D)] * 5
        + [pl.BlockSpec((1, D), lambda t: (0, 0)), tile(HL * HEAD)]
        + [pl.BlockSpec((D, D), lambda t: (0, 2))],
        out_specs=tile(D),
        out_shape=pltpu.HBM((CH, D), F32),
        compiler_params=params(16),
        cost_estimate=cost(4),
        name="begin_rows",
    )(*far_from([rows, own, *parts]), bias, *far_from([mixed]), weights)


def end_kernel(live, begun, rows, cot, own, part1, part2, part3, gain, *refs):
    messages, theirs, (output, input_grad) = refs[:3], refs[3:6], refs[6:]
    t = pl.program_id(0)
    total = begun[...]
    width = HL * HEAD
    for message, their in zip(messages, theirs):
        blocks = [message[:, i * width : (i + 1) * width] for i in range(4)]
        first = jnp.concatenate(blocks[:2], axis=0)
        second = jnp.concatenate(blocks[2:], axis=0)
        total = total + dot(jnp.where(t == 0, first, second), their[...], NN)
    output[...] = total.astype(BF16)

    total = own[...]
    for part in (part1, part2, part3):
        total = total + part[...].astype(F32)
    hat, inverse = norm_parts(rows[...].astype(F32))
    place = lax.broadcasted_iota(jnp.int32, (TILE, 1), 0) + t * TILE
    ups = jnp.where(place < live[0], cot[...].astype(F32), 0.0)
    input_grad[...] = (ups + norm_back(total * gain[...], hat, inverse)).astype(BF16)


def end_rows(live, begun, rows, cot, own, gain, messages, parts):
    tile = pl.BlockSpec((TILE, D), lambda t: (t, 0))
    below = pl.BlockSpec((128, D), lambda t: (CH // 128, 0))
    weight = pl.BlockSpec((pl.Element(HL * HEAD), pl.Element(D)), lambda t: (CH, 0))
    return pl.pallas_call(
        end_kernel,
        grid=(PER,),
        in_specs=[pl.BlockSpec(memory_space=pltpu.SMEM)]
        + [tile] * 7
        + [pl.BlockSpec((1, D), lambda t: (0, 0))]
        + [below] * 3
        + [weight] * 3,
        out_specs=[tile, tile],
        out_shape=[jax.ShapeDtypeStruct((CH, D), BF16)] * 2,
        compiler_params=params(20),
        cost_estimate=cost(6),
        name="end_rows",
    )(
        live,
        *far_from([begun, rows, cot, own, *messages]),
        gain,
        *far_from([*messages, *parts]),
    )


def tell_kernel(late_parts, early, gains_0, gains_1, gains_2, gains_3, head_gains, told, late):
    late[...] = jnp.sum(late_parts[...].astype(F32), axis=0)
    squares = jnp.sum(late[...] * late[...])
    squares = squares + jnp.sum(early[:, : 2 * HID] * early[:, : 2 * HID])
    gains = gains_0[...] + gains_1[...] + gains_2[...] + gains_3[...]
    gains = jnp.sum(gains, axis=0, keepdims=True)
    heads = jnp.sum(head_gains[...], axis=0, keepdims=True)
    q_part = sum(heads[:, h * HEAD : (h + 1) * HEAD] for h in range(HL))
    k_part = sum(heads[:, QK // 2 + h * HEAD : QK // 2 + (h + 1) * HEAD] for h in range(HL))
    biases = early[:, 2 * HID :].T
    depth = D // 32
    lane = lax.broadcasted_iota(jnp.int32, (1, TOLD - BASE - 2 * depth), 1)
    last = jnp.where(lane == 0, squares, 0.0)
    row = [gains, q_part, k_part, biases[0:1, :], biases[1:2, :], last]
    told[...] = jnp.broadcast_to(jnp.concatenate(row, axis=1)[None], told.shape)


def tell(late_parts, early, gains, head_gains):
    return pl.pallas_call(
        tell_kernel,
        out_shape=[
            pltpu.HBM((128, 1, TOLD), F32),
            pltpu.HBM((D // 32, D), F32),
        ],
        compiler_params=params(16),
        cost_estimate=cost(2),
        name="tell",
    )(*far_from([late_parts, early, *gains, head_gains]))


def finish_kernel(heard, early, late, *refs):
    ins, outs, norm, out_bias, hidden_bias, small = refs[:15], refs[15:30], *refs[30:]
    depth = D // 32
    for g in range(32):
        lane = slice(g * depth, (g + 1) * depth)
        rows = heard[4 * g : 4 * g + 4, BASE : BASE + 2 * depth]
        out_bias[:, lane] = rows[0:1, :depth]
        hidden_bias[:, lane] = rows[:, depth:]
    totals = jnp.sum(heard[...], axis=0, keepdims=True)
    for i in range(D // 128):
        lane = slice(i * 128, (i + 1) * 128)
        small[i : i + 1, :] = totals[:, lane]
        small[7 + i : 8 + i, :] = out_bias[:, lane]
        for j in range(BR):
            place = 13 + j * (HID // 128) + i
            small[place : place + 1, :] = hidden_bias[j : j + 1, lane]
    small[6:7, :] = totals[:, D:BASE]
    squares = totals[:, BASE + 2 * depth : BASE + 2 * depth + 1]
    small_squares = jnp.sum(small[...] * small[...], axis=1, keepdims=True)
    squares = squares + jnp.sum(small_squares, axis=0, keepdims=True)
    length = jnp.sqrt(squares)
    norm[...] = length
    factor = 1.0 / jnp.maximum(length, 1.0)

    def update(i, gradient, at=Ellipsis, rate=RATE_MATRIX, decay=DECAY_MATRIX):
        news = adam_update(
            ins[3 * i][at], ins[3 * i + 1][at], ins[3 * i + 2][at], gradient, factor, rate, decay
        )
        for out, new in zip(outs[3 * i : 3 * i + 3], news):
            out[at] = new

    for j in range(3):
        update(0, late[:, j * HL * HEAD : (j + 1) * HL * HEAD], at=j)
    update(1, late[:, QKV:])
    update(2, early[:, :HID])
    update(3, early[:, HID : 2 * HID])
    update(4, small[...], rate=RATE_SMALL, decay=0.0)


def finish(heard, early, late, arrays):
    return pl.pallas_call(
        finish_kernel,
        out_shape=[jax.ShapeDtypeStruct(value.shape, F32) for value in arrays]
        + [jax.ShapeDtypeStruct((1, 1), F32)],
        scratch_shapes=[
            pltpu.VMEM((1, D), F32),
            pltpu.VMEM((BR, HID), F32),
            pltpu.VMEM((37, 128), F32),
        ],
        compiler_params=params(16),
        cost_estimate=cost(4),
        name="finish",
    )(heard, *far_from([early, late, *arrays]))


def dp_pairs(step):
    pairs = []
    for y in range(4):
        for z in range(4):
            for c in range(2):
                y2, z2, c2 = step(y, z, c)
                pairs.append(((y * 4 + z) * 2 + c, ((y2 % 4) * 4 + z2 % 4) * 2 + c2))
    return pairs


def move_x(value, k):
    return lax.ppermute(value, "branch", [(i, (i + k) % BR) for i in range(BR)])


def move_y(value, k):
    return lax.ppermute(value, "dp", dp_pairs(lambda y, z, c: (y + k, z, c)))


def move_z(value, k):
    return lax.ppermute(value, "dp", dp_pairs(lambda y, z, c: (y, z + k, c)))


def move_core(value):
    return lax.ppermute(value, "dp", dp_pairs(lambda y, z, c: (y, z, 1 - c)))


def put(buffer, value, index, axis):
    return lax.dynamic_update_index_in_dim(buffer, value, index, axis)


def take(buffer, index, axis):
    return lax.dynamic_index_in_dim(buffer, index, axis, keepdims=False)


def gather_plane(own, y, z):
    line = jnp.zeros((4, *own.shape), own.dtype)
    line = put(line, own, z, 0)
    for k in (1, 3, 2):
        line = put(line, move_z(own, -k), (z + k) % 4, 0)
    plane = jnp.zeros((4, *line.shape), own.dtype)
    plane = put(plane, line, y, 0)
    came = [move_y(line, -k) for k in (1, 3, 2)]
    for k, part in zip((1, 3, 2), came):
        plane = put(plane, part, (y + k) % 4, 0)
    return plane, came[0]


def gather_cores(plane, other, c):
    whole = jnp.zeros((4, 4, 2, *plane.shape[2:]), plane.dtype)
    whole = put(whole, plane, c, 2)
    whole = put(whole, other, 1 - c, 2)
    return whole.reshape(32 * plane.shape[2], plane.shape[3])


def after(values, *earlier):
    return lax.optimization_barrier((values, earlier))[0]


def gather_rows(own):
    near = [move_x(own, -k) for k in (1, 3)]
    half = own.shape[0] // 2
    far = (move_x(near[0][:half], -1), move_x(near[1][half:], 1))
    return [own, near[0], far, near[1]]


def to_owners(grad):
    return lax.all_to_all(grad.reshape(32, D // 32, -1), "dp", 0, 0, tiled=True)


def adam_update(weight, first_moment, second_moment, gradient, factor, rate, decay):
    clipped = gradient * factor
    first_new = BETA_ONE * first_moment + (1.0 - BETA_ONE) * clipped
    second_new = BETA_TWO * second_moment + (1.0 - BETA_TWO) * clipped * clipped
    ratio = (
        first_new
        / (1.0 - BETA_ONE**STEP)
        / (jnp.sqrt(second_new / (1.0 - BETA_TWO**STEP)) + EPS_ADAM)
    )
    return (clipped, second_new, weight - rate * (ratio + decay * weight))


def body(
    block_input,
    cotangent,
    image_owner,
    image_length,
    image_start,
    qkv_weight,
    qkv_first,
    qkv_second,
    out_weight,
    out_first,
    out_second,
    up_weight,
    up_first,
    up_second,
    down_weight,
    down_first,
    down_second,
    small_weight,
    small_first,
    small_second,
):
    b = lax.axis_index("branch")
    g = lax.axis_index("dp")
    y, z, c = g // 8, (g // 2) % 4, g % 2
    depth = up_weight.shape[0]

    own = pack(up_weight, down_weight.T, qkv_weight, out_weight.T)
    plane, came = gather_plane(own, y, z)

    rows = gather_rows(block_input)
    other = move_core(after(plane, rows[1], rows[3]))
    weights = gather_cores(plane, other, c)
    cots = gather_rows(after(cotangent, rows[1], rows[3], other))

    plan, live, seg_row, seg_col, ln_gain, qk_gain, out_bias, hidden_bias = make_plan(
        after(small_weight, came).reshape(-1, 128), image_owner[None], image_length[None]
    )

    normed, q, key, v, hats, inverses = ([None] * BR for _ in range(6))
    for k in (0, 1, 3, 2):
        normed[k], q[k], key[k], v[k], hats[k], inverses[k] = project(
            rows[k], weights, ln_gain, qk_gain
        )

    ffn, back, act, pre, ups, mixed_grad = ([None] * BR for _ in range(6))
    for k in (0, 1, 3, 2):
        ffn[k], back[k], act[k], pre[k], ups[k], mixed_grad[k] = mlp(
            live[k][None], cots[k], normed[k], weights, hidden_bias, *((MSG, BF16) if k else (CH, F32))
        )

    ffn_parts = [move_x(ffn[k], k) for k in (1, 2, 3)]
    early_grad, normed, ups = early_weights(normed, pre, ups, act)
    early_parts = to_owners(early_grad)
    mixed, dq, dk, dv = attend(plan, q, key, v, after(mixed_grad, early_grad), seg_row, seg_col)
    qkv_grads, mixed, head_gains = back_heads(
        qk_gain, hats, inverses, (after(dq, early_parts, ffn_parts), dk, dv, mixed)
    )
    grads, gain_parts, messages = [None] * BR, [None] * BR, [None] * BR
    grads[2], gain_parts[2] = close(2, weights, rows[2], back[2], qkv_grads, mixed)
    messages[2] = move_x(grads[2], 2)
    late_grad = late_weights(normed, ups, after(qkv_grads, grads[2]), mixed)
    late_parts = to_owners(late_grad)
    for k in (1, 3, 0):
        grads[k], gain_parts[k] = close(k, weights, rows[k], back[k], qkv_grads, mixed)
    for k in (1, 3):
        messages[k] = move_x(grads[k], k)
    begun = begin_rows(block_input, ffn[0], ffn_parts, out_bias, mixed, weights)
    block_output, input_grad = end_rows(
        live[:1], begun, block_input, cotangent, grads[0], ln_gain, messages[1:], ffn_parts
    )

    early = jnp.sum(early_parts.astype(F32), axis=0)
    told, late = tell(late_parts, early, gain_parts, head_gains)
    heard = lax.all_to_all(told, ("dp", "branch"), 0, 0, tiled=True).reshape(128, TOLD)
    flat = lambda value: value.reshape(-1, 128)
    *news, norm = finish(
        heard,
        early,
        late,
        (
            *(qkv_weight, qkv_first, qkv_second),
            *(out_weight.T, out_first.T, out_second.T),
            *(up_weight, up_first, up_second),
            *(down_weight.T, down_first.T, down_second.T),
            *(flat(small_weight), flat(small_first), flat(small_second)),
        ),
    )
    qkv_new, out_new, up_new, down_new, small_new = (news[3 * i : 3 * i + 3] for i in range(5))
    return (
        block_output,
        input_grad,
        norm.reshape(()),
        *qkv_new,
        *(value.T for value in out_new),
        *up_new,
        *(value.T for value in down_new),
        *(value.reshape(-1) for value in small_new),
    )


def solution(mesh):
    rows = P(("dp", "branch"), None)
    qkv = [P(None, "dp", "branch")] * 3
    out = [P("branch", "dp")] * 3
    up = [P("dp", "branch")] * 3
    small = [P()] * 3
    return jax.shard_map(
        body,
        mesh=mesh,
        in_specs=(rows, rows, P(), P(), P(), *qkv, *out, *up, *out, *small),
        out_specs=(rows, rows, P(), *qkv, *out, *up, *out, *small),
        check_vma=False,
    )
```

```python
import functools

import jax
import jax.numpy as jnp
from jax import lax
from jax.experimental import pallas as pl
from jax.experimental.pallas import tpu as pltpu
from jax.sharding import PartitionSpec as P

D = 768
HEADS = 12
HEAD = 64
FF = 3072
CAP = 2048
SMALL_LEN = 196
STEP = 10

EPS_NORM = 1e-06
BETA_ONE = 0.9
BETA_TWO = 0.95
EPS_ADAM = 1e-08
RATE_MATRIX = 0.1
RATE_SMALL = 1.0
DECAY_MATRIX = 0.1

F32 = jnp.float32
BF16 = jnp.bfloat16
NN = (((1,), (0,)), ((), ()))
NT = (((1,), (1,)), ((), ()))
TN = (((0,), (0,)), ((), ()))

BR = 4
HL = HEADS // BR
HID = FF // BR
QK = 2 * HL * HEAD
QKV = 3 * HL * HEAD
EARLY = 2 * HID + 128
BASE = D + 2 * HEAD
TOLD = 1024
CH = CAP // BR
MSG = CH + HL * HEAD
TILE = 256
PER = CH // TILE
QT = 512
KS = 512
MS = 256
SAFE = 60.0


def dot(left, right, dims):
    return lax.dot_general(left, right, dims, preferred_element_type=F32)


def cost(us):
    return pl.CostEstimate(flops=int(us * 1.1e9), bytes_accessed=0, transcendentals=0)


def params(mib):
    return pltpu.CompilerParams(vmem_limit_bytes=mib * 2**20)


def far_from(arrays):
    return [pltpu.with_memory_space_constraint(value, pltpu.HBM) for value in arrays]


def norm_parts(values):
    average = jnp.mean(values, axis=-1, keepdims=True)
    centered = values - average
    inverse = lax.rsqrt(jnp.mean(centered * centered, axis=-1, keepdims=True) + EPS_NORM)
    return (centered * inverse, inverse)


def norm_back(grad, hat, inverse):
    return inverse * (
        grad
        - jnp.mean(grad, axis=-1, keepdims=True)
        - hat * jnp.mean(grad * hat, axis=-1, keepdims=True)
    )


def lane_sum(values):
    width = values.shape[1] // 128
    total = values[:, :128]
    for i in range(1, width):
        total = total + values[:, i * 128 : (i + 1) * 128]
    return total


def row_sum8(values):
    return jnp.sum(values.reshape(values.shape[0] // 8, 8, values.shape[1]), axis=0)


def head_means(values, heads_matrix):
    high = values.astype(BF16)
    rest = (values - high.astype(F32)).astype(BF16)
    return dot(high, heads_matrix, NN) + dot(rest, heads_matrix, NN)


def heads_of(width):
    row = lax.broadcasted_iota(jnp.int32, (width, width), 0) >> 6
    column = lax.broadcasted_iota(jnp.int32, (width, width), 1) >> 6
    return jnp.where(row == column, 1.0 / HEAD, 0.0).astype(BF16)


def head_norm(pair, heads_matrix):
    centered = pair - head_means(pair, heads_matrix)
    inverse = lax.rsqrt(head_means(centered * centered, heads_matrix) + EPS_NORM)
    return (centered * inverse, inverse)


def pack_kernel(up, down_t, qkv, out_t, packed):
    packed[:, :HID] = up[...].astype(BF16)
    packed[:, HID : 2 * HID] = down_t[...].astype(BF16)
    parts = [qkv[j] for j in range(3)] + [out_t[...]]
    packed[:, 2 * HID :] = jnp.concatenate(parts, axis=1).astype(BF16)


def pack(up, down_t, qkv, out_t):
    return pl.pallas_call(
        pack_kernel,
        out_shape=jax.ShapeDtypeStruct((D // 32, 2 * HID + D), BF16),
        cost_estimate=cost(1),
        name="pack",
    )(up, down_t, qkv, out_t)


def plan_kernel(
    small, owner, length,
    plan, live, seg_row, seg_col, ln_gain, qk_gain, out_bias, hidden_bias,
):
    group, branch = lax.axis_index("dp"), lax.axis_index("branch")
    gains = D // 128
    for i in range(gains):
        lane = slice(i * 128, (i + 1) * 128)
        ln_gain[:, lane] = small[i : i + 1, :]
        out_bias[:, lane] = small[gains + 1 + i : gains + 2 + i, :]
        hidden_bias[:, lane] = small[pl.ds(2 * gains + 1 + branch * (HID // 128) + i, 1), :]
    both = small[gains : gains + 1, :]
    q_gain, k_gain = both[:, :HEAD], both[:, HEAD:]
    qk_gain[...] = jnp.concatenate([q_gain] * HL + [k_gain] * HL, axis=1)
    bound = 8.0 * 1.02 * jnp.max(jnp.abs(q_gain)) * jnp.max(jnp.abs(k_gain))

    size = jnp.where(owner[...] == group, length[...], 0)
    tokens = jnp.sum(size)
    big = jnp.where(jnp.max(size) == CAP, 1, 0)

    def label(shape, axis):
        place = lax.broadcasted_iota(jnp.int32, shape, axis) + CH * branch
        place = jnp.where(place >= CAP, place - CAP, place)
        image = jnp.where(big == 1, 0, (place * 2675) >> 19)
        return jnp.where(place < tokens, image, CAP)

    seg_row[...] = label((1, CAP), 1)
    seg_col[...] = label((CAP, 1), 0)
    plan[0] = jnp.where(bound <= SAFE, 1 + big, 0)
    for t in range(CAP // QT):
        start = lax.rem(t * QT + CH * branch, CAP)
        last = start + QT - 1
        begin = jnp.where(start < tokens, ((start * 2675) >> 19) * SMALL_LEN, tokens)
        end = jnp.minimum((((last * 2675) >> 19) + 1) * SMALL_LEN, tokens)
        end = jnp.where(last >= tokens, CAP, end)
        begin = jnp.where(big == 1, 0, begin)
        end = jnp.where(big == 1, CAP, end)
        strip = begin // MS
        plan[1 + t] = lax.rem(strip + CAP // MS - (CH // MS) * branch, CAP // MS)
        plan[5 + t] = (end + MS - 1) // MS - strip
        plan[9 + t] = jnp.where(start < tokens, 1, 0)
        plan[21 + t] = jnp.where(last >= tokens, 1, 0)
    for t in range(CAP // MS):
        start = lax.rem(t * MS + CH * branch, CAP)
        plan[13 + t] = jnp.where(start < tokens, 1, 0)
    for k in range(BR):
        start = lax.rem((branch + k) * CH, CAP)
        live[k] = jnp.clip(tokens - start, 0, CH)


def make_plan(small, owner, length):
    smem = pl.BlockSpec(memory_space=pltpu.SMEM)
    vmem = pl.BlockSpec(memory_space=pltpu.VMEM)
    row = lambda width, kind=F32: jax.ShapeDtypeStruct((1, width), kind)
    return pl.pallas_call(
        plan_kernel,
        in_specs=[vmem] * 3,
        out_specs=[smem, smem] + [vmem] * 6,
        out_shape=[
            jax.ShapeDtypeStruct((25,), jnp.int32),
            jax.ShapeDtypeStruct((BR,), jnp.int32),
            row(CAP, jnp.int32),
            jax.ShapeDtypeStruct((CAP, 1), jnp.int32),
            row(D),
            row(QK),
            row(D),
            row(HID),
        ],
        cost_estimate=cost(3),
        name="make_plan",
    )(small, owner, length)


def tiles_of(chunk):
    if isinstance(chunk, tuple):
        return list(chunk), [pl.BlockSpec((TILE, D), lambda t: (0, 0))] * 2
    specs = [pl.BlockSpec((TILE, D), lambda t, i=i: (i, 0)) for i in range(PER)]
    return [chunk] * PER, specs


def tile_now(first, second):
    return jnp.where(pl.program_id(0) == 0, first[...], second[...]).astype(F32)


def project_kernel(
    rows_0, rows_1, weight, gain, qk_gain, normed, q_out, k_out, v_out, qk_hat, qk_inverse
):
    hat, _ = norm_parts(tile_now(rows_0, rows_1))
    low = (hat * gain[...]).astype(BF16)
    normed[...] = low
    raw = dot(low, weight[:, :QKV], NN)
    hat, inverse = head_norm(raw[:, :QK], heads_of(QK))
    qk_hat[...] = hat
    qk_inverse[...] = inverse
    value = (hat * qk_gain[...]).astype(BF16)
    vals = raw[:, QK:].astype(BF16)
    for h in range(HL):
        lane = slice(h * HEAD, (h + 1) * HEAD)
        q_out[h] = value[:, lane] * jnp.asarray(HEAD**-0.5, BF16)
        k_out[h] = value[:, QK // 2 + h * HEAD : QK // 2 + (h + 1) * HEAD]
        v_out[h] = vals[:, lane]


def project(rows, weights, gain, qk_gain):
    whole = lambda shape: pl.BlockSpec(shape, lambda t: (0,) * len(shape))
    heads = pl.BlockSpec((HL, TILE, HEAD), lambda t: (0, t, 0))
    tile = pl.BlockSpec((TILE, D), lambda t: (t, 0))
    rows, rows_specs = tiles_of(rows)
    return pl.pallas_call(
        project_kernel,
        grid=(PER,),
        in_specs=rows_specs
        + [
            pl.BlockSpec((D, D), lambda t: (0, 2)),
            whole((1, D)),
            whole((1, QK)),
        ],
        out_specs=[tile, heads, heads, heads] + [pl.BlockSpec((TILE, QK), lambda t: (t, 0))] * 2,
        out_shape=[jax.ShapeDtypeStruct((CH, D), BF16)]
        + [pltpu.HBM((HL, CH, HEAD), BF16)] * 3
        + [pltpu.HBM((CH, QK), F32)] * 2,
        compiler_params=params(16),
        cost_estimate=cost(3),
        name="project",
    )(*rows, weights, gain, qk_gain)


def mlp_kernel(
    live, cot_0, cot_1, normed, up, down_t, proj, bias,
    ffn, back, act_out, pre_out, ups_out, mix_out,
):
    t = pl.program_id(0)
    pre = dot(normed[...], up[...], NN) + bias[...]
    half = 0.5 * (1.0 + lax.erf(pre * (2.0**-0.5)))
    act = (pre * half).astype(BF16)
    slope = half + pre * (jnp.exp(-0.5 * pre * pre) * 0.3989422804014327)
    act_out[...] = act
    ffn[pl.ds(t * TILE, TILE), :] = dot(act, down_t[...], NT).astype(ffn.dtype)
    place = lax.broadcasted_iota(jnp.int32, (TILE, 1), 0) + t * TILE
    ups = jnp.where(place < live[0], tile_now(cot_0, cot_1), 0.0).astype(BF16)
    ups_out[...] = ups
    grad = (dot(ups, down_t[...], NN) * slope).astype(BF16)
    pre_out[...] = grad
    back[...] = dot(grad, up[...], NT)
    mixed = dot(ups, proj[:, QKV:], NN).astype(BF16)
    if ffn.shape[0] > CH:

        @pl.when(t == 0)
        def _():
            ffn[CH:, :] = proj[:, QKV:].astype(F32).T.astype(BF16)

    for h in range(HL):
        mix_out[h] = mixed[:, h * HEAD : (h + 1) * HEAD]


def mlp(live, cot, normed, weights, bias, height, kind):
    whole = lambda shape: pl.BlockSpec(shape, lambda t: (0,) * len(shape))
    tile = pl.BlockSpec((TILE, D), lambda t: (t, 0))
    cot, cot_specs = tiles_of(cot)
    return pl.pallas_call(
        mlp_kernel,
        grid=(PER,),
        in_specs=[pl.BlockSpec(memory_space=pltpu.SMEM)]
        + cot_specs
        + [
            tile,
            pl.BlockSpec((D, HID), lambda t: (0, 0)),
            pl.BlockSpec((D, HID), lambda t: (0, 1)),
            pl.BlockSpec((D, D), lambda t: (0, 2)),
            whole((1, HID)),
        ],
        out_specs=[whole((height, D))]
        + [tile] * 4
        + [pl.BlockSpec((HL, TILE, HEAD), lambda t: (0, t, 0))],
        out_shape=[pltpu.HBM((height, D), kind), pltpu.HBM((CH, D), F32)]
        + [jax.ShapeDtypeStruct((CH, D), BF16)] * 3
        + [pltpu.HBM((HL, CH, HEAD), BF16)],
        compiler_params=params(20),
        cost_estimate=cost(6),
        name="mlp",
    )(live, *cot, normed, weights, weights, weights, bias)


def attend_kernel(plan, *refs):
    q_refs, k_refs, v_refs, g_refs = (refs[i * BR : (i + 1) * BR] for i in range(4))
    seg_row, seg_col, mixed, dq_out, dk_out, dv_out = refs[4 * BR : 4 * BR + 6]
    probs, pgrad, dk_sum, dv_sum, q_ref, k_ref, v_ref, g_ref = refs[4 * BR + 6 :]
    t = pl.program_id(1)
    for k in range(BR):

        @pl.when(t == k)
        def _():
            q_ref[...] = q_refs[k][...]
            g_ref[...] = g_refs[k][...]

    @pl.when(t == 0)
    def _():
        dk_sum[...] = jnp.zeros_like(dk_sum)
        dv_sum[...] = jnp.zeros_like(dv_sum)
        for k in range(BR):
            k_ref[:, k * CH : (k + 1) * CH] = k_refs[k][...]
            v_ref[:, k * CH : (k + 1) * CH] = v_refs[k][...]

    query = q_ref[0]
    grad = g_ref[0]

    @pl.when(plan[0] == 2)
    def _():
        total = jnp.zeros((QT, 128), F32)
        weighted = jnp.zeros((QT, 128), F32)
        for j in range(CAP // KS):
            part = slice(j * KS, (j + 1) * KS)
            e = jnp.exp(dot(query, k_ref[0, part], NT))
            probs[:, part] = e
            pg = dot(grad, v_ref[0, part], NT)
            pgrad[:, part] = pg
            total = total + lane_sum(e)
            weighted = weighted + lane_sum(e * pg)
        scale = 1.0 / jnp.sum(total, axis=1, keepdims=True)
        delta = jnp.sum(weighted, axis=1, keepdims=True) * scale
        out = jnp.zeros((QT, HEAD), F32)
        dq = jnp.zeros((QT, HEAD), F32)
        for j in range(CAP // KS):
            part = slice(j * KS, (j + 1) * KS)
            p = probs[:, part] * scale
            low = p.astype(BF16)
            ds = (p * (pgrad[:, part] - delta)).astype(BF16)
            out = out + dot(low, v_ref[0, part], NN)
            dq = dq + dot(ds, k_ref[0, part], NN)
            dv_sum[:, part] += dot(grad, low, TN)
            dk_sum[:, part] += dot(query, ds, TN)
        mixed[0] = out.astype(BF16)
        dq_out[0] = dq * HEAD**-0.5

    @pl.when(plan[0] == 1)
    def _():
        mixed[...] = jnp.zeros_like(mixed)
        dq_out[...] = jnp.zeros_like(dq_out)
        for s in range(QT // MS):
            index = t * (QT // MS) + s
            at = slice(s * MS, (s + 1) * MS)

            @pl.when(plan[13 + index] == 1)
            def _():
                qs, gs, seg = query[at], grad[at], seg_col[at, :]
                strips, es, pgs = [], [], []
                for j in range(3):
                    near = lax.rem(index + (CAP // MS - 1) + j, CAP // MS)
                    strip = pl.ds(pl.multiple_of(near * MS, MS), MS)
                    score = dot(qs, k_ref[0, strip], NT)
                    strips.append(strip)
                    es.append(jnp.where(seg == seg_row[:, strip], jnp.exp(score), 0.0))
                    pgs.append(dot(gs, v_ref[0, strip], NT))
                total = sum(lane_sum(e) for e in es)
                weighted = sum(lane_sum(e * pg) for e, pg in zip(es, pgs))
                scale = 1.0 / jnp.sum(total, axis=1, keepdims=True)
                delta = jnp.sum(weighted, axis=1, keepdims=True) * scale
                out = jnp.zeros((MS, HEAD), F32)
                dq = jnp.zeros((MS, HEAD), F32)
                for strip, e, pg in zip(strips, es, pgs):
                    p = e * scale
                    low = p.astype(BF16)
                    ds = (p * (pg - delta)).astype(BF16)
                    out = out + dot(low, v_ref[0, strip], NN)
                    dq = dq + dot(ds, k_ref[0, strip], NN)
                    dv_sum[:, strip] += dot(gs, low, TN)
                    dk_sum[:, strip] += dot(qs, ds, TN)
                mixed[0, at, :] = out.astype(BF16)
                dq_out[0, at, :] = dq * HEAD**-0.5

        @pl.when(plan[21 + t] == 1)
        def _():
            total = jnp.zeros((QT, 128), F32)
            for j in range(CAP // KS):
                part = slice(j * KS, (j + 1) * KS)
                e = jnp.exp(dot(query, k_ref[0, part], NT))
                e = jnp.where(seg_row[:, part] == CAP, e, 0.0)
                probs[:, part] = e
                total = total + lane_sum(e)
            scale = 1.0 / jnp.sum(total, axis=1, keepdims=True)
            out = jnp.zeros((QT, HEAD), F32)
            for j in range(CAP // KS):
                part = slice(j * KS, (j + 1) * KS)
                out = out + dot((probs[:, part] * scale).astype(BF16), v_ref[0, part], NN)
            mixed[0] = jnp.where(seg_col[...] == CAP, out, mixed[0].astype(F32)).astype(BF16)

    @pl.when(plan[0] == 0)
    def _():
        first, count, live = plan[1 + t], plan[5 + t], plan[9 + t]
        seg = seg_col[...]

        def strip(i):
            return pl.ds(pl.multiple_of(lax.rem(first + i, CAP // MS) * MS, MS), MS)

        def scores(i, top):
            at = strip(i)
            s = dot(query, k_ref[0, at], NT)
            s = jnp.where(seg == seg_row[:, at], s, -1e30)
            probs[:, at] = s
            return jnp.maximum(top, jnp.max(s, axis=1, keepdims=True))

        top = lax.fori_loop(0, count, scores, jnp.full((QT, 1), -1e30, F32))

        def exps(i, total):
            at = strip(i)
            e = jnp.exp(probs[:, at] - top)
            probs[:, at] = e
            return total + jnp.sum(e, axis=1, keepdims=True)

        total = lax.fori_loop(0, count, exps, jnp.zeros((QT, 1), F32))
        scale = 1.0 / total

        def sums(i, out):
            at = strip(i)
            p = probs[:, at] * scale
            probs[:, at] = p
            return out + dot(p.astype(BF16), v_ref[0, at], NN)

        out = lax.fori_loop(0, count, sums, jnp.zeros((QT, HEAD), F32))
        mixed[0] = out.astype(BF16)
        dq_out[...] = jnp.zeros_like(dq_out)

        @pl.when(live == 1)
        def _():
            def deltas(i, delta):
                at = strip(i)
                pg = dot(grad, v_ref[0, at], NT)
                pgrad[:, at] = pg
                return delta + jnp.sum(probs[:, at] * pg, axis=1, keepdims=True)

            delta = lax.fori_loop(0, count, deltas, jnp.zeros((QT, 1), F32))

            def backs(i, carry):
                at = strip(i)
                p = probs[:, at]
                low = p.astype(BF16)
                ds = (p * (pgrad[:, at] - delta)).astype(BF16)
                dq_out[0] += dot(ds, k_ref[0, at], NN) * HEAD**-0.5
                dv_sum[:, at] += dot(grad, low, TN)
                dk_sum[:, at] += dot(query, ds, TN)
                return carry

            lax.fori_loop(0, count, backs, 0)

    @pl.when(t == CAP // QT - 1)
    def _():
        dv_out[0] = dv_sum[...].astype(BF16)
        dk_out[0] = dk_sum[...]


def attend(plan, q, k, v, g, seg_row, seg_col):
    chunk = pl.BlockSpec((1, CH, HEAD), lambda h, t: (h, 0, 0))
    out = pl.BlockSpec((1, QT, HEAD), lambda h, t: (h, t, 0))
    flat = lambda kind: pltpu.HBM((HL, CAP, HEAD), kind)
    turned = pl.BlockSpec((1, HEAD, CAP), lambda h, t: (h, 0, 0))
    return pl.pallas_call(
        attend_kernel,
        grid=(HL, CAP // QT),
        in_specs=[pl.BlockSpec(memory_space=pltpu.SMEM)]
        + [chunk] * (4 * BR)
        + [
            pl.BlockSpec((1, CAP), lambda h, t: (0, 0)),
            pl.BlockSpec((QT, 1), lambda h, t: (t, 0)),
        ],
        out_specs=[out, out, turned, turned],
        out_shape=[flat(BF16), flat(F32)]
        + [pltpu.HBM((HL, HEAD, CAP), kind) for kind in (F32, BF16)],
        scratch_shapes=[
            pltpu.VMEM((QT, CAP), F32),
            pltpu.VMEM((QT, CAP), F32),
            pltpu.VMEM((HEAD, CAP), F32),
            pltpu.VMEM((HEAD, CAP), F32),
            pltpu.VMEM((1, QT, HEAD), BF16),
            pltpu.VMEM((1, CAP, HEAD), BF16),
            pltpu.VMEM((1, CAP, HEAD), BF16),
            pltpu.VMEM((1, QT, HEAD), BF16),
        ],
        compiler_params=params(24),
        cost_estimate=cost(48),
        name="attend",
    )(plan, *far_from([*q, *k, *v, *g, seg_row, seg_col]))


def early_kernel(*refs):
    normed, pre, ups, act = (refs[i * BR : (i + 1) * BR] for i in range(4))
    out, normed_out, ups_out, total, bias = refs[4 * BR :]
    t = pl.program_id(0)

    @pl.when(t == 0)
    def _():
        total[...] = jnp.zeros_like(total)
        bias[...] = jnp.zeros_like(bias)

    def joined(parts):
        return jnp.concatenate([part[...] for part in parts], axis=0)

    for k in range(BR):
        normed_out[k] = normed[k][...]
        ups_out[k] = ups[k][...]
        bias[...] += row_sum8(pre[k][...].astype(F32))
    lane = lax.broadcasted_iota(jnp.int32, (CH, 128), 1)
    first = jnp.where(lane == 0, 1.0, 0.0).astype(BF16)
    total[:, :HID] += dot(joined(normed), joined(pre), TN)
    right = jnp.concatenate([joined(act), first], axis=1)
    total[:, HID:] += dot(joined(ups), right, TN)

    @pl.when(t == BR - 1)
    def _():
        out[:, : 2 * HID] = total[:, : 2 * HID].astype(BF16)
        column = jnp.sum(bias[...].T, axis=1, keepdims=True)
        lane = lax.broadcasted_iota(jnp.int32, (D, 128), 1)
        out[:, 2 * HID :] = jnp.where(lane == 1, column, total[:, 2 * HID :]).astype(BF16)


def early_weights(normed, pre, ups, act):
    tile = pl.BlockSpec((CH // BR, D), lambda t: (t, 0))
    joined = pl.BlockSpec((BR, CH // BR, D), lambda t: (0, t, 0))
    return pl.pallas_call(
        early_kernel,
        grid=(BR,),
        in_specs=[tile] * (4 * BR),
        out_specs=[pl.BlockSpec((D, EARLY), lambda t: (0, 0)), joined, joined],
        out_shape=[pltpu.HBM((D, EARLY), BF16)]
        + [pltpu.HBM((BR, CH, D), BF16)] * 2,
        scratch_shapes=[pltpu.VMEM((D, EARLY), F32), pltpu.VMEM((8, HID), F32)],
        compiler_params=params(26),
        cost_estimate=cost(6),
        name="early_weights",
    )(*normed, *pre, *ups, *act)


def back_kernel(qk_gain, *refs):
    hats, inverses, pieces = refs[:BR], refs[BR : 2 * BR], refs[2 * BR : -3]
    grads_out, mixed_out, gains = refs[-3:]
    t = pl.program_id(0)
    dq, dk, dv, mixed = pieces

    @pl.when(t == 0)
    def _():
        gains[...] = jnp.zeros_like(gains)

    matrix = heads_of(QK)
    pair = [dq[h] for h in range(HL)] + [dk[h].T for h in range(HL)]
    pair = jnp.concatenate(pair, axis=1)

    def back(hat, inverse):
        gains[...] += row_sum8(pair * hat)
        scaled = pair * qk_gain[...]
        mean = dot(scaled.astype(BF16), matrix, NN)
        slope = dot((scaled * hat).astype(BF16), matrix, NN)
        raw = inverse * (scaled - mean - hat * slope)
        grads_out[:, :QK] = raw.astype(BF16)

    for k in range(BR):

        @pl.when(t == k)
        def _():
            back(hats[k][...], inverses[k][...])

    values = jnp.concatenate([dv[h].astype(F32).T for h in range(HL)], axis=1)
    grads_out[:, QK:] = values.astype(BF16)
    mixed_out[...] = jnp.concatenate([mixed[h] for h in range(HL)], axis=1)


def back_heads(qk_gain, hats, inverses, pieces):
    tile = lambda width: pl.BlockSpec((CH, width), lambda t: (t, 0))
    whole = lambda shape: pl.BlockSpec(shape, lambda t: (0,) * len(shape))
    once = pl.BlockSpec((CH, QK), lambda t: (0, 0), pipeline_mode=pl.Buffered(1))
    by_rows = pl.BlockSpec((HL, CH, HEAD), lambda t: (0, t, 0))
    by_lanes = pl.BlockSpec((HL, HEAD, CH), lambda t: (0, 0, t))
    return pl.pallas_call(
        back_kernel,
        grid=(BR,),
        in_specs=[whole((1, QK))]
        + [once] * (2 * BR)
        + [by_rows, by_lanes, by_lanes, by_rows],
        out_specs=[tile(QKV), tile(HL * HEAD), whole((8, QK))],
        out_shape=[
            pltpu.HBM((CAP, QKV), BF16),
            pltpu.HBM((CAP, HL * HEAD), BF16),
            jax.ShapeDtypeStruct((8, QK), F32),
        ],
        compiler_params=params(24),
        cost_estimate=cost(6),
        name="back_heads",
    )(qk_gain, *far_from([*hats, *inverses, *pieces]))


def late_kernel(normed, ups, grads, mixed, out, total):
    t = pl.program_id(0)

    @pl.when(t == 0)
    def _():
        total[...] = jnp.zeros_like(total)

    total[:, :QKV] += dot(normed[0], grads[...], TN)
    total[:, QKV:] += dot(ups[0], mixed[...], TN)

    @pl.when(t == BR - 1)
    def _():
        out[...] = total[...].astype(BF16)


def late_weights(normed, ups, grads, mixed):
    tile = lambda width: pl.BlockSpec((CH, width), lambda t: (t, 0))
    return pl.pallas_call(
        late_kernel,
        grid=(BR,),
        in_specs=[pl.BlockSpec((1, CH, D), lambda t: (t, 0, 0))] * 2
        + [tile(QKV), tile(HL * HEAD)],
        out_specs=pl.BlockSpec((D, D), lambda t: (0, 0)),
        out_shape=pltpu.HBM((D, D), BF16),
        scratch_shapes=[pltpu.VMEM((D, D), F32)],
        compiler_params=params(20),
        cost_estimate=cost(6),
        name="late_weights",
    )(*far_from((normed, ups, grads, mixed)))


def close_kernel(weight, rows_0, rows_1, back, grads, *refs):
    out, gains = refs[-2:]
    t = pl.program_id(0)
    total = back[...] + dot(grads[...], weight[:, :QKV], NT)
    out[pl.ds(t * TILE, TILE), :] = total.astype(out.dtype)
    hat, _ = norm_parts(tile_now(rows_0, rows_1))

    @pl.when(t == 0)
    def _():
        gains[...] = jnp.zeros_like(gains)
        if len(refs) > 2:
            width = HL * HEAD
            for i in range(4):
                part = refs[0][i * 128 : (i + 1) * 128, :]
                out[CH:, i * width : (i + 1) * width] = part

    gains[...] += row_sum8(total * hat)


def close(chunk, weight, rows, back, grads, mixed):
    tile = pl.BlockSpec((TILE, D), lambda t: (t, 0))
    whole = lambda shape: pl.BlockSpec(shape, lambda t: (0,) * len(shape))
    rows, rows_specs = tiles_of(rows)
    height, kind = (CH, F32) if chunk == 0 else (CH + 128, BF16)
    more, more_specs = [], []
    if chunk != 0:
        more, more_specs = [mixed], [pl.BlockSpec((CH, HL * HEAD), lambda t: (chunk, 0))]
    return pl.pallas_call(
        close_kernel,
        grid=(PER,),
        in_specs=[pl.BlockSpec((D, D), lambda t: (0, 2))]
        + rows_specs
        + [tile, pl.BlockSpec((TILE, QKV), lambda t: (chunk * PER + t, 0))]
        + more_specs,
        out_specs=[whole((height, D)), whole((8, D))],
        out_shape=[pltpu.HBM((height, D), kind), pltpu.HBM((8, D), F32)],
        compiler_params=params(14),
        cost_estimate=cost(3),
        name="close",
    )(weight, *far_from(rows), *far_from([back, grads, *more]))


def begin_kernel(rows, own, part1, part2, part3, bias, mixed, weight, out):
    total = rows[...].astype(F32) + own[...] + bias[...]
    for part in (part1, part2, part3):
        total = total + part[...].astype(F32)
    out[...] = total + dot(mixed[...], weight[:, QKV:], NT)


def begin_rows(rows, own, parts, bias, mixed, weights):
    tile = lambda width: pl.BlockSpec((TILE, width), lambda t: (t, 0))
    return pl.pallas_call(
        begin_kernel,
        grid=(PER,),
        in_specs=[tile(D)] * 5
        + [pl.BlockSpec((1, D), lambda t: (0, 0)), tile(HL * HEAD)]
        + [pl.BlockSpec((D, D), lambda t: (0, 2))],
        out_specs=tile(D),
        out_shape=pltpu.HBM((CH, D), F32),
        compiler_params=params(16),
        cost_estimate=cost(4),
        name="begin_rows",
    )(*far_from([rows, own, *parts]), bias, *far_from([mixed]), weights)


def end_kernel(live, begun, rows, cot, own, part1, part2, part3, gain, *refs):
    messages, theirs, (output, input_grad) = refs[:3], refs[3:6], refs[6:]
    t = pl.program_id(0)
    total = begun[...]
    width = HL * HEAD
    for message, their in zip(messages, theirs):
        blocks = [message[:, i * width : (i + 1) * width] for i in range(4)]
        first = jnp.concatenate(blocks[:2], axis=0)
        second = jnp.concatenate(blocks[2:], axis=0)
        total = total + dot(jnp.where(t == 0, first, second), their[...], NN)
    output[...] = total.astype(BF16)

    total = own[...]
    for part in (part1, part2, part3):
        total = total + part[...].astype(F32)
    hat, inverse = norm_parts(rows[...].astype(F32))
    place = lax.broadcasted_iota(jnp.int32, (TILE, 1), 0) + t * TILE
    ups = jnp.where(place < live[0], cot[...].astype(F32), 0.0)
    input_grad[...] = (ups + norm_back(total * gain[...], hat, inverse)).astype(BF16)


def end_rows(live, begun, rows, cot, own, gain, messages, parts):
    tile = pl.BlockSpec((TILE, D), lambda t: (t, 0))
    below = pl.BlockSpec((128, D), lambda t: (CH // 128, 0))
    weight = pl.BlockSpec((pl.Element(HL * HEAD), pl.Element(D)), lambda t: (CH, 0))
    return pl.pallas_call(
        end_kernel,
        grid=(PER,),
        in_specs=[pl.BlockSpec(memory_space=pltpu.SMEM)]
        + [tile] * 7
        + [pl.BlockSpec((1, D), lambda t: (0, 0))]
        + [below] * 3
        + [weight] * 3,
        out_specs=[tile, tile],
        out_shape=[jax.ShapeDtypeStruct((CH, D), BF16)] * 2,
        compiler_params=params(20),
        cost_estimate=cost(6),
        name="end_rows",
    )(
        live,
        *far_from([begun, rows, cot, own, *messages]),
        gain,
        *far_from([*messages, *parts]),
    )


def tell_kernel(
    late_parts, early_parts, gains_0, gains_1, gains_2, gains_3, head_gains, told, late, early
):
    late[...] = jnp.sum(late_parts[...].astype(F32), axis=0)
    early[...] = jnp.sum(early_parts[...].astype(F32), axis=0)
    squares = jnp.sum(late[...] * late[...])
    squares = squares + jnp.sum(early[:, : 2 * HID] * early[:, : 2 * HID])
    gains = gains_0[...] + gains_1[...] + gains_2[...] + gains_3[...]
    gains = jnp.sum(gains, axis=0, keepdims=True)
    heads = jnp.sum(head_gains[...], axis=0, keepdims=True)
    q_part = sum(heads[:, h * HEAD : (h + 1) * HEAD] for h in range(HL))
    k_part = sum(heads[:, QK // 2 + h * HEAD : QK // 2 + (h + 1) * HEAD] for h in range(HL))
    biases = early[:, 2 * HID :].T
    depth = D // 32
    lane = lax.broadcasted_iota(jnp.int32, (1, TOLD - BASE - 2 * depth), 1)
    last = jnp.where(lane == 0, squares, 0.0)
    row = [gains, q_part, k_part, biases[0:1, :], biases[1:2, :], last]
    told[...] = jnp.broadcast_to(jnp.concatenate(row, axis=1)[None], told.shape)


def tell(late_parts, early_parts, gains, head_gains):
    return pl.pallas_call(
        tell_kernel,
        out_shape=[
            pltpu.HBM((128, 1, TOLD), F32),
            pltpu.HBM((D // 32, D), F32),
            pltpu.HBM((D // 32, EARLY), F32),
        ],
        compiler_params=params(24),
        cost_estimate=cost(3),
        name="tell",
    )(*far_from([late_parts, early_parts, *gains, head_gains]))


def finish_kernel(heard, early, late, *refs):
    ins, outs, norm, out_bias, hidden_bias, small = refs[:15], refs[15:30], *refs[30:]
    depth = D // 32
    for g in range(32):
        lane = slice(g * depth, (g + 1) * depth)
        rows = heard[4 * g : 4 * g + 4, BASE : BASE + 2 * depth]
        out_bias[:, lane] = rows[0:1, :depth]
        hidden_bias[:, lane] = rows[:, depth:]
    totals = jnp.sum(heard[...], axis=0, keepdims=True)
    for i in range(D // 128):
        lane = slice(i * 128, (i + 1) * 128)
        small[i : i + 1, :] = totals[:, lane]
        small[7 + i : 8 + i, :] = out_bias[:, lane]
        for j in range(BR):
            place = 13 + j * (HID // 128) + i
            small[place : place + 1, :] = hidden_bias[j : j + 1, lane]
    small[6:7, :] = totals[:, D:BASE]
    squares = totals[:, BASE + 2 * depth : BASE + 2 * depth + 1]
    small_squares = jnp.sum(small[...] * small[...], axis=1, keepdims=True)
    squares = squares + jnp.sum(small_squares, axis=0, keepdims=True)
    length = jnp.sqrt(squares)
    norm[...] = length
    factor = 1.0 / jnp.maximum(length, 1.0)

    def update(i, gradient, at=Ellipsis, rate=RATE_MATRIX, decay=DECAY_MATRIX):
        news = adam_update(
            ins[3 * i][at], ins[3 * i + 1][at], ins[3 * i + 2][at], gradient, factor, rate, decay
        )
        for out, new in zip(outs[3 * i : 3 * i + 3], news):
            out[at] = new

    for j in range(3):
        update(0, late[:, j * HL * HEAD : (j + 1) * HL * HEAD], at=j)
    update(1, late[:, QKV:])
    update(2, early[:, :HID])
    update(3, early[:, HID : 2 * HID])
    update(4, small[...], rate=RATE_SMALL, decay=0.0)


def finish(heard, early, late, arrays):
    return pl.pallas_call(
        finish_kernel,
        out_shape=[jax.ShapeDtypeStruct(value.shape, F32) for value in arrays]
        + [jax.ShapeDtypeStruct((1, 1), F32)],
        scratch_shapes=[
            pltpu.VMEM((1, D), F32),
            pltpu.VMEM((BR, HID), F32),
            pltpu.VMEM((37, 128), F32),
        ],
        compiler_params=params(16),
        cost_estimate=cost(4),
        name="finish",
    )(heard, *far_from([early, late, *arrays]))


def dp_pairs(step):
    pairs = []
    for y in range(4):
        for z in range(4):
            for c in range(2):
                y2, z2, c2 = step(y, z, c)
                pairs.append(((y * 4 + z) * 2 + c, ((y2 % 4) * 4 + z2 % 4) * 2 + c2))
    return pairs


def move_x(value, k):
    return lax.ppermute(value, "branch", [(i, (i + k) % BR) for i in range(BR)])


def move_y(value, k):
    return lax.ppermute(value, "dp", dp_pairs(lambda y, z, c: (y + k, z, c)))


def move_z(value, k):
    return lax.ppermute(value, "dp", dp_pairs(lambda y, z, c: (y, z + k, c)))


def move_core(value):
    return lax.ppermute(value, "dp", dp_pairs(lambda y, z, c: (y, z, 1 - c)))


def put(buffer, value, index, axis):
    return lax.dynamic_update_index_in_dim(buffer, value, index, axis)


def take(buffer, index, axis):
    return lax.dynamic_index_in_dim(buffer, index, axis, keepdims=False)


def gather_plane(own, y, z):
    line = jnp.zeros((4, *own.shape), own.dtype)
    line = put(line, own, z, 0)
    for k in (1, 3, 2):
        line = put(line, move_z(own, -k), (z + k) % 4, 0)
    plane = jnp.zeros((4, *line.shape), own.dtype)
    plane = put(plane, line, y, 0)
    came = [move_y(line, -k) for k in (1, 3, 2)]
    for k, part in zip((1, 3, 2), came):
        plane = put(plane, part, (y + k) % 4, 0)
    return plane, came[0]


def gather_cores(plane, other, c):
    whole = jnp.zeros((4, 4, 2, *plane.shape[2:]), plane.dtype)
    whole = put(whole, plane, c, 2)
    whole = put(whole, other, 1 - c, 2)
    return whole.reshape(32 * plane.shape[2], plane.shape[3])


def after(values, *earlier):
    return lax.optimization_barrier((values, earlier))[0]


def gather_rows(own):
    near = [move_x(own, -k) for k in (1, 3)]
    half = own.shape[0] // 2
    far = (move_x(near[0][:half], -1), move_x(near[1][half:], 1))
    return [own, near[0], far, near[1]]


def to_owners(grad):
    return lax.all_to_all(grad.reshape(32, D // 32, -1), "dp", 0, 0, tiled=True)


def adam_update(weight, first_moment, second_moment, gradient, factor, rate, decay):
    clipped = gradient * factor
    first_new = BETA_ONE * first_moment + (1.0 - BETA_ONE) * clipped
    second_new = BETA_TWO * second_moment + (1.0 - BETA_TWO) * clipped * clipped
    ratio = (
        first_new
        / (1.0 - BETA_ONE**STEP)
        / (jnp.sqrt(second_new / (1.0 - BETA_TWO**STEP)) + EPS_ADAM)
    )
    return (clipped, second_new, weight - rate * (ratio + decay * weight))


def body(
    block_input,
    cotangent,
    image_owner,
    image_length,
    image_start,
    qkv_weight,
    qkv_first,
    qkv_second,
    out_weight,
    out_first,
    out_second,
    up_weight,
    up_first,
    up_second,
    down_weight,
    down_first,
    down_second,
    small_weight,
    small_first,
    small_second,
):
    b = lax.axis_index("branch")
    g = lax.axis_index("dp")
    y, z, c = g // 8, (g // 2) % 4, g % 2
    depth = up_weight.shape[0]

    own = pack(up_weight, down_weight.T, qkv_weight, out_weight.T)
    plane, came = gather_plane(own, y, z)

    rows = gather_rows(block_input)
    other = move_core(after(plane, rows[1], rows[3]))
    weights = gather_cores(plane, other, c)
    cots = gather_rows(after(cotangent, rows[1], rows[3], other))

    plan, live, seg_row, seg_col, ln_gain, qk_gain, out_bias, hidden_bias = make_plan(
        after(small_weight, came).reshape(-1, 128), image_owner[None], image_length[None]
    )

    normed, q, key, v, hats, inverses = ([None] * BR for _ in range(6))
    for k in (0, 1, 3, 2):
        normed[k], q[k], key[k], v[k], hats[k], inverses[k] = project(
            rows[k], weights, ln_gain, qk_gain
        )

    ffn, back, act, pre, ups, mixed_grad = ([None] * BR for _ in range(6))
    for k in (0, 1, 3, 2):
        ffn[k], back[k], act[k], pre[k], ups[k], mixed_grad[k] = mlp(
            live[k][None], cots[k], normed[k], weights, hidden_bias, *((MSG, BF16) if k else (CH, F32))
        )

    ffn_parts = [move_x(ffn[k], k) for k in (1, 2, 3)]
    early_grad, normed, ups = early_weights(normed, pre, ups, act)
    early_parts = to_owners(early_grad)
    mixed, dq, dk, dv = attend(plan, q, key, v, after(mixed_grad, early_grad), seg_row, seg_col)
    qkv_grads, mixed, head_gains = back_heads(
        qk_gain, hats, inverses, (after(dq, early_parts, ffn_parts), dk, dv, mixed)
    )
    grads, gain_parts, messages = [None] * BR, [None] * BR, [None] * BR
    grads[2], gain_parts[2] = close(2, weights, rows[2], back[2], qkv_grads, mixed)
    messages[2] = move_x(grads[2], 2)
    late_grad = late_weights(normed, ups, after(qkv_grads, grads[2]), mixed)
    late_parts = to_owners(late_grad)
    for k in (1, 3, 0):
        grads[k], gain_parts[k] = close(k, weights, rows[k], back[k], qkv_grads, mixed)
    for k in (1, 3):
        messages[k] = move_x(grads[k], k)
    begun = begin_rows(block_input, ffn[0], ffn_parts, out_bias, mixed, weights)
    block_output, input_grad = end_rows(
        live[:1], begun, block_input, cotangent, grads[0], ln_gain, messages[1:], ffn_parts
    )

    told, late, early = tell(late_parts, early_parts, gain_parts, head_gains)
    heard = lax.all_to_all(told, ("dp", "branch"), 0, 0, tiled=True).reshape(128, TOLD)
    flat = lambda value: value.reshape(-1, 128)
    *news, norm = finish(
        heard,
        early,
        late,
        (
            *(qkv_weight, qkv_first, qkv_second),
            *(out_weight.T, out_first.T, out_second.T),
            *(up_weight, up_first, up_second),
            *(down_weight.T, down_first.T, down_second.T),
            *(flat(small_weight), flat(small_first), flat(small_second)),
        ),
    )
    qkv_new, out_new, up_new, down_new, small_new = (news[3 * i : 3 * i + 3] for i in range(5))
    return (
        block_output,
        input_grad,
        norm.reshape(()),
        *qkv_new,
        *(value.T for value in out_new),
        *up_new,
        *(value.T for value in down_new),
        *(value.reshape(-1) for value in small_new),
    )


def solution(mesh):
    rows = P(("dp", "branch"), None)
    qkv = [P(None, "dp", "branch")] * 3
    out = [P("branch", "dp")] * 3
    up = [P("dp", "branch")] * 3
    small = [P()] * 3
    return jax.shard_map(
        body,
        mesh=mesh,
        in_specs=(rows, rows, P(), P(), P(), *qkv, *out, *up, *out, *small),
        out_specs=(rows, rows, P(), *qkv, *out, *up, *out, *small),
        check_vma=False,
    )
```
